32 devices in a mesh: gx: 4 (over z), gy: 4 (over x, core), gz: 2 (over y).
Axes of the slice: x: 2, y: 2, z: 4, core: 2. Of those that a mesh axis runs over, the one named last changes fastest.
Arguments:
- loads: bfloat16 [4, 4, 2, 1024, 256], P('gx', 'gy', 'gz'), may hold values from -6 to 6
- start: bfloat16 [4, 4, 2, 1024, 256], P('gx', 'gy', 'gz'), may hold values from -6 to 6
- interface_op: bfloat16 [4, 4, 2, 1024, 1024], P('gx', 'gy', 'gz'), as said below
- block_order: int32 [4, 4, 2, 8], P('gx', 'gy', 'gz'), may hold values from 0 to 7, each once within a row
- interface_weights: float32 [4, 4, 2, 1024], P('gx', 'gy', 'gz'), may hold values from 0.1 to 0.3
- coarse_modes: float32 [4, 4, 2, 32, 1024], P('gx', 'gy', 'gz'), as said below
- region_weights: float32 [4, 4, 2, 32, 16], P('gx', 'gy', 'gz'), as said below
- region_inverse: float32 [4, 256, 256], P('gx', ('gy', 'gz')), as said below
- root_inverse: float32 [64, 64], P('gx'), as said below
Outputs:
- solution: float32 [4, 4, 2, 1024, 256], P('gx', 'gy', 'gz')
The draws below stay inside these ranges and needn't reach their ends.
Inputs may be any that keep to these rules, and one draw needn't show every extreme that they name: `block_order`: each row lists every number from 0 to 7 once. `interface_op`: each subdomain's matrix has a dominant positive diagonal and full dense off-diagonal part. `region_inverse`: dense, with a dominant positive diagonal. `root_inverse`: dense, with a dominant positive diagonal. `coarse_modes`: dense. `region_weights`: dense.
All inputs are finite; a program needn't handle non-finite values.
Results may differ from the reference program's by a relative error of at most 0.0003.
Values sent between devices are 32-bit elements; how exact they have to be, the bound alone decides.
No kernel may reach another device: no remote copies, remote signals or barrier semaphores. Data moves between devices by JAX's collectives and lax.ppermute only.
A program may use at most 64 MiB of HBM per device.

```python
import math
import jax
import jax.numpy as jnp
from jax import lax

BLOCK = 128
IFACE = 1024
CASES = 256
MODES = 32
RM = 16
ITERS = 2
SX = 4
SY = 4
SZ = 2
RORD = 256
ROOT = 64


def dominant_matrix(key, count, order, diag_low, diag_high, spread):
    noise_key, diag_key = jax.random.split(key, 2)
    noise = jax.random.normal(noise_key, (count, order, order), jnp.float32)
    diagonal = jax.random.uniform(diag_key, (count, order), jnp.float32, diag_low, diag_high)
    return noise * (spread / order ** 0.5) + diagonal[:, :, None] * jnp.eye(order, dtype=jnp.float32)


def draw_interface_op(key, part):
    matrix = dominant_matrix(jax.random.fold_in(key, 11), SX * SY * SZ, IFACE, 1.5, 2.5, 0.6)
    return matrix.reshape(SX, SY, SZ, IFACE, IFACE).astype(jnp.bfloat16)


def draw_region_inverse(key, part):
    return dominant_matrix(jax.random.fold_in(key, 12), SX, RORD, 0.5, 1.5, 0.5)


def draw_root_inverse(key, part):
    return dominant_matrix(jax.random.fold_in(key, 13), 1, ROOT, 0.5, 1.5, 0.5)[0]


def draw_coarse_modes(key, part):
    inner = jax.random.fold_in(key, 14)
    scale = float(MODES * IFACE) ** (-0.25)
    values = jax.random.normal(inner, (SX, SY, SZ, MODES, IFACE), jnp.float32)
    return values * scale


def draw_region_weights(key, part):
    inner = jax.random.fold_in(key, 15)
    scale = float(RORD * RM) ** (-0.25)
    values = jax.random.normal(inner, (SX, SY, SZ, MODES, RM), jnp.float32)
    return values * scale


def levels(stream_key, shape, cuts, least, high):
    level, own = 1.0, jax.random.fold_in(stream_key, 6)
    for axis_at, parts in cuts:
        draws = jnp.exp(jax.random.uniform(jax.random.fold_in(own, axis_at), (parts,), jnp.float32, least / len(cuts), high / len(cuts)))
        level = level * jnp.repeat(draws, shape[axis_at] // parts).reshape([-1 if axis == axis_at else 1 for axis in range(len(shape))])
    return level


def centred(own_key, dims, width, most, cuts=(), kind=jnp.bfloat16):
    level = levels(own_key, dims, cuts, -0.22, 0.18) if cuts else 1.0
    drawn = jax.random.normal(own_key, dims, jnp.float32) * width * level
    return jnp.minimum(jnp.maximum(drawn, -most), most).astype(kind)


def setup_inputs(seed: int = 0) -> dict:
    splits = jax.random.split(jax.random.key(seed), 10)
    loads = centred(splits[0], (SX, SY, SZ, IFACE, CASES), 1.0, 6.0, ((0, 4), (1, 4), (2, 2)))
    start = centred(splits[1], (SX, SY, SZ, IFACE, CASES), 1.0, 6.0, ((0, 4), (1, 4), (2, 2)))
    interface_op = draw_interface_op(jax.random.fold_in(splits[9], 71), 0)
    block_order = jax.vmap(lambda own: jax.random.permutation(own, 8))(jax.random.split(splits[3], SX * SY * SZ)).reshape((SX, SY, SZ, 8)).astype(jnp.int32)
    interface_weights = jnp.clip(jnp.exp(math.log(0.3) - 1.0986123 * jax.random.uniform(splits[4], (SX, SY, SZ, IFACE), jnp.float32) ** levels(splits[4], (SX, SY, SZ, IFACE), ((0, 4), (1, 4), (2, 2)), -0.2, 0.2)), 0.1, 0.3)
    coarse_modes = draw_coarse_modes(jax.random.fold_in(splits[9], 71), 0)
    region_weights = draw_region_weights(jax.random.fold_in(splits[9], 71), 0)
    region_inverse = draw_region_inverse(jax.random.fold_in(splits[9], 71), 0)
    root_inverse = draw_root_inverse(jax.random.fold_in(splits[9], 71), 0)
    return dict(loads=loads, start=start, interface_op=interface_op, block_order=block_order, interface_weights=interface_weights, coarse_modes=coarse_modes, region_weights=region_weights, region_inverse=region_inverse, root_inverse=root_inverse)


HIGH = lax.Precision.HIGHEST


def apply_local(operator, local_iter, order):
    def single(items):
        matrix, values, perm = items
        blocks = values.reshape(8, BLOCK, CASES)
        gathered = blocks[perm].reshape(8 * BLOCK, CASES)
        result = jnp.dot(matrix, gathered, preferred_element_type=jnp.float32).reshape(8, BLOCK, CASES)
        return jnp.zeros_like(result).at[perm].set(result)

    count = SX * SY * SZ
    outputs = lax.map(single, (operator.reshape(count, IFACE, IFACE), local_iter.reshape(count, IFACE, CASES), order.reshape(count, 8)))
    return outputs.reshape(SX, SY, SZ, 8, BLOCK, CASES)


def assemble(product):
    result = product
    result = result.at[1:, :, :, 0].add(product[:-1, :, :, 1])
    result = result.at[:-1, :, :, 1].add(product[1:, :, :, 0])
    result = result.at[:, 1:, :, 2].add(product[:, :-1, :, 3])
    result = result.at[:, :-1, :, 3].add(product[:, 1:, :, 2])
    result = result.at[:, :, 1:, 4].add(product[:, :, :-1, 5])
    result = result.at[:, :, :-1, 5].add(product[:, :, 1:, 4])
    return result.reshape(SX, SY, SZ, IFACE, CASES)


def reference(loads, start, interface_op, block_order, interface_weights, coarse_modes, region_weights, region_inverse, root_inverse):
    solution = start.astype(jnp.float32)
    for step in range(ITERS):
        local_iter = solution.astype(jnp.bfloat16)
        product = apply_local(interface_op, local_iter, block_order)
        assembled = assemble(product)
        residual = loads.astype(jnp.float32) - assembled
        coarse = jnp.einsum("abcmi,abcin->abcmn", coarse_modes, residual, precision=HIGH)
        stacked = coarse.reshape(SX, RORD, CASES)
        region_part = jnp.einsum("xij,xjn->xin", region_inverse, stacked, precision=HIGH).reshape(SX, SY, SZ, MODES, CASES)
        root_input = jnp.einsum("abcmk,abcmn->akn", region_weights, coarse, precision=HIGH).reshape(ROOT, CASES)
        root_part = jnp.dot(root_inverse, root_input, precision=HIGH).reshape(SX, RM, CASES)
        amplitude = region_part + jnp.einsum("abcmk,akn->abcmn", region_weights, root_part, precision=HIGH)
        solution = solution + interface_weights[..., None] * residual + jnp.einsum("abcmi,abcmn->abcin", coarse_modes, amplitude, precision=HIGH)
    return solution
```

```python
import functools
import itertools

import jax
import jax.numpy as jnp
from jax import lax
from jax.experimental import pallas as pl
from jax.experimental.pallas import tpu as pltpu
from jax.sharding import PartitionSpec as P

ITERS = 2
FACES = 8
AXES = ("gx", "gy", "gz")
F32 = jnp.float32
BF16 = jnp.bfloat16
VMEM = pl.BlockSpec(memory_space=pltpu.VMEM)
SMEM = pl.BlockSpec(memory_space=pltpu.SMEM)
ROWS = (((1,), (0,)), ((), ()))
COLS = (((0,), (0,)), ((), ()))


def neighbour_pairs(count, odd):
    pairs = []
    for low in range(odd, count - 1, 2):
        pairs += [(low, low + 1), (low + 1, low)]
    return pairs


def swap_list(sizes):
    swaps = []
    for dim, count in enumerate(sizes):
        for odd in (0, 1):
            if neighbour_pairs(count, odd):
                swaps.append((dim, odd))
    return swaps


def swap_face(dim, odd):
    high = (lax.axis_index(AXES[dim]) + odd + 1) % 2
    return 2 * dim + high


def partner(index, offset, count):
    if count & (count - 1):
        return (index + offset) % count
    return index ^ offset


def source(index, offset, count):
    if count & (count - 1):
        return lax.rem(index + count - offset, count)
    return index ^ offset


def split(value):
    high = value.astype(BF16)
    return high, (value - high.astype(F32)).astype(BF16)


def dot3(left, right, dims=ROWS):
    left_high, left_low = split(left)
    right_high, right_low = split(right)
    dot = functools.partial(lax.dot_general, dimension_numbers=dims, preferred_element_type=F32)
    return dot(left_high, right_high) + (dot(left_low, right_high) + dot(left_high, right_low))


def call(body, outs, ins, name, scratch=()):
    return pl.pallas_call(
        body,
        out_shape=[jax.ShapeDtypeStruct(shape, dtype) for shape, dtype in outs],
        in_specs=[SMEM if item.dtype == jnp.int32 else VMEM for item in ins],
        out_specs=[VMEM] * len(outs),
        scratch_shapes=list(scratch),
        compiler_params=pltpu.CompilerParams(vmem_limit_bytes=16 * 1024 * 1024),
        name=name,
    )(*ins)


def rows_of(index, height):
    return pl.ds(pl.multiple_of(index * height, height), height)


def multiply(swaps, order, matrix, read, loads, rest, messages, local_iter, product):
    height = matrix.shape[0] // FACES
    for j in range(FACES):
        local_iter[j * height : (j + 1) * height, :] = read(rows_of(order[j], height))
    product[...] = jnp.dot(matrix[...], local_iter[...], preferred_element_type=F32)
    inverse = [rows_of(order[j], height) for j in range(FACES)]
    for j in range(FACES):
        block = slice(j * height, (j + 1) * height)
        rest[inverse[j], :] = loads[inverse[j], :].astype(F32) - product[block, :]
    for (dim, odd), message in zip(swaps, messages):
        face = rows_of(swap_face(dim, odd), height)
        message[...] = loads[face, :].astype(F32) - rest[face, :]


def first_kernel(swaps, order, matrix, start, loads, rest, *more):
    messages, (local_iter, product) = more[: len(swaps)], more[len(swaps) :]

    def read(rows):
        return start[rows, :]

    multiply(swaps, order, matrix, read, loads, rest, messages, local_iter, product)


def residual_kernel(swaps, rest, modes, root_map, *more):
    halos, (residual, coarse, root) = more[: len(swaps)], more[len(swaps) :]
    height = rest.shape[0] // FACES
    residual[...] = rest[...]
    for (dim, odd), halo in zip(swaps, halos):
        face = rows_of(swap_face(dim, odd), height)
        residual[face, :] -= halo[...]
    coarse[...] = dot3(modes[...], residual[...])
    root[...] = dot3(root_map[...], coarse[...], COLS)


def root_kernel(count, coarse, root_inverse, root, *more):
    received, (message, stack) = more[: count - 1], more[count - 1 :]
    modes, height = coarse.shape[0], root.shape[0]
    me = lax.axis_index("gx")
    stack[rows_of(me, height), :] = root[...]
    for offset, piece in enumerate(received, 1):
        stack[rows_of(source(me, offset, count), height), :] = piece[...]
    message[:modes, :] = coarse[...]
    message[modes:, :] = dot3(root_inverse[...], stack[...])


def pair_kernel(modes, first, *more):
    received, out = more[:-1], more[-1]
    height = first.shape[0]
    total = first[modes:, :]
    out[:modes, :] = first[:modes, :]
    for k, piece in enumerate(received, 1):
        out[k * modes : (k + 1) * modes, :] = piece[:modes, :]
        total = total + piece[modes:, :]
    out[(len(received) + 1) * modes :, :] = total


def amplitude_of(members, sizes, region_rows, root_map, own, other, stack):
    modes = root_map.shape[0]
    y, z = lax.axis_index("gy"), lax.axis_index("gz")
    half = sizes[0] // 2
    count = len(members)
    for k, (dy, dz) in enumerate(members):
        at_y = 2 * source(y // 2, dy, half) + y % 2
        at_z = source(z, dz, sizes[1])
        piece = slice(k * modes, (k + 1) * modes)
        stack[rows_of(at_y * sizes[1] + at_z, modes), :] = own[piece, :]
        stack[rows_of((at_y ^ 1) * sizes[1] + at_z, modes), :] = other[piece, :]
    root_part = own[count * modes :, :] + other[count * modes :, :]
    return dot3(region_rows[...], stack[...]) + dot3(root_map[...], root_part)


def update(members, sizes, solution, residual, weights, modes, root_map, region_rows, own, other, stack, write):
    height = residual.shape[0] // FACES
    amplitude = amplitude_of(members, sizes, region_rows, root_map, own, other, stack)
    lanes = residual.shape[1]
    correction = dot3(modes[...], amplitude, COLS)
    for j in range(FACES):
        block = slice(j * height, (j + 1) * height)
        scale = jnp.broadcast_to(weights[:, block], (height, height)).T[:, :1]
        write(
            block,
            solution[block, :].astype(F32) + scale * residual[block, :] + correction[block, :],
        )


def middle_kernel(
    swaps, members, sizes, order, matrix, solution, loads, residual, weights, modes, root_map, region_rows,
    own, other, next_solution, rest, *more
):
    messages, (stack, local_iter, product) = more[: len(swaps)], more[len(swaps) :]

    def write(block, value):
        next_solution[block, :] = value

    update(members, sizes, solution, residual, weights, modes, root_map, region_rows, own, other, stack, write)

    def read(rows):
        return next_solution[rows, :].astype(BF16)

    multiply(swaps, order, matrix, read, loads, rest, messages, local_iter, product)


def last_kernel(
    members, sizes, solution, residual, weights, modes, root_map, region_rows, own, other, next_solution, stack
):
    def write(block, value):
        next_solution[block, :] = value

    update(members, sizes, solution, residual, weights, modes, root_map, region_rows, own, other, stack, write)


def per_device(
    loads,
    start,
    interface_op,
    block_order,
    interface_weights,
    coarse_modes,
    region_weights,
    region_inverse,
    root_inverse,
):
    sizes = tuple(lax.axis_size(axis) for axis in AXES)
    iface = interface_op.shape[-1]
    cases = loads.shape[-1]
    height = iface // FACES
    matrix = interface_op.reshape(iface, iface)
    order = block_order.reshape(FACES)
    weights = interface_weights.reshape(1, iface)
    modes = coarse_modes.reshape(coarse_modes.shape[-2], iface)
    mode_count = modes.shape[0]
    root_map = region_weights.reshape(mode_count, region_weights.shape[-1])
    root_modes = root_map.shape[1]
    region_rows = region_inverse.reshape(mode_count, region_inverse.shape[-1])
    target = loads.reshape(iface, cases)
    solution = start.reshape(iface, cases)

    swaps = swap_list(sizes)
    half = sizes[1] // 2
    members = list(itertools.product(range(half), range(sizes[2])))

    full = ((iface, cases), F32)
    face = ((height, cases), F32)
    work = [pltpu.VMEM((iface, cases), BF16), pltpu.VMEM((iface, cases), F32)]
    stack = [pltpu.VMEM((region_rows.shape[1], cases), F32)]

    for step in range(ITERS):
        if step == 0:
            rest, *messages = call(
                functools.partial(first_kernel, swaps),
                [full] + [face] * len(swaps),
                [order, matrix, solution, target],
                "first_product",
                work,
            )
        else:
            solution, rest, *messages = call(
                functools.partial(middle_kernel, swaps, members, sizes[1:]),
                [full, full] + [face] * len(swaps),
                [order, matrix, solution, target, residual, weights, modes, root_map, region_rows, own, other],
                "update_product",
                stack + work,
            )
        halos = [
            lax.ppermute(message, AXES[dim], neighbour_pairs(sizes[dim], odd))
            for (dim, odd), message in zip(swaps, messages)
        ]
        residual, coarse, root = call(
            functools.partial(residual_kernel, swaps),
            [full, ((mode_count, cases), F32), ((root_modes, cases), F32)],
            [rest, modes, root_map] + halos,
            "residual_coarse",
        )
        received = [
            lax.ppermute(root, "gx", [(i, partner(i, offset, sizes[0])) for i in range(sizes[0])])
            for offset in range(1, sizes[0])
        ]
        (message,) = call(
            functools.partial(root_kernel, sizes[0]),
            [((mode_count + root_modes, cases), F32)],
            [coarse, root_inverse, root] + received,
            "root_part",
            [pltpu.VMEM((root_inverse.shape[1], cases), F32)],
        )
        pieces = []
        for dy, dz in members[1:]:
            moves = [
                (y * sizes[2] + z, (2 * partner(y // 2, dy, half) + y % 2) * sizes[2] + partner(z, dz, sizes[2]))
                for y in range(sizes[1])
                for z in range(sizes[2])
            ]
            pieces.append(lax.ppermute(message, ("gy", "gz"), moves))
        (own,) = call(
            functools.partial(pair_kernel, mode_count),
            [((len(members) * mode_count + root_modes, cases), F32)],
            [message] + pieces,
            "pair_message",
        )
        other = lax.ppermute(own, "gy", neighbour_pairs(sizes[1], 0))
    (solution,) = call(
        functools.partial(last_kernel, members, sizes[1:]),
        [full],
        [solution, residual, weights, modes, root_map, region_rows, own, other],
        "update_last",
        stack,
    )
    return solution.reshape(1, 1, 1, iface, cases)


def solution(mesh):
    placed = (
        P("gx", "gy", "gz", None, None),
        P("gx", "gy", "gz", None, None),
        P("gx", "gy", "gz", None, None),
        P("gx", "gy", "gz", None),
        P("gx", "gy", "gz", None),
        P("gx", "gy", "gz", None, None),
        P("gx", "gy", "gz", None, None),
        P("gx", ("gy", "gz"), None),
        P("gx", None),
    )
    return jax.shard_map(
        per_device,
        mesh=mesh,
        in_specs=placed,
        out_specs=P("gx", "gy", "gz", None, None),
        check_vma=False,
    )
```

```python
import functools
import itertools

import jax
import jax.numpy as jnp
from jax import lax
from jax.experimental import pallas as pl
from jax.experimental.pallas import tpu as pltpu
from jax.sharding import PartitionSpec as P

ITERS = 2
FACES = 8
AXES = ("gx", "gy", "gz")
F32 = jnp.float32
BF16 = jnp.bfloat16
ROWS = (((1,), (0,)), ((), ()))
COLS = (((0,), (0,)), ((), ()))


def neighbour_pairs(count, odd):
    pairs = []
    for low in range(odd, count - 1, 2):
        pairs += [(low, low + 1), (low + 1, low)]
    return pairs


def swap_list(sizes):
    swaps = []
    for dim, count in enumerate(sizes):
        for odd in (0, 1):
            if neighbour_pairs(count, odd):
                swaps.append((dim, odd))
    return swaps


def swap_face(dim, odd):
    high = (lax.axis_index(AXES[dim]) + odd + 1) % 2
    return 2 * dim + high


def partner(index, offset, count):
    if count & (count - 1):
        return (index + offset) % count
    return index ^ offset


def source(index, offset, count):
    if count & (count - 1):
        return lax.rem(index + count - offset, count)
    return index ^ offset


def split(value):
    high = value.astype(BF16)
    return high, (value - high.astype(F32)).astype(BF16)


def dot3(left, right, dims=ROWS):
    left_high, left_low = split(left)
    right_high, right_low = split(right)
    dot = functools.partial(lax.dot_general, dimension_numbers=dims, preferred_element_type=F32)
    return dot(left_high, right_high) + (dot(left_low, right_high) + dot(left_high, right_low))


def call(body, outs, ins, name, scratch=(), fixed=0):
    spaces = [pltpu.HBM] * fixed + [pltpu.VMEM] * (len(ins) - fixed)
    return pl.pallas_call(
        body,
        out_shape=[item(shape, dtype) for item, shape, dtype in outs],
        in_specs=[pl.BlockSpec(memory_space=space) for space in spaces],
        out_specs=[
            pl.BlockSpec(memory_space=pltpu.HBM if item is jax.ShapeDtypeStruct else pltpu.VMEM)
            for item, _, _ in outs
        ],
        scratch_shapes=list(scratch),
        compiler_params=pltpu.CompilerParams(vmem_limit_bytes=8 * 1024 * 1024),
        name=name,
    )(*[pltpu.with_memory_space_constraint(item, space) for item, space in zip(ins, spaces)])


def rows_of(index, height):
    return pl.ds(pl.multiple_of(index * height, height), height)


def send_rest(swaps, order, loads, product, rest, messages):
    height = rest.shape[0] // FACES
    for j in range(FACES):
        face = rows_of(order[0, j], height)
        rest[face, :] = product[j * height : (j + 1) * height, :]
    for (dim, odd), message in zip(swaps, messages):
        message[...] = rest[rows_of(swap_face(dim, odd), height), :]
    rest[...] = loads[...].astype(F32) - rest[...]


def reorder(order, read, local_iter):
    height = local_iter.shape[0] // FACES
    for j in range(FACES):
        local_iter[j * height : (j + 1) * height, :] = read(rows_of(order[0, j], height))


def first_kernel(swaps, order_hbm, *refs):
    hbm, held, refs = refs[:8], refs[8:16], refs[16:]
    (rest, *messages), scratch = refs[: 1 + len(swaps)], refs[1 + len(swaps) :]
    matrix, loads, modes_t, modes_s, scale, *small = held
    order, start, modes, weights, local_iter, product, sems = scratch
    matrix_hbm, start_hbm, loads_hbm, modes_hbm, weights_hbm, *small_hbm = hbm
    height = rest.shape[0] // FACES
    part = matrix.shape[0] // 2

    pairs = [(order_hbm, order), (modes_hbm, modes), (weights_hbm, weights), (start_hbm, start)]
    pairs += [(matrix_hbm.at[k * part : (k + 1) * part, :], matrix.at[k * part : (k + 1) * part, :]) for k in range(2)]
    pairs += [(loads_hbm, loads)] + list(zip(small_hbm, small))
    copies = [pltpu.make_async_copy(*pair, sems.at[k]) for k, pair in enumerate(pairs)]
    for copy in copies:
        copy.start()
    copies[1].wait()
    high, low = split(modes[...])
    count = high.shape[0]
    modes_s[:count, :] = high
    modes_s[count : 2 * count, :] = low
    modes_s[2 * count :, :] = high
    modes_t[...] = jnp.concatenate([high.T, low.T, high.T], axis=1)
    copies[2].wait()
    for j in range(FACES):
        block = slice(j * height, (j + 1) * height)
        scale[block, :] = jnp.broadcast_to(weights[:, block], (height, height)).T
    copies[0].wait()
    copies[3].wait()
    reorder(order, lambda rows: start[rows, :], local_iter)
    for k in range(2):
        copies[4 + k].wait()
        rows = slice(k * part, (k + 1) * part)
        product[rows, :] = jnp.dot(matrix[rows, :], local_iter[...], preferred_element_type=F32)
    for copy in copies[6:]:
        copy.wait()
    send_rest(swaps, order, loads, product, rest, messages)


def residual_kernel(swaps, rest, modes_s, root_map, *more):
    halos, (residual, coarse, root) = more[: len(swaps)], more[len(swaps) :]
    height = rest.shape[0] // FACES
    count = coarse.shape[0]
    residual[...] = rest[...]
    for (dim, odd), halo in zip(swaps, halos):
        face = rows_of(swap_face(dim, odd), height)
        residual[face, :] -= halo[...]
    high, low = split(residual[...])
    both = jnp.dot(modes_s[: 2 * count, :], high, preferred_element_type=F32)
    fine = jnp.dot(modes_s[:count, :], low, preferred_element_type=F32)
    coarse[...] = both[:count, :] + (both[count:, :] + fine)
    root[...] = dot3(root_map[...], coarse[...], COLS)


def root_kernel(count, coarse, root_inverse, root, *more):
    received, (message, stack) = more[: count - 1], more[count - 1 :]
    modes, height = coarse.shape[0], root.shape[0]
    me = lax.axis_index("gx")
    stack[rows_of(me, height), :] = root[...]
    for offset, piece in enumerate(received, 1):
        stack[rows_of(source(me, offset, count), height), :] = piece[...]
    message[:modes, :] = coarse[...]
    message[modes:, :] = dot3(root_inverse[...], stack[...])


def pair_kernel(modes, first, *more):
    received, out = more[:-1], more[-1]
    height = first.shape[0]
    total = first[modes:, :]
    out[:modes, :] = first[:modes, :]
    for k, piece in enumerate(received, 1):
        out[k * modes : (k + 1) * modes, :] = piece[:modes, :]
        total = total + piece[modes:, :]
    out[(len(received) + 1) * modes :, :] = total


def amplitude_of(members, sizes, region_rows, root_map, own, other, stack):
    modes = root_map.shape[0]
    y, z = lax.axis_index("gy"), lax.axis_index("gz")
    half = sizes[0] // 2
    count = len(members)
    for k, (dy, dz) in enumerate(members):
        at_y = 2 * source(y // 2, dy, half) + y % 2
        at_z = source(z, dz, sizes[1])
        piece = slice(k * modes, (k + 1) * modes)
        stack[rows_of(at_y * sizes[1] + at_z, modes), :] = own[piece, :]
        stack[rows_of((at_y ^ 1) * sizes[1] + at_z, modes), :] = other[piece, :]
    root_part = own[count * modes :, :] + other[count * modes :, :]
    return dot3(region_rows[...], stack[...]) + dot3(root_map[...], root_part)


def correction_of(modes_t, amplitude):
    high, low = split(amplitude)
    tall = jnp.concatenate([high, high, low], axis=0)
    return jnp.dot(modes_t[...], tall, preferred_element_type=F32)


def scaled(scale, residual, block):
    lanes = residual.shape[1] // scale.shape[1]
    return jnp.concatenate([scale[block, :]] * lanes, axis=1) * residual[block, :]


def middle_kernel(
    swaps, members, sizes, order_hbm, matrix, solution, loads, residual, scale, modes_t, root_map, region_rows,
    own, other, next_solution, rest, *more
):
    messages, (stack, local_iter, product, order, sem) = more[: len(swaps)], more[len(swaps) :]
    copy = pltpu.make_async_copy(order_hbm, order, sem)
    copy.start()
    amplitude = amplitude_of(members, sizes, region_rows, root_map, own, other, stack)
    product[...] = correction_of(modes_t, amplitude)
    every = slice(0, residual.shape[0])
    next_solution[...] = solution[...].astype(F32) + scaled(scale, residual, every) + product[...]
    copy.wait()
    reorder(order, lambda rows: next_solution[rows, :].astype(BF16), local_iter)
    product[...] = jnp.dot(matrix[...], local_iter[...], preferred_element_type=F32)
    send_rest(swaps, order, loads, product, rest, messages)


def last_kernel(
    members, sizes, solution, residual, scale, modes_t, root_map, region_rows, own, other, out, stack, result, sems
):
    amplitude = amplitude_of(members, sizes, region_rows, root_map, own, other, stack)
    part = result.shape[0] // 4
    copies = []
    for k in range(4):
        block = slice(k * part, (k + 1) * part)
        base = solution[block, :].astype(F32) + scaled(scale, residual, block)
        result[block, :] = base + correction_of(modes_t.at[block, :], amplitude)
        copies.append(pltpu.make_async_copy(result.at[block, :], out.at[block, :], sems.at[k]))
        copies[-1].start()
    for copy in copies:
        copy.wait()


def per_device(
    loads,
    start,
    interface_op,
    block_order,
    interface_weights,
    coarse_modes,
    region_weights,
    region_inverse,
    root_inverse,
):
    sizes = tuple(lax.axis_size(axis) for axis in AXES)
    iface = interface_op.shape[-1]
    cases = loads.shape[-1]
    height = iface // FACES
    matrix = interface_op.reshape(iface, iface)
    order = block_order.reshape(1, FACES)
    weights = interface_weights.reshape(1, iface)
    modes = coarse_modes.reshape(coarse_modes.shape[-2], iface)
    mode_count = modes.shape[0]
    root_map = region_weights.reshape(mode_count, region_weights.shape[-1])
    root_modes = root_map.shape[1]
    region_rows = region_inverse.reshape(mode_count, region_inverse.shape[-1])
    target = loads.reshape(iface, cases)
    solution = start.reshape(iface, cases)

    swaps = swap_list(sizes)
    half = sizes[1] // 2
    members = list(itertools.product(range(half), range(sizes[2])))

    full = (pltpu.VMEM, (iface, cases), F32)
    face = (pltpu.VMEM, (height, cases), F32)
    work = [pltpu.VMEM((iface, cases), BF16), pltpu.VMEM((iface, cases), F32)]
    stack = [pltpu.VMEM((region_rows.shape[1], cases), F32)]
    places = [pltpu.SMEM((1, FACES), jnp.int32)]

    for step in range(ITERS):
        if step == 0:
            held = [
                (pltpu.VMEM, matrix.shape, BF16),
                (pltpu.VMEM, target.shape, BF16),
                (pltpu.VMEM, (iface, 3 * mode_count), BF16),
                (pltpu.VMEM, (3 * mode_count, iface), BF16),
                (pltpu.VMEM, (iface, height), F32),
                (pltpu.VMEM, root_map.shape, F32),
                (pltpu.VMEM, region_rows.shape, F32),
                (pltpu.VMEM, root_inverse.shape, F32),
            ]
            inputs = [order, matrix, solution, target, modes, weights, root_map, region_rows, root_inverse]
            outs = call(
                functools.partial(first_kernel, swaps),
                held + [full] + [face] * len(swaps),
                inputs,
                "first_product",
                places
                + [pltpu.VMEM((iface, cases), BF16), pltpu.VMEM(modes.shape, F32), pltpu.VMEM(weights.shape, F32)]
                + work
                + [pltpu.SemaphoreType.DMA((10,))],
                len(inputs),
            )
            matrix, target, modes_t, modes_s, scale, root_map, region_rows, root_inverse, rest, *messages = outs
        else:
            solution, rest, *messages = call(
                functools.partial(middle_kernel, swaps, members, sizes[1:]),
                [full, full] + [face] * len(swaps),
                [order, matrix, solution, target, residual, scale, modes_t, root_map, region_rows, own, other],
                "update_product",
                stack + work + places + [pltpu.SemaphoreType.DMA],
                1,
            )
        halos = [
            lax.ppermute(message, AXES[dim], neighbour_pairs(sizes[dim], odd))
            for (dim, odd), message in zip(swaps, messages)
        ]
        residual, coarse, root = call(
            functools.partial(residual_kernel, swaps),
            [full, (pltpu.VMEM, (mode_count, cases), F32), (pltpu.VMEM, (root_modes, cases), F32)],
            [rest, modes_s, root_map] + halos,
            "residual_coarse",
        )
        received = [
            lax.ppermute(root, "gx", [(i, partner(i, offset, sizes[0])) for i in range(sizes[0])])
            for offset in range(1, sizes[0])
        ]
        (message,) = call(
            functools.partial(root_kernel, sizes[0]),
            [(pltpu.VMEM, (mode_count + root_modes, cases), F32)],
            [coarse, root_inverse, root] + received,
            "root_part",
            [pltpu.VMEM((root_inverse.shape[1], cases), F32)],
        )
        pieces = []
        for dy, dz in members[1:]:
            moves = [
                (y * sizes[2] + z, (2 * partner(y // 2, dy, half) + y % 2) * sizes[2] + partner(z, dz, sizes[2]))
                for y in range(sizes[1])
                for z in range(sizes[2])
            ]
            pieces.append(lax.ppermute(message, ("gy", "gz"), moves))
        (own,) = call(
            functools.partial(pair_kernel, mode_count),
            [(pltpu.VMEM, (len(members) * mode_count + root_modes, cases), F32)],
            [message] + pieces,
            "pair_message",
        )
        other = lax.ppermute(own, "gy", neighbour_pairs(sizes[1], 0))
    (solution,) = call(
        functools.partial(last_kernel, members, sizes[1:]),
        [(jax.ShapeDtypeStruct, (iface, cases), F32)],
        [solution, residual, scale, modes_t, root_map, region_rows, own, other],
        "update_last",
        stack + [pltpu.VMEM((iface, cases), F32), pltpu.SemaphoreType.DMA((4,))],
    )
    return solution.reshape(1, 1, 1, iface, cases)


def solution(mesh):
    placed = (
        P("gx", "gy", "gz", None, None),
        P("gx", "gy", "gz", None, None),
        P("gx", "gy", "gz", None, None),
        P("gx", "gy", "gz", None),
        P("gx", "gy", "gz", None),
        P("gx", "gy", "gz", None, None),
        P("gx", "gy", "gz", None, None),
        P("gx", ("gy", "gz"), None),
        P("gx", None),
    )
    return jax.shard_map(
        per_device,
        mesh=mesh,
        in_specs=placed,
        out_specs=P("gx", "gy", "gz", None, None),
        check_vma=False,
    )
```

```python
import functools
import itertools

import jax
import jax.numpy as jnp
from jax import lax
from jax.experimental import pallas as pl
from jax.experimental.pallas import tpu as pltpu
from jax.sharding import PartitionSpec as P

ITERS = 2
FACES = 8
AXES = ("gx", "gy", "gz")
F32 = jnp.float32
BF16 = jnp.bfloat16
ROWS = (((1,), (0,)), ((), ()))
COLS = (((0,), (0,)), ((), ()))


def neighbour(index, count, odd):
    other = index + 1 if index % 2 == odd else index - 1
    return other if 0 <= other < count else None


def swap_list(sizes):
    swaps = [(dim, odd) for odd in (1, 0) for dim in (0, 1, 2) if sizes[dim] > 1 + odd]
    return sorted(swaps, key=lambda swap: swap == (1, 0))


def flat(sizes, place):
    return (place[0] * sizes[1] + place[1]) * sizes[2] + place[2]


def swap_pairs(sizes, dim, odd):
    pairs = []
    for place in itertools.product(*map(range, sizes)):
        there = list(place)
        other = neighbour(place[dim], sizes[dim], odd)
        if other is not None:
            there[dim] = other
        elif odd and sizes[dim] % 2 == 0:
            if dim == 1:
                there[1] = sizes[1] - 1 - place[1]
            elif sizes[1] % 2 == 0:
                there[1] = place[1] ^ 1
        if tuple(there) != place:
            pairs.append((flat(sizes, place), flat(sizes, there)))
    return pairs


def swap_face(dim, odd):
    high = (lax.axis_index(AXES[dim]) + odd + 1) % 2
    return 2 * dim + high


def add_halos(swaps, sizes, total, halos):
    height = total.shape[0] // FACES
    for (dim, odd), halo in zip(swaps, halos):
        face = swap_face(dim, odd)
        other = lax.axis_index(AXES[dim]) + 2 * (face - 2 * dim) - 1

        @pl.when(jnp.logical_and(other >= 0, other < sizes[dim]))
        def _():
            total[rows_of(face, height), :] -= halo[...]


def partner(index, offset, count):
    if count & (count - 1):
        return (index + offset) % count
    return index ^ offset


def source(index, offset, count):
    if count & (count - 1):
        return lax.rem(index + count - offset, count)
    return index ^ offset


def split(value):
    high = value.astype(BF16)
    return high, (value - high.astype(F32)).astype(BF16)


def dot3(left, right, dims=ROWS):
    left_high, left_low = split(left)
    right_high, right_low = split(right)
    dot = functools.partial(lax.dot_general, dimension_numbers=dims, preferred_element_type=F32)
    return dot(left_high, right_high) + (dot(left_low, right_high) + dot(left_high, right_low))


def call(body, outs, ins, name, scratch=(), fixed=0):
    spaces = [pltpu.HBM] * fixed + [pltpu.VMEM] * (len(ins) - fixed)
    return pl.pallas_call(
        body,
        out_shape=[item(shape, dtype) for item, shape, dtype in outs],
        in_specs=[pl.BlockSpec(memory_space=space) for space in spaces],
        out_specs=[
            pl.BlockSpec(memory_space=pltpu.HBM if item is jax.ShapeDtypeStruct else pltpu.VMEM)
            for item, _, _ in outs
        ],
        scratch_shapes=list(scratch),
        compiler_params=pltpu.CompilerParams(vmem_limit_bytes=8 * 1024 * 1024),
        name=name,
    )(*[pltpu.with_memory_space_constraint(item, space) for item, space in zip(ins, spaces)])


def rows_of(index, height):
    return pl.ds(pl.multiple_of(index * height, height), height)


def send_rest(swaps, order, loads, product, rest, messages):
    height = rest.shape[0] // FACES
    for j in range(FACES):
        face = rows_of(order[0, j], height)
        rest[face, :] = product[j * height : (j + 1) * height, :]
    for (dim, odd), message in zip(swaps, messages):
        message[...] = rest[rows_of(swap_face(dim, odd), height), :]
    rest[...] = loads[...].astype(F32) - rest[...]


def reorder(order, read, local_iter):
    height = local_iter.shape[0] // FACES
    for j in range(FACES):
        local_iter[j * height : (j + 1) * height, :] = read(rows_of(order[0, j], height))


def first_kernel(swaps, order_hbm, *refs):
    hbm, held, refs = refs[:8], refs[8:15], refs[15:]
    (rest, *messages), scratch = refs[: 1 + len(swaps)], refs[1 + len(swaps) :]
    matrix, loads = held[:2]
    order, start, local_iter, product, sems = scratch
    matrix_hbm, start_hbm = hbm[:2]
    parts = 4
    part = matrix.shape[0] // parts

    pairs = [(order_hbm, order), (start_hbm, start)]
    for k in range(parts):
        rows = slice(k * part, (k + 1) * part)
        pairs.append((matrix_hbm.at[rows, :], matrix.at[rows, :]))
    pairs += list(zip(hbm[2:], held[1:]))
    copies = [pltpu.make_async_copy(*pair, sems.at[k]) for k, pair in enumerate(pairs)]
    for copy in copies:
        copy.start()
    copies[0].wait()
    copies[1].wait()
    reorder(order, lambda rows: start[rows, :], local_iter)
    for k in range(parts):
        copies[2 + k].wait()
        rows = slice(k * part, (k + 1) * part)
        product[rows, :] = jnp.dot(matrix[rows, :], local_iter[...], preferred_element_type=F32)
    for copy in copies[2 + parts :]:
        copy.wait()
    send_rest(swaps, order, loads, product, rest, messages)


def constants_kernel(modes, weights, modes_t, modes_s, scale):
    high, low = split(modes[...])
    count = high.shape[0]
    height = scale.shape[1]
    modes_s[:count, :] = high
    modes_s[count:, :] = low
    modes_t[...] = jnp.concatenate([high.T, low.T, high.T], axis=1)
    for j in range(FACES):
        block = slice(j * height, (j + 1) * height)
        scale[block, :] = jnp.broadcast_to(weights[:, block], (height, height)).T


def residual_kernel(swaps, sizes, rest, modes_s, root_map, *more):
    halos, (residual, coarse, root) = more[: len(swaps)], more[len(swaps) :]
    count = coarse.shape[0]
    residual[...] = rest[...]
    add_halos(swaps, sizes, residual, halos)
    high, low = split(residual[...])
    both = jnp.dot(modes_s[...], high, preferred_element_type=F32)
    fine = jnp.dot(modes_s[:count, :], low, preferred_element_type=F32)
    coarse[...] = both[:count, :] + (both[count:, :] + fine)
    root[...] = dot3(root_map[...], coarse[...])


def root_kernel(count, coarse, root_inverse, root, *more):
    received, (message, stack) = more[: count - 1], more[count - 1 :]
    modes, height = coarse.shape[0], root.shape[0]
    me = lax.axis_index("gx")
    stack[rows_of(me, height), :] = root[...]
    for offset, piece in enumerate(received, 1):
        stack[rows_of(source(me, offset, count), height), :] = piece[...]
    message[:modes, :] = coarse[...]
    message[modes:, :] = dot3(root_inverse[...], stack[...])


def pair_kernel(modes, first, *more):
    received, out = more[:-1], more[-1]
    height = first.shape[0]
    total = first[modes:, :]
    out[:modes, :] = first[:modes, :]
    for k, piece in enumerate(received, 1):
        out[k * modes : (k + 1) * modes, :] = piece[:modes, :]
        total = total + piece[modes:, :]
    out[(len(received) + 1) * modes :, :] = total


def amplitude_of(members, sizes, region_rows, root_map, own, other, stack):
    modes = root_map.shape[1]
    y, z = lax.axis_index("gy"), lax.axis_index("gz")
    half = sizes[0] // 2
    count = len(members)
    for k, (dy, dz) in enumerate(members):
        at_y = 2 * source(y // 2, dy, half) + y % 2
        at_z = source(z, dz, sizes[1])
        piece = slice(k * modes, (k + 1) * modes)
        stack[rows_of(at_y * sizes[1] + at_z, modes), :] = own[piece, :]
        stack[rows_of((at_y ^ 1) * sizes[1] + at_z, modes), :] = other[piece, :]
    root_part = own[count * modes :, :] + other[count * modes :, :]
    return dot3(region_rows[...], stack[...]) + dot3(root_map[...], root_part, COLS)


def correction_of(modes_t, amplitude):
    high, low = split(amplitude)
    tall = jnp.concatenate([high, high, low], axis=0)
    return jnp.dot(modes_t[...], tall, preferred_element_type=F32)


def scaled(scale, residual, block):
    lanes = residual.shape[1] // scale.shape[1]
    return jnp.concatenate([scale[block, :]] * lanes, axis=1) * residual[block, :]


def middle_kernel(
    swaps, members, sizes, order_hbm, matrix, solution, loads, residual, scale, modes_t, root_map, region_rows,
    own, other, next_solution, rest, *more
):
    messages, (stack, local_iter, product, order, sem) = more[: len(swaps)], more[len(swaps) :]
    copy = pltpu.make_async_copy(order_hbm, order, sem)
    copy.start()
    amplitude = amplitude_of(members, sizes, region_rows, root_map, own, other, stack)
    product[...] = correction_of(modes_t, amplitude)
    every = slice(0, residual.shape[0])
    next_solution[...] = solution[...].astype(F32) + scaled(scale, residual, every) + product[...]
    copy.wait()
    reorder(order, lambda rows: next_solution[rows, :].astype(BF16), local_iter)
    product[...] = jnp.dot(matrix[...], local_iter[...], preferred_element_type=F32)
    send_rest(swaps, order, loads, product, rest, messages)


def last_kernel(
    members, sizes, solution, residual, scale, modes_t, root_map, region_rows, own, other, out, stack, result, sems
):
    amplitude = amplitude_of(members, sizes, region_rows, root_map, own, other, stack)
    part = result.shape[0] // 4
    copies = []
    for k in range(4):
        block = slice(k * part, (k + 1) * part)
        base = solution[block, :].astype(F32) + scaled(scale, residual, block)
        result[block, :] = base + correction_of(modes_t.at[block, :], amplitude)
        copies.append(pltpu.make_async_copy(result.at[block, :], out.at[block, :], sems.at[k]))
        copies[-1].start()
    for copy in copies:
        copy.wait()


def per_device(
    loads,
    start,
    interface_op,
    block_order,
    interface_weights,
    coarse_modes,
    region_weights,
    region_inverse,
    root_inverse,
):
    sizes = tuple(lax.axis_size(axis) for axis in AXES)
    iface = interface_op.shape[-1]
    cases = loads.shape[-1]
    height = iface // FACES
    matrix = interface_op.reshape(iface, iface)
    order = block_order.reshape(1, FACES)
    weights = interface_weights.reshape(1, iface)
    modes = coarse_modes.reshape(coarse_modes.shape[-2], iface)
    mode_count = modes.shape[0]
    root_map = region_weights.reshape(mode_count, region_weights.shape[-1]).T
    root_modes = root_map.shape[0]
    region_rows = region_inverse.reshape(mode_count, region_inverse.shape[-1])
    target = loads.reshape(iface, cases)
    solution = start.reshape(iface, cases)

    swaps = swap_list(sizes)
    half = sizes[1] // 2
    members = list(itertools.product(range(half), range(sizes[2])))

    full = (pltpu.VMEM, (iface, cases), F32)
    face = (pltpu.VMEM, (height, cases), F32)
    work = [pltpu.VMEM((iface, cases), BF16), pltpu.VMEM((iface, cases), F32)]
    stack = [pltpu.VMEM((region_rows.shape[1], cases), F32)]
    places = [pltpu.SMEM((1, FACES), jnp.int32)]

    for step in range(ITERS):
        if step == 0:
            inputs = [order, matrix, solution, target, modes, weights, root_map, region_rows, root_inverse]
            held = [(pltpu.VMEM, item.shape, item.dtype) for item in [matrix] + inputs[3:]]
            outs = call(
                functools.partial(first_kernel, swaps),
                held + [full] + [face] * len(swaps),
                inputs,
                "first_product",
                places + [pltpu.VMEM((iface, cases), BF16)] + work + [pltpu.SemaphoreType.DMA((12,))],
                len(inputs),
            )
            matrix, target, modes, weights, root_map, region_rows, root_inverse, rest, *messages = outs
            modes_t, modes_s, scale = call(
                constants_kernel,
                [
                    (pltpu.VMEM, (iface, 3 * mode_count), BF16),
                    (pltpu.VMEM, (2 * mode_count, iface), BF16),
                    (pltpu.VMEM, (iface, height), F32),
                ],
                [modes, weights],
                "constants",
            )
        else:
            solution, rest, *messages = call(
                functools.partial(middle_kernel, swaps, members, sizes[1:]),
                [full, full] + [face] * len(swaps),
                [order, matrix, solution, target, residual, scale, modes_t, root_map, region_rows, own, other],
                "update_product",
                stack + work + places + [pltpu.SemaphoreType.DMA],
                1,
            )
        halos = [
            lax.ppermute(message, AXES, swap_pairs(sizes, dim, odd))
            for (dim, odd), message in zip(swaps, messages)
        ]
        residual, coarse, root = call(
            functools.partial(residual_kernel, swaps, sizes),
            [full, (pltpu.VMEM, (mode_count, cases), F32), (pltpu.VMEM, (root_modes, cases), F32)],
            [rest, modes_s, root_map] + halos,
            "residual_coarse",
        )
        received = [
            lax.ppermute(root, "gx", [(i, partner(i, offset, sizes[0])) for i in range(sizes[0])])
            for offset in range(1, sizes[0])
        ]
        (message,) = call(
            functools.partial(root_kernel, sizes[0]),
            [(pltpu.VMEM, (mode_count + root_modes, cases), F32)],
            [coarse, root_inverse, root] + received,
            "root_part",
            [pltpu.VMEM((root_inverse.shape[1], cases), F32)],
        )
        pieces = []
        for dy, dz in members[1:]:
            moves = [
                (y * sizes[2] + z, (2 * partner(y // 2, dy, half) + y % 2) * sizes[2] + partner(z, dz, sizes[2]))
                for y in range(sizes[1])
                for z in range(sizes[2])
            ]
            pieces.append(lax.ppermute(message, ("gy", "gz"), moves))
        (own,) = call(
            functools.partial(pair_kernel, mode_count),
            [(pltpu.VMEM, (len(members) * mode_count + root_modes, cases), F32)],
            [message] + pieces,
            "pair_message",
        )
        other = lax.ppermute(own, AXES, swap_pairs(sizes, 1, 0))
    (solution,) = call(
        functools.partial(last_kernel, members, sizes[1:]),
        [(jax.ShapeDtypeStruct, (iface, cases), F32)],
        [solution, residual, scale, modes_t, root_map, region_rows, own, other],
        "update_last",
        stack + [pltpu.VMEM((iface, cases), F32), pltpu.SemaphoreType.DMA((4,))],
    )
    return solution.reshape(1, 1, 1, iface, cases)


def solution(mesh):
    placed = (
        P("gx", "gy", "gz", None, None),
        P("gx", "gy", "gz", None, None),
        P("gx", "gy", "gz", None, None),
        P("gx", "gy", "gz", None),
        P("gx", "gy", "gz", None),
        P("gx", "gy", "gz", None, None),
        P("gx", "gy", "gz", None, None),
        P("gx", ("gy", "gz"), None),
        P("gx", None),
    )
    return jax.shard_map(
        per_device,
        mesh=mesh,
        in_specs=placed,
        out_specs=P("gx", "gy", "gz", None, None),
        check_vma=False,
    )
```

```python
import functools
import itertools

import jax
import jax.numpy as jnp
from jax import lax
from jax.experimental import pallas as pl
from jax.experimental.pallas import tpu as pltpu
from jax.sharding import PartitionSpec as P

ITERS = 2
FACES = 8
AXES = ("gx", "gy", "gz")
F32 = jnp.float32
BF16 = jnp.bfloat16
ROWS = (((1,), (0,)), ((), ()))
COLS = (((0,), (0,)), ((), ()))


def neighbour(index, count, odd):
    other = index + 1 if index % 2 == odd else index - 1
    return other if 0 <= other < count else None


def swap_list(sizes):
    swaps = [(dim, odd) for odd in (1, 0) for dim in (0, 1, 2) if sizes[dim] > 1 + odd]
    return sorted(swaps, key=lambda swap: swap == (1, 0))


def flat(sizes, place):
    return (place[0] * sizes[1] + place[1]) * sizes[2] + place[2]


def swap_pairs(sizes, dim, odd):
    pairs = []
    for place in itertools.product(*map(range, sizes)):
        there = list(place)
        other = neighbour(place[dim], sizes[dim], odd)
        if other is not None:
            there[dim] = other
        elif odd and sizes[dim] % 2 == 0:
            if dim == 1:
                there[1] = sizes[1] - 1 - place[1]
            elif sizes[1] % 2 == 0:
                there[1] = place[1] ^ 1
        if tuple(there) != place:
            pairs.append((flat(sizes, place), flat(sizes, there)))
    return pairs


def swap_face(dim, odd):
    high = (lax.axis_index(AXES[dim]) + odd + 1) % 2
    return 2 * dim + high


def has_neighbour(dim, face, sizes):
    other = lax.axis_index(AXES[dim]) + 2 * (face - 2 * dim) - 1
    return jnp.logical_and(other >= 0, other < sizes[dim])


def add_halos(swaps, sizes, total, halos):
    height = total.shape[0] // FACES
    for (dim, odd), halo in zip(swaps, halos):
        face = swap_face(dim, odd)

        @pl.when(has_neighbour(dim, face, sizes))
        def _():
            total[rows_of(face, height), :] -= halo[:height, :]


def partner(index, offset, count):
    if count & (count - 1):
        return (index + offset) % count
    return index ^ offset


def source(index, offset, count):
    if count & (count - 1):
        return lax.rem(index + count - offset, count)
    return index ^ offset


def split(value):
    high = value.astype(BF16)
    return high, (value - high.astype(F32)).astype(BF16)


def dot3(left, right, dims=ROWS):
    left_high, left_low = split(left)
    right_high, right_low = split(right)
    dot = functools.partial(lax.dot_general, dimension_numbers=dims, preferred_element_type=F32)
    return dot(left_high, right_high) + (dot(left_low, right_high) + dot(left_high, right_low))


def call(body, outs, ins, name, scratch=(), fixed=0):
    spaces = [pltpu.HBM] * fixed + [pltpu.VMEM] * (len(ins) - fixed)
    return pl.pallas_call(
        body,
        out_shape=[item(shape, dtype) for item, shape, dtype in outs],
        in_specs=[pl.BlockSpec(memory_space=space) for space in spaces],
        out_specs=[
            pl.BlockSpec(memory_space=pltpu.HBM if item is jax.ShapeDtypeStruct else pltpu.VMEM)
            for item, _, _ in outs
        ],
        scratch_shapes=list(scratch),
        compiler_params=pltpu.CompilerParams(vmem_limit_bytes=8 * 1024 * 1024),
        name=name,
    )(*[pltpu.with_memory_space_constraint(item, space) for item, space in zip(ins, spaces)])


def rows_of(index, height):
    return pl.ds(pl.multiple_of(index * height, height), height)


def place_faces(swaps, order, product, rest, messages):
    height = rest.shape[0] // FACES
    for j in range(FACES):
        face = rows_of(order[0, j], height)
        rest[face, :] = product[j * height : (j + 1) * height, :]
    for (dim, odd), message in zip(swaps, messages):
        message[:height, :] = rest[rows_of(swap_face(dim, odd), height), :]


def reorder(order, read, local_iter):
    height = local_iter.shape[0] // FACES
    for j in range(FACES):
        local_iter[j * height : (j + 1) * height, :] = read(rows_of(order[0, j], height))


def first_kernel(swaps, order_hbm, *refs):
    hbm, held, refs = refs[:8], refs[8:15], refs[15:]
    (rest, *messages), scratch = refs[: 1 + len(swaps)], refs[1 + len(swaps) :]
    matrix, loads, modes, _, root_map = held[:5]
    order, start, local_iter, product, mapped, sems = scratch
    matrix_hbm, start_hbm = hbm[:2]
    parts = 4
    part = matrix.shape[0] // parts

    pairs = [(order_hbm, order), (start_hbm, start)]
    for k in range(parts):
        rows = slice(k * part, (k + 1) * part)
        pairs.append((matrix_hbm.at[rows, :], matrix.at[rows, :]))
    pairs += list(zip(hbm[2:], held[1:]))
    copies = [pltpu.make_async_copy(*pair, sems.at[k]) for k, pair in enumerate(pairs)]
    for copy in copies:
        copy.start()
    copies[0].wait()
    copies[1].wait()
    reorder(order, lambda rows: start[rows, :], local_iter)
    for k in range(parts):
        copies[2 + k].wait()
        rows = slice(k * part, (k + 1) * part)
        product[rows, :] = jnp.dot(matrix[rows, :], local_iter[...], preferred_element_type=F32)
    for copy in copies[2 + parts :]:
        copy.wait()
    place_faces(swaps, order, product, rest, messages)
    rest[...] = loads[...].astype(F32) - rest[...]
    mapped[...] = dot3(root_map[...], modes[...])
    height, lanes = rest.shape[0] // FACES, rest.shape[1]
    for (dim, odd), message in zip(swaps, messages):
        link = mapped[:, rows_of(swap_face(dim, odd), height)]
        extra = message.shape[0] - height
        for k in range(lanes // height):
            message[height:, k * height : (k + 1) * height] = link[k * extra : (k + 1) * extra, :]


def constants_kernel(modes, weights, modes_t, modes_s, scale):
    high, low = split(modes[...])
    count = high.shape[0]
    height = scale.shape[1]
    modes_s[:count, :] = high
    modes_s[count:, :] = low
    modes_t[...] = jnp.concatenate([high.T, low.T, high.T], axis=1)
    for j in range(FACES):
        block = slice(j * height, (j + 1) * height)
        scale[block, :] = jnp.broadcast_to(weights[:, block], (height, height)).T


def coarse_of(modes_s, residual, coarse):
    count = modes_s.shape[0] // 2
    high, low = split(residual[...])
    both = jnp.dot(modes_s[...], high, preferred_element_type=F32)
    fine = jnp.dot(modes_s[:count, :], low, preferred_element_type=F32)
    coarse[:count, :] = both[:count, :] + (both[count:, :] + fine)


def residual_kernel(swaps, sizes, rest, modes_s, root_map, *more):
    halos, (residual, coarse, root, links) = more[: len(swaps)], more[len(swaps) :]
    residual[...] = rest[...]
    add_halos(swaps, sizes, residual, halos)
    coarse_of(modes_s, residual, coarse)
    root[...] = dot3(root_map[...], coarse[...])
    height, lanes = rest.shape[0] // FACES, rest.shape[1]
    count = root.shape[0]
    for at, ((dim, odd), halo) in enumerate(zip(swaps, halos)):
        known = has_neighbour(dim, swap_face(dim, odd), sizes)
        extra = halo.shape[0] - height
        for k in range(lanes // height):
            link = halo[height:, k * height : (k + 1) * height]
            rows = slice(at * count + k * extra, at * count + (k + 1) * extra)
            links[rows, :] = jnp.where(known, link, 0.0)


def links_kernel(swaps, modes, root_map, links, loads, ahead_s, ahead_loads, ahead):
    count, height = root_map.shape[0], links.shape[1]
    ahead[...] = jnp.zeros_like(ahead)
    own = dot3(root_map[...], modes[...])
    ahead[count : 2 * count, :] = own
    for at, (dim, odd) in enumerate(swaps):
        face = swap_face(dim, odd)
        link = links[at * count : (at + 1) * count, :]
        if dim == 0:
            ahead[rows_of(2 * face, count), rows_of(face, height)] = link
        else:
            ahead[count : 2 * count, rows_of(face, height)] += link
    high, low = split(ahead[...])
    ahead_s[: 3 * count, :] = high
    ahead_s[3 * count :, :] = low
    high, low = split(own)
    ahead_loads[...] = jnp.zeros_like(ahead_loads)
    dot = functools.partial(jnp.dot, preferred_element_type=F32)
    ahead_loads[count : 2 * count, :] = dot(high, loads[...]) + dot(low, loads[...])


def merged_kernel(
    swaps, sizes, ride, rest, modes_s, root_inverse, ahead, *more
):
    halos, more = more[: len(swaps)], more[len(swaps) :]
    received, (residual, message, stack) = more[:-3], more[-3:]
    residual[...] = rest[...]
    add_halos(swaps, sizes, residual, halos)
    coarse_of(modes_s, residual, message)
    modes, height = modes_s.shape[0] // 2, rest.shape[0] // FACES
    count = message.shape[0] - modes
    me = lax.axis_index("gx")
    stack[...] = jnp.zeros_like(stack)
    pieces = [(me, ahead)]
    for (dim, odd), halo in zip(swaps, halos):
        if ride and (dim, odd) == (0, 0):
            pieces.append((me ^ 1, halo.at[height:, :]))
    for offset, piece in received_offsets(ride, sizes[0], received):
        pieces.append((source(me, offset, sizes[0]), piece))
    for index, piece in pieces:
        rows = pl.ds(pl.multiple_of(index * count, count), 3 * count)
        stack[rows, :] += piece[...]
    message[modes:, :] = dot3(root_inverse[...], stack[count:-count, :])


def received_offsets(ride, count, pieces):
    return list(zip(range(count - 1, ride, -1), pieces))


def root_kernel(count, coarse, root_inverse, root, *more):
    received, (message, stack) = more[: count - 1], more[count - 1 :]
    modes, height = coarse.shape[0], root.shape[0]
    me = lax.axis_index("gx")
    stack[rows_of(me, height), :] = root[...]
    for offset, piece in enumerate(received, 1):
        stack[rows_of(source(me, offset, count), height), :] = piece[...]
    message[:modes, :] = coarse[...]
    message[modes:, :] = dot3(root_inverse[...], stack[...])


def pair_kernel(modes, first, *more):
    received, out = more[:-1], more[-1]
    height = first.shape[0]
    total = first[modes:, :]
    out[:modes, :] = first[:modes, :]
    for k, piece in enumerate(received, 1):
        out[k * modes : (k + 1) * modes, :] = piece[:modes, :]
        total = total + piece[modes:, :]
    out[(len(received) + 1) * modes :, :] = total


def amplitude_of(members, sizes, region_rows, root_map, own, other, stack):
    modes = root_map.shape[1]
    y, z = lax.axis_index("gy"), lax.axis_index("gz")
    half = sizes[0] // 2
    count = len(members)
    for k, (dy, dz) in enumerate(members):
        at_y = 2 * source(y // 2, dy, half) + y % 2
        at_z = source(z, dz, sizes[1])
        piece = slice(k * modes, (k + 1) * modes)
        stack[rows_of(at_y * sizes[1] + at_z, modes), :] = own[piece, :]
        stack[rows_of((at_y ^ 1) * sizes[1] + at_z, modes), :] = other[piece, :]
    root_part = own[count * modes :, :] + other[count * modes :, :]
    return dot3(region_rows[...], stack[...]) + dot3(root_map[...], root_part, COLS)


def correction_of(modes_t, amplitude):
    high, low = split(amplitude)
    tall = jnp.concatenate([high, high, low], axis=0)
    return jnp.dot(modes_t[...], tall, preferred_element_type=F32)


def scaled(scale, residual, block):
    lanes = residual.shape[1] // scale.shape[1]
    return jnp.concatenate([scale[block, :]] * lanes, axis=1) * residual[block, :]


def middle_kernel(
    swaps, members, sizes, order_hbm, matrix, solution, loads, residual, scale, modes_t, root_map, region_rows,
    own, other, ahead_s, ahead_loads, next_solution, rest, ahead, *more
):
    messages, (stack, local_iter, product, order, sem) = more[: len(swaps)], more[len(swaps) :]
    copy = pltpu.make_async_copy(order_hbm, order, sem)
    copy.start()
    amplitude = amplitude_of(members, sizes, region_rows, root_map, own, other, stack)
    product[...] = correction_of(modes_t, amplitude)
    every = slice(0, residual.shape[0])
    next_solution[...] = solution[...].astype(F32) + scaled(scale, residual, every) + product[...]
    copy.wait()
    reorder(order, lambda rows: next_solution[rows, :].astype(BF16), local_iter)
    product[...] = jnp.dot(matrix[...], local_iter[...], preferred_element_type=F32)
    place_faces(swaps, order, product, rest, messages)
    count = ahead.shape[0]
    high, low = split(rest[...])
    both = jnp.dot(ahead_s[...], high, preferred_element_type=F32)
    fine = jnp.dot(ahead_s[:count, :], low, preferred_element_type=F32)
    ahead[...] = ahead_loads[...] - (both[:count, :] + (both[count:, :] + fine))
    height = rest.shape[0] // FACES
    for message in messages:
        if message.shape[0] > height:
            message[height:, :] = ahead[...]
    rest[...] = loads[...].astype(F32) - rest[...]


def last_kernel(
    members, sizes, solution, residual, scale, modes_t, root_map, region_rows, own, other, out, stack, result, sems
):
    amplitude = amplitude_of(members, sizes, region_rows, root_map, own, other, stack)
    part = result.shape[0] // 4
    copies = []
    for k in range(4):
        block = slice(k * part, (k + 1) * part)
        base = solution[block, :].astype(F32) + scaled(scale, residual, block)
        result[block, :] = base + correction_of(modes_t.at[block, :], amplitude)
        copies.append(pltpu.make_async_copy(result.at[block, :], out.at[block, :], sems.at[k]))
        copies[-1].start()
    for copy in copies:
        copy.wait()


def per_device(
    loads,
    start,
    interface_op,
    block_order,
    interface_weights,
    coarse_modes,
    region_weights,
    region_inverse,
    root_inverse,
):
    sizes = tuple(lax.axis_size(axis) for axis in AXES)
    iface = interface_op.shape[-1]
    cases = loads.shape[-1]
    height = iface // FACES
    matrix = interface_op.reshape(iface, iface)
    order = block_order.reshape(1, FACES)
    weights = interface_weights.reshape(1, iface)
    modes = coarse_modes.reshape(coarse_modes.shape[-2], iface)
    mode_count = modes.shape[0]
    root_map = region_weights.reshape(mode_count, region_weights.shape[-1]).T
    root_modes = root_map.shape[0]
    region_rows = region_inverse.reshape(mode_count, region_inverse.shape[-1])
    target = loads.reshape(iface, cases)
    solution = start.reshape(iface, cases)

    swaps = swap_list(sizes)
    half = sizes[1] // 2
    members = list(itertools.product(range(half), range(sizes[2])))

    ride = int(sizes[0] & (sizes[0] - 1) == 0)
    full = (pltpu.VMEM, (iface, cases), F32)
    work = [pltpu.VMEM((iface, cases), BF16), pltpu.VMEM((iface, cases), F32)]
    stack = [pltpu.VMEM((region_rows.shape[1], cases), F32)]
    places = [pltpu.SMEM((1, FACES), jnp.int32)]

    def held(rows):
        return (pltpu.VMEM, (rows, cases), F32)

    def along(value, offset):
        pairs = []
        for place in itertools.product(*map(range, sizes)):
            there = (partner(place[0], offset, sizes[0]),) + place[1:]
            pairs.append((flat(sizes, place), flat(sizes, there)))
        return lax.ppermute(value, AXES, pairs)

    def exchange(messages):
        return [
            lax.ppermute(message, AXES, swap_pairs(sizes, dim, odd))
            for (dim, odd), message in zip(swaps, messages)
        ]

    for step in range(ITERS):
        if step == 0:
            inputs = [order, matrix, solution, target, modes, weights, root_map, region_rows, root_inverse]
            kept = [(pltpu.VMEM, item.shape, item.dtype) for item in [matrix] + inputs[3:]]
            outs = call(
                functools.partial(first_kernel, swaps),
                kept + [full] + [held(height + root_modes * height // cases)] * len(swaps),
                inputs,
                "first_product",
                places
                + [pltpu.VMEM((iface, cases), BF16)]
                + work
                + [pltpu.VMEM((root_modes, iface), F32), pltpu.SemaphoreType.DMA((12,))],
                len(inputs),
            )
            matrix, target, modes, weights, root_map, region_rows, root_inverse, rest, *messages = outs
            modes_t, modes_s, scale = call(
                constants_kernel,
                [
                    (pltpu.VMEM, (iface, 3 * mode_count), BF16),
                    (pltpu.VMEM, (2 * mode_count, iface), BF16),
                    (pltpu.VMEM, (iface, height), F32),
                ],
                [modes, weights],
                "constants",
            )
            halos = exchange(messages)
            residual, coarse, root, links = call(
                functools.partial(residual_kernel, swaps, sizes),
                [full, held(mode_count), held(root_modes), (pltpu.VMEM, (len(swaps) * root_modes, height), F32)],
                [rest, modes_s, root_map] + halos,
                "residual_coarse",
            )
            received = [along(root, offset) for offset in range(1, sizes[0])]
            (message,) = call(
                functools.partial(root_kernel, sizes[0]),
                [held(mode_count + root_modes)],
                [coarse, root_inverse, root] + received,
                "root_part",
                [pltpu.VMEM((root_inverse.shape[1], cases), F32)],
            )
            ahead_s, ahead_loads = call(
                functools.partial(links_kernel, swaps),
                [(pltpu.VMEM, (6 * root_modes, iface), BF16), held(3 * root_modes)],
                [modes, root_map, links, target],
                "links",
                [pltpu.VMEM((3 * root_modes, iface), F32)],
            )
        else:
            extra = [3 * root_modes if ride and swap == (0, 0) else 0 for swap in swaps]
            solution, rest, ahead, *messages = call(
                functools.partial(middle_kernel, swaps, members, sizes[1:]),
                [full, full, held(3 * root_modes)] + [held(height + more) for more in extra],
                [order, matrix, solution, target, residual, scale, modes_t, root_map, region_rows, own, other]
                + [ahead_s, ahead_loads],
                "update_product",
                stack + work + places + [pltpu.SemaphoreType.DMA],
                1,
            )
            received = [along(ahead, offset) for offset in range(sizes[0] - 1, ride, -1)]
            halos = exchange(messages)
            residual, message = call(
                functools.partial(merged_kernel, swaps, sizes, ride),
                [full, held(mode_count + root_modes)],
                [rest, modes_s, root_inverse, ahead] + halos + received,
                "residual_root",
                [pltpu.VMEM((root_inverse.shape[1] + 2 * root_modes, cases), F32)],
            )
        pieces = []
        for dy, dz in members[1:]:
            moves = [
                (y * sizes[2] + z, (2 * partner(y // 2, dy, half) + y % 2) * sizes[2] + partner(z, dz, sizes[2]))
                for y in range(sizes[1])
                for z in range(sizes[2])
            ]
            pieces.append(lax.ppermute(message, ("gy", "gz"), moves))
        (own,) = call(
            functools.partial(pair_kernel, mode_count),
            [held(len(members) * mode_count + root_modes)],
            [message] + pieces,
            "pair_message",
        )
        other = lax.ppermute(own, AXES, swap_pairs(sizes, 1, 0))
    (solution,) = call(
        functools.partial(last_kernel, members, sizes[1:]),
        [(jax.ShapeDtypeStruct, (iface, cases), F32)],
        [solution, residual, scale, modes_t, root_map, region_rows, own, other],
        "update_last",
        stack + [pltpu.VMEM((iface, cases), F32), pltpu.SemaphoreType.DMA((4,))],
    )
    return solution.reshape(1, 1, 1, iface, cases)


def solution(mesh):
    placed = (
        P("gx", "gy", "gz", None, None),
        P("gx", "gy", "gz", None, None),
        P("gx", "gy", "gz", None, None),
        P("gx", "gy", "gz", None),
        P("gx", "gy", "gz", None),
        P("gx", "gy", "gz", None, None),
        P("gx", "gy", "gz", None, None),
        P("gx", ("gy", "gz"), None),
        P("gx", None),
    )
    return jax.shard_map(
        per_device,
        mesh=mesh,
        in_specs=placed,
        out_specs=P("gx", "gy", "gz", None, None),
        check_vma=False,
    )
```

```python
import functools
import itertools

import jax
import jax.numpy as jnp
from jax import lax
from jax.experimental import pallas as pl
from jax.experimental.pallas import tpu as pltpu
from jax.sharding import PartitionSpec as P

ITERS = 2
FACES = 8
AXES = ("gx", "gy", "gz")
F32 = jnp.float32
BF16 = jnp.bfloat16
ROWS = (((1,), (0,)), ((), ()))
COLS = (((0,), (0,)), ((), ()))


def neighbour(index, count, odd):
    other = index + 1 if index % 2 == odd else index - 1
    return other if 0 <= other < count else None


def swap_list(sizes):
    swaps = [(dim, odd) for odd in (1, 0) for dim in (0, 1, 2) if sizes[dim] > 1 + odd]
    return sorted(swaps, key=lambda swap: swap == (1, 0))


def flat(sizes, place):
    return (place[0] * sizes[1] + place[1]) * sizes[2] + place[2]


def swap_pairs(sizes, dim, odd):
    pairs = []
    for place in itertools.product(*map(range, sizes)):
        there = list(place)
        other = neighbour(place[dim], sizes[dim], odd)
        if other is not None:
            there[dim] = other
        elif odd and sizes[dim] % 2 == 0:
            if dim == 1:
                there[1] = sizes[1] - 1 - place[1]
            elif sizes[1] % 2 == 0:
                there[1] = place[1] ^ 1
        if tuple(there) != place:
            pairs.append((flat(sizes, place), flat(sizes, there)))
    return pairs


def swap_face(dim, odd):
    high = (lax.axis_index(AXES[dim]) + odd + 1) % 2
    return 2 * dim + high


def has_neighbour(dim, face, sizes):
    other = lax.axis_index(AXES[dim]) + 2 * (face - 2 * dim) - 1
    return jnp.logical_and(other >= 0, other < sizes[dim])


def partner(index, offset, count):
    if count & (count - 1):
        return (index + offset) % count
    return index ^ offset


def source(index, offset, count):
    if count & (count - 1):
        return lax.rem(index + count - offset, count)
    return index ^ offset


def split(value):
    high = value.astype(BF16)
    return high, (value - high.astype(F32)).astype(BF16)


def dot3(left, right, dims=ROWS):
    left_high, left_low = split(left)
    right_high, right_low = split(right)
    dot = functools.partial(lax.dot_general, dimension_numbers=dims, preferred_element_type=F32)
    return dot(left_high, right_high) + (dot(left_low, right_high) + dot(left_high, right_low))


def call(body, outs, ins, name, scratch=(), fixed=0):
    spaces = [pltpu.HBM] * fixed + [pltpu.VMEM] * (len(ins) - fixed)
    return pl.pallas_call(
        body,
        out_shape=[item(shape, dtype) for item, shape, dtype in outs],
        in_specs=[pl.BlockSpec(memory_space=space) for space in spaces],
        out_specs=[
            pl.BlockSpec(memory_space=pltpu.HBM if item is jax.ShapeDtypeStruct else pltpu.VMEM)
            for item, _, _ in outs
        ],
        scratch_shapes=list(scratch),
        compiler_params=pltpu.CompilerParams(vmem_limit_bytes=8 * 1024 * 1024),
        name=name,
    )(*[pltpu.with_memory_space_constraint(item, space) for item, space in zip(ins, spaces)])


def rows_of(index, height):
    return pl.ds(pl.multiple_of(index * height, height), height)


def send_faces(swaps, placed, messages):
    height = placed.shape[0] // FACES
    for (dim, odd), message in zip(swaps, messages):
        message[:height, :] = placed[rows_of(swap_face(dim, odd), height), :]


def first_kernel(swaps, order_hbm, start_hbm, matrix_hbm, modes_hbm, root_hbm, matrix, modes, root_map, placed, *more):
    messages, (order, start, local_iter, mapped, sems) = more[: len(swaps)], more[len(swaps) :]
    pairs = [(order_hbm, order), (start_hbm, start), (matrix_hbm, matrix), (modes_hbm, modes), (root_hbm, root_map)]
    copies = [pltpu.make_async_copy(*pair, sems.at[k]) for k, pair in enumerate(pairs)]
    for copy in copies:
        copy.start()
    height, lanes = placed.shape[0] // FACES, placed.shape[1]
    copies[0].wait()
    copies[1].wait()
    for j in range(FACES):
        local_iter[j * height : (j + 1) * height, :] = start[rows_of(order[0, j], height), :]
    copies[3].wait()
    copies[4].wait()
    mapped[...] = dot3(root_map[...], modes[...])
    for (dim, odd), message in zip(swaps, messages):
        link = mapped[:, rows_of(swap_face(dim, odd), height)]
        extra = message.shape[0] - height
        for k in range(lanes // height):
            message[height:, k * height : (k + 1) * height] = link[k * extra : (k + 1) * extra, :]
    copies[2].wait()
    product = jnp.dot(matrix[...], local_iter[...], preferred_element_type=F32)
    for j in range(FACES):
        placed[rows_of(order[0, j], height), :] = product[j * height : (j + 1) * height, :]
    send_faces(swaps, placed, messages)


def constants_kernel(
    swaps, sizes, order_hbm, matrix, modes, weights, loads, placed,
    modes_t, scale, modes_f, matrix_f, modes_a, modes_b, ready, wide, order, sem
):
    copy = pltpu.make_async_copy(order_hbm, order, sem)
    copy.start()
    count, height = modes.shape[0], scale.shape[1]
    high, low = split(modes[...])
    modes_t[...] = jnp.concatenate([high.T, low.T, high.T], axis=1)
    for j in range(FACES):
        block = slice(j * height, (j + 1) * height)
        scale[block, :] = jnp.broadcast_to(weights[:, block], (height, height)).T
    for at, (dim, odd) in enumerate(swaps):
        face = swap_face(dim, odd)
        columns = modes[:, rows_of(face, height)]
        columns = jnp.where(has_neighbour(dim, face, sizes), columns, 0.0)
        block = slice(at * height, (at + 1) * height)
        modes_f[:count, block], modes_f[count:, block] = split(columns)
    dot = functools.partial(jnp.dot, preferred_element_type=F32)
    modes_b[...] = dot(high, loads[...]) + dot(low, loads[...])
    ready[...] = modes_b[...] - dot3(modes[...], placed[...])
    copy.wait()
    for j in range(FACES):
        block = slice(j * height, (j + 1) * height)
        wide[:, rows_of(order[0, j], height)] = matrix[:, block]
    for j in range(FACES):
        block = slice(j * height, (j + 1) * height)
        matrix_f[rows_of(order[0, j], height), :] = wide[block, :]
    modes_a[:count, :], modes_a[count:, :] = split(dot(high, matrix_f[...]) + dot(low, matrix_f[...]))


def coarse_of(swaps, sizes, ready, modes_f, halos, stack):
    height, count = stack.shape[0] // len(swaps), ready.shape[0]
    for at, ((dim, odd), halo) in enumerate(zip(swaps, halos)):
        known = has_neighbour(dim, swap_face(dim, odd), sizes)
        stack[at * height : (at + 1) * height, :] = jnp.where(known, halo[:height, :], 0.0)
    high, low = split(stack[...])
    both = jnp.dot(modes_f[...], high, preferred_element_type=F32)
    fine = jnp.dot(modes_f[:count, :], low, preferred_element_type=F32)
    return ready[...] - (both[:count, :] + (both[count:, :] + fine))


def coarse_kernel(swaps, sizes, ready, modes_f, root_map, *more):
    halos, (coarse, root, stack) = more[: len(swaps)], more[len(swaps) :]
    coarse[...] = coarse_of(swaps, sizes, ready, modes_f, halos, stack)
    root[...] = dot3(root_map[...], coarse[...])


def base_kernel(swaps, sizes, solution, loads, placed, scale, *more):
    halos, base = more[: len(swaps)], more[-1]
    height, lanes = scale.shape[1], placed.shape[1]

    def wide(rows):
        return jnp.concatenate([scale[rows, :]] * (lanes // height), axis=1)

    for j in range(FACES):
        rows = slice(j * height, (j + 1) * height)
        rest = loads[rows, :].astype(F32) - placed[rows, :]
        base[rows, :] = solution[rows, :].astype(F32) + wide(rows) * rest
    for (dim, odd), halo in zip(swaps, halos):
        face = swap_face(dim, odd)
        rows = rows_of(face, height)

        @pl.when(has_neighbour(dim, face, sizes))
        def _():
            base[rows, :] -= wide(rows) * halo[:height, :]


def links_kernel(swaps, sizes, modes, root_map, loads, matrix_f, modes_a, *more):
    halos, (tail, ahead_loads, ahead) = more[: len(swaps)], more[len(swaps) :]
    count, height = root_map.shape[0], loads.shape[0] // FACES
    lanes = loads.shape[1]
    ahead[...] = jnp.zeros_like(ahead)
    own = dot3(root_map[...], modes[...])
    ahead[count : 2 * count, :] = own
    for (dim, odd), halo in zip(swaps, halos):
        face = swap_face(dim, odd)
        known = has_neighbour(dim, face, sizes)
        extra = halo.shape[0] - height
        pieces = [halo[height:, k * height : (k + 1) * height] for k in range(lanes // height)]
        link = jnp.where(known, jnp.concatenate(pieces, axis=0), 0.0)
        if dim == 0:
            ahead[rows_of(2 * face, count), rows_of(face, height)] = link
        else:
            ahead[count : 2 * count, rows_of(face, height)] += link
    dot = functools.partial(jnp.dot, preferred_element_type=F32)
    high, low = split(ahead[...])
    both = dot(jnp.concatenate([high, low], axis=0), matrix_f[...])
    done = modes_a.shape[0]
    tail[:done, :] = modes_a[...]
    high, low = split(both[: 3 * count, :] + both[3 * count :, :])
    tail[done : done + 3 * count, :] = high
    tail[done + 3 * count :, :] = low
    high, low = split(own)
    ahead_loads[...] = jnp.zeros_like(ahead_loads)
    ahead_loads[count : 2 * count, :] = dot(high, loads[...]) + dot(low, loads[...])


def merged_kernel(swaps, sizes, ride, ready, modes_f, root_inverse, ahead, *more):
    halos, more = more[: len(swaps)], more[len(swaps) :]
    received, (message, faces, stack) = more[:-3], more[-3:]
    modes, height = ready.shape[0], faces.shape[0] // len(swaps)
    count = message.shape[0] - modes
    message[:modes, :] = coarse_of(swaps, sizes, ready, modes_f, halos, faces)
    me = lax.axis_index("gx")
    stack[...] = jnp.zeros_like(stack)
    pieces = [(me, ahead)]
    for (dim, odd), halo in zip(swaps, halos):
        if ride and (dim, odd) == (0, 0):
            pieces.append((me ^ 1, halo.at[height:, :]))
    for offset, piece in zip(range(1 + ride, sizes[0]), received):
        pieces.append((source(me, offset, sizes[0]), piece))
    for index, piece in pieces:
        rows = pl.ds(pl.multiple_of(index * count, count), 3 * count)
        stack[rows, :] += piece[...]
    message[modes:, :] = dot3(root_inverse[...], stack[count:-count, :])


def root_kernel(count, coarse, root_inverse, root, *more):
    received, (message, stack) = more[: count - 1], more[count - 1 :]
    modes, height = coarse.shape[0], root.shape[0]
    me = lax.axis_index("gx")
    stack[rows_of(me, height), :] = root[...]
    for offset, piece in enumerate(received, 1):
        stack[rows_of(source(me, offset, count), height), :] = piece[...]
    message[:modes, :] = coarse[...]
    message[modes:, :] = dot3(root_inverse[...], stack[...])


def pair_kernel(modes, first, *more):
    received, out = more[:-1], more[-1]
    height = first.shape[0]
    total = first[modes:, :]
    out[:modes, :] = first[:modes, :]
    for k, piece in enumerate(received, 1):
        out[k * modes : (k + 1) * modes, :] = piece[:modes, :]
        total = total + piece[modes:, :]
    out[(len(received) + 1) * modes :, :] = total


def amplitude_of(members, sizes, region_rows, root_map, own, other, stack):
    modes = root_map.shape[1]
    y, z = lax.axis_index("gy"), lax.axis_index("gz")
    half = sizes[0] // 2
    count = len(members)
    for k, (dy, dz) in enumerate(members):
        at_y = 2 * source(y // 2, dy, half) + y % 2
        at_z = source(z, dz, sizes[1])
        piece = slice(k * modes, (k + 1) * modes)
        stack[rows_of(at_y * sizes[1] + at_z, modes), :] = own[piece, :]
        stack[rows_of((at_y ^ 1) * sizes[1] + at_z, modes), :] = other[piece, :]
    root_part = own[count * modes :, :] + other[count * modes :, :]
    return dot3(region_rows[...], stack[...]) + dot3(root_map[...], root_part, COLS)


def correction_factor(amplitude):
    high, low = split(amplitude)
    return jnp.concatenate([high, high, low], axis=0)


def middle_kernel(
    swaps, members, sizes, base, modes_t, root_map, region_rows, own, other, matrix_f, tail, modes_b, ahead_loads,
    next_solution, placed, ready, ahead, *more
):
    messages, (stack,) = more[: len(swaps)], more[len(swaps) :]
    height = placed.shape[0] // FACES
    amplitude = amplitude_of(members, sizes, region_rows, root_map, own, other, stack)
    tall = correction_factor(amplitude)
    next_solution[...] = base[...] + jnp.dot(modes_t[...], tall, preferred_element_type=F32)
    local_iter = next_solution[...].astype(BF16)
    placed[...] = jnp.dot(matrix_f[...], local_iter, preferred_element_type=F32)
    more = jnp.dot(tail[...], local_iter, preferred_element_type=F32)
    modes, count = ready.shape[0], ahead.shape[0]
    ready[...] = modes_b[...] - (more[:modes, :] + more[modes : 2 * modes, :])
    more = more[2 * modes :, :]
    ahead[...] = ahead_loads[...] - (more[:count, :] + more[count:, :])
    send_faces(swaps, placed, messages)
    for message in messages:
        if message.shape[0] > height:
            message[height:, :] = ahead[...]


def last_kernel(members, sizes, base, modes_t, root_map, region_rows, own, other, out, stack, result, sems):
    amplitude = amplitude_of(members, sizes, region_rows, root_map, own, other, stack)
    tall = correction_factor(amplitude)
    parts = sems.shape[0]
    part = result.shape[0] // parts
    copies = []
    for k in range(parts):
        rows = slice(k * part, (k + 1) * part)
        result[rows, :] = base[rows, :] + jnp.dot(modes_t[rows, :], tall, preferred_element_type=F32)
        copies.append(pltpu.make_async_copy(result.at[rows, :], out.at[rows, :], sems.at[k]))
        copies[-1].start()
    for copy in copies:
        copy.wait()


def per_device(
    loads,
    start,
    interface_op,
    block_order,
    interface_weights,
    coarse_modes,
    region_weights,
    region_inverse,
    root_inverse,
):
    sizes = tuple(lax.axis_size(axis) for axis in AXES)
    iface = interface_op.shape[-1]
    cases = loads.shape[-1]
    height = iface // FACES
    matrix = interface_op.reshape(iface, iface)
    order = block_order.reshape(1, FACES)
    weights = interface_weights.reshape(1, iface)
    modes = coarse_modes.reshape(coarse_modes.shape[-2], iface)
    mode_count = modes.shape[0]
    root_map = region_weights.reshape(mode_count, region_weights.shape[-1]).T
    root_modes = root_map.shape[0]
    region_rows = region_inverse.reshape(mode_count, region_inverse.shape[-1])
    target = loads.reshape(iface, cases)
    solution = start.reshape(iface, cases)

    swaps = swap_list(sizes)
    half = sizes[1] // 2
    members = list(itertools.product(range(half), range(sizes[2])))

    ride = int(sizes[0] & (sizes[0] - 1) == 0)
    full = (pltpu.VMEM, (iface, cases), F32)
    places = [pltpu.SMEM((1, FACES), jnp.int32)]
    stack = [pltpu.VMEM((region_rows.shape[1], cases), F32)]
    faces = [pltpu.VMEM((len(swaps) * height, cases), F32)]

    def wide(rows, dtype=BF16):
        return (pltpu.VMEM, (rows, iface), dtype)

    def held(rows):
        return (pltpu.VMEM, (rows, cases), F32)

    def along(value, offset):
        pairs = []
        for place in itertools.product(*map(range, sizes)):
            there = (partner(place[0], offset, sizes[0]),) + place[1:]
            pairs.append((flat(sizes, place), flat(sizes, there)))
        return lax.ppermute(value, AXES, pairs)

    def exchange(messages):
        return [
            lax.ppermute(message, AXES, swap_pairs(sizes, dim, odd))
            for (dim, odd), message in zip(swaps, messages)
        ]

    def base_of(solution, placed, halos):
        return call(
            functools.partial(base_kernel, swaps, sizes),
            [full],
            [solution, target, placed, scale] + halos,
            "base",
        )[0]

    for step in range(ITERS):
        if step == 0:
            inputs = [order, solution, matrix, modes, root_map]
            matrix, modes, root_map, placed, *messages = call(
                functools.partial(first_kernel, swaps),
                [(pltpu.VMEM, item.shape, item.dtype) for item in inputs[2:]]
                + [full]
                + [held(height + root_modes * height // cases)] * len(swaps),
                inputs,
                "first_product",
                places
                + [pltpu.VMEM((iface, cases), BF16)] * 2
                + [pltpu.VMEM((root_modes, iface), F32), pltpu.SemaphoreType.DMA((5,))],
                len(inputs),
            )
            modes_t, scale, modes_f, matrix_f, modes_a, modes_b, ready = call(
                functools.partial(constants_kernel, swaps, sizes),
                [
                    (pltpu.VMEM, (iface, 3 * mode_count), BF16),
                    (pltpu.VMEM, (iface, height), F32),
                    (pltpu.VMEM, (2 * mode_count, len(swaps) * height), BF16),
                    wide(iface),
                    wide(2 * mode_count),
                    held(mode_count),
                    held(mode_count),
                ],
                [order, matrix, modes, weights, target, placed],
                "constants",
                [pltpu.VMEM((iface, iface), BF16)] + places + [pltpu.SemaphoreType.DMA],
                1,
            )
            halos = exchange(messages)
            coarse, root = call(
                functools.partial(coarse_kernel, swaps, sizes),
                [held(mode_count), held(root_modes)],
                [ready, modes_f, root_map] + halos,
                "coarse",
                faces,
            )
            received = [along(root, offset) for offset in range(1, sizes[0])]
            base = base_of(solution, placed, halos)
            tail, ahead_loads = call(
                functools.partial(links_kernel, swaps, sizes),
                [wide(2 * mode_count + 6 * root_modes), held(3 * root_modes)],
                [modes, root_map, target, matrix_f, modes_a] + halos,
                "links",
                [pltpu.VMEM((3 * root_modes, iface), F32)],
            )
            (message,) = call(
                functools.partial(root_kernel, sizes[0]),
                [held(mode_count + root_modes)],
                [coarse, root_inverse, root] + received,
                "root_part",
                [pltpu.VMEM((root_inverse.shape[1], cases), F32)],
            )
        else:
            extra = [3 * root_modes if ride and swap == (0, 0) else 0 for swap in swaps]
            solution, placed, ready, ahead, *messages = call(
                functools.partial(middle_kernel, swaps, members, sizes[1:]),
                [full, full, held(mode_count), held(3 * root_modes)] + [held(height + more) for more in extra],
                [base, modes_t, root_map, region_rows, own, other, matrix_f, tail, modes_b, ahead_loads],
                "update_product",
                stack,
            )
            received = [along(ahead, offset) for offset in range(1 + ride, sizes[0])]
            halos = exchange(messages)
            (message,) = call(
                functools.partial(merged_kernel, swaps, sizes, ride),
                [held(mode_count + root_modes)],
                [ready, modes_f, root_inverse, ahead] + halos + received,
                "coarse_root",
                faces + [pltpu.VMEM((root_inverse.shape[1] + 2 * root_modes, cases), F32)],
            )
            base = base_of(solution, placed, halos)
        pieces = []
        for dy, dz in members[1:]:
            moves = [
                (y * sizes[2] + z, (2 * partner(y // 2, dy, half) + y % 2) * sizes[2] + partner(z, dz, sizes[2]))
                for y in range(sizes[1])
                for z in range(sizes[2])
            ]
            pieces.append(lax.ppermute(message, ("gy", "gz"), moves))
        (own,) = call(
            functools.partial(pair_kernel, mode_count),
            [held(len(members) * mode_count + root_modes)],
            [message] + pieces,
            "pair_message",
        )
        other = lax.ppermute(own, AXES, swap_pairs(sizes, 1, 0))
    (solution,) = call(
        functools.partial(last_kernel, members, sizes[1:]),
        [(jax.ShapeDtypeStruct, (iface, cases), F32)],
        [base, modes_t, root_map, region_rows, own, other],
        "update_last",
        stack + [pltpu.VMEM((iface, cases), F32), pltpu.SemaphoreType.DMA((FACES,))],
    )
    return solution.reshape(1, 1, 1, iface, cases)


def solution(mesh):
    placed = (
        P("gx", "gy", "gz", None, None),
        P("gx", "gy", "gz", None, None),
        P("gx", "gy", "gz", None, None),
        P("gx", "gy", "gz", None),
        P("gx", "gy", "gz", None),
        P("gx", "gy", "gz", None, None),
        P("gx", "gy", "gz", None, None),
        P("gx", ("gy", "gz"), None),
        P("gx", None),
    )
    return jax.shard_map(
        per_device,
        mesh=mesh,
        in_specs=placed,
        out_specs=P("gx", "gy", "gz", None, None),
        check_vma=False,
    )
```

```python
import functools
import itertools

import jax
import jax.numpy as jnp
from jax import lax
from jax.experimental import pallas as pl
from jax.experimental.pallas import tpu as pltpu
from jax.sharding import PartitionSpec as P

ITERS = 2
FACES = 8
AXES = ("gx", "gy", "gz")
F32 = jnp.float32
BF16 = jnp.bfloat16
ROWS = (((1,), (0,)), ((), ()))
COLS = (((0,), (0,)), ((), ()))


def neighbour(index, count, odd):
    other = index + 1 if index % 2 == odd else index - 1
    return other if 0 <= other < count else None


def swap_list(sizes):
    swaps = [(dim, odd) for odd in (1, 0) for dim in (0, 1, 2) if sizes[dim] > 1 + odd]
    return sorted(swaps, key=lambda swap: swap == (1, 0))


def flat(sizes, place):
    return (place[0] * sizes[1] + place[1]) * sizes[2] + place[2]


def swap_pairs(sizes, dim, odd):
    pairs = []
    for place in itertools.product(*map(range, sizes)):
        there = list(place)
        other = neighbour(place[dim], sizes[dim], odd)
        if other is not None:
            there[dim] = other
        elif odd and sizes[dim] % 2 == 0:
            if dim == 1:
                there[1] = sizes[1] - 1 - place[1]
            elif sizes[1] % 2 == 0:
                there[1] = place[1] ^ 1
        if tuple(there) != place:
            pairs.append((flat(sizes, place), flat(sizes, there)))
    return pairs


def swap_face(dim, odd):
    high = (lax.axis_index(AXES[dim]) + odd + 1) % 2
    return 2 * dim + high


def has_neighbour(dim, face, sizes):
    other = lax.axis_index(AXES[dim]) + 2 * (face - 2 * dim) - 1
    return jnp.logical_and(other >= 0, other < sizes[dim])


def partner(index, offset, count):
    if count & (count - 1):
        return (index + offset) % count
    return index ^ offset


def source(index, offset, count):
    if count & (count - 1):
        return lax.rem(index + count - offset, count)
    return index ^ offset


def split(value):
    high = value.astype(BF16)
    return high, (value - high.astype(F32)).astype(BF16)


def dot3(left, right, dims=ROWS):
    left_high, left_low = split(left)
    right_high, right_low = split(right)
    dot = functools.partial(lax.dot_general, dimension_numbers=dims, preferred_element_type=F32)
    return dot(left_high, right_high) + (dot(left_low, right_high) + dot(left_high, right_low))


def call(body, outs, ins, name, scratch=(), fixed=0):
    spaces = [pltpu.HBM] * fixed + [pltpu.VMEM] * (len(ins) - fixed)
    return pl.pallas_call(
        body,
        out_shape=[item(shape, dtype) for item, shape, dtype in outs],
        in_specs=[pl.BlockSpec(memory_space=space) for space in spaces],
        out_specs=[
            pl.BlockSpec(memory_space=pltpu.HBM if item is jax.ShapeDtypeStruct else pltpu.VMEM)
            for item, _, _ in outs
        ],
        scratch_shapes=list(scratch),
        compiler_params=pltpu.CompilerParams(vmem_limit_bytes=8 * 1024 * 1024),
        name=name,
    )(*[pltpu.with_memory_space_constraint(item, space) for item, space in zip(ins, spaces)])


def rows_of(index, height):
    return pl.ds(pl.multiple_of(index * height, height), height)


def send_faces(swaps, placed, messages):
    height = placed.shape[0] // FACES
    for (dim, odd), message in zip(swaps, messages):
        message[:height, :] = placed[rows_of(swap_face(dim, odd), height), :]


def first_kernel(swaps, order_hbm, start_hbm, matrix_hbm, modes_hbm, root_hbm, matrix, modes, root_map, placed, *more):
    messages, (order, start, local_iter, mapped, sems) = more[: len(swaps)], more[len(swaps) :]
    pairs = [(order_hbm, order), (start_hbm, start), (matrix_hbm, matrix), (modes_hbm, modes), (root_hbm, root_map)]
    copies = [pltpu.make_async_copy(*pair, sems.at[k]) for k, pair in enumerate(pairs)]
    for copy in copies:
        copy.start()
    height, lanes = placed.shape[0] // FACES, placed.shape[1]
    copies[0].wait()
    copies[1].wait()
    for j in range(FACES):
        local_iter[j * height : (j + 1) * height, :] = start[rows_of(order[0, j], height), :]
    copies[3].wait()
    copies[4].wait()
    mapped[...] = dot3(root_map[...], modes[...])
    for (dim, odd), message in zip(swaps, messages):
        link = mapped[:, rows_of(swap_face(dim, odd), height)]
        extra = message.shape[0] - height
        for k in range(lanes // height):
            message[height:, k * height : (k + 1) * height] = link[k * extra : (k + 1) * extra, :]
    copies[2].wait()
    product = jnp.dot(matrix[...], local_iter[...], preferred_element_type=F32)
    for j in range(FACES):
        placed[rows_of(order[0, j], height), :] = product[j * height : (j + 1) * height, :]
    send_faces(swaps, placed, messages)


def constants_kernel(
    swaps, sizes, order_hbm, matrix, modes, root_map, weights, loads, placed,
    modes_t, scale, modes_f, matrix_f, modes_a, modes_b, ready, wide, order, sem
):
    copy = pltpu.make_async_copy(order_hbm, order, sem)
    copy.start()
    count, height = modes.shape[0], scale.shape[1]
    high, low = split(modes[...])
    modes_t[...] = jnp.concatenate([high.T, low.T, high.T], axis=1)
    for j in range(FACES):
        block = slice(j * height, (j + 1) * height)
        scale[block, :] = jnp.broadcast_to(weights[:, block], (height, height)).T
    for at, (dim, odd) in enumerate(swaps):
        face = swap_face(dim, odd)
        columns = modes[:, rows_of(face, height)]
        columns = jnp.where(has_neighbour(dim, face, sizes), columns, 0.0)
        block = slice(at * height, (at + 1) * height)
        modes_f[:count, block], modes_f[count : 2 * count, block] = split(columns)
        rows = root_map.shape[0]
        parts = split(dot3(root_map[...], columns))
        modes_f[2 * count : 2 * count + rows, block], modes_f[2 * count + rows :, block] = parts
    dot = functools.partial(jnp.dot, preferred_element_type=F32)
    modes_b[...] = dot(high, loads[...]) + dot(low, loads[...])
    ready[:count, :] = modes_b[...] - dot3(modes[...], placed[...])
    ready[count:, :] = dot3(root_map[...], ready[:count, :])
    copy.wait()
    for j in range(FACES):
        block = slice(j * height, (j + 1) * height)
        wide[:, rows_of(order[0, j], height)] = matrix[:, block]
    for j in range(FACES):
        block = slice(j * height, (j + 1) * height)
        matrix_f[rows_of(order[0, j], height), :] = wide[block, :]
    modes_a[:count, :], modes_a[count:, :] = split(dot(high, matrix_f[...]) + dot(low, matrix_f[...]))


def stack_halos(swaps, sizes, halos, stack):
    height = stack.shape[0] // len(swaps)
    for at, ((dim, odd), halo) in enumerate(zip(swaps, halos)):
        known = has_neighbour(dim, swap_face(dim, odd), sizes)
        stack[at * height : (at + 1) * height, :] = jnp.where(known, halo[:height, :], 0.0)
    return split(stack[...])


def coarse_kernel(swaps, sizes, ready, modes_f, *more):
    halos, (coarse, root, stack) = more[: len(swaps)], more[len(swaps) :]
    modes, count = coarse.shape[0], root.shape[0]
    high, low = stack_halos(swaps, sizes, halos, stack)
    both = jnp.dot(modes_f[...], high, preferred_element_type=F32)
    fine = jnp.dot(modes_f[: 2 * modes + count, :], low, preferred_element_type=F32)
    coarse[...] = ready[:modes, :] - (both[:modes, :] + (both[modes : 2 * modes, :] + fine[:modes, :]))
    at = 2 * modes
    root[...] = ready[modes:, :] - (both[at : at + count, :] + (both[at + count :, :] + fine[at:, :]))


def base_kernel(swaps, sizes, solution, loads, placed, scale, *more):
    halos, base = more[: len(swaps)], more[-1]
    height, lanes = scale.shape[1], placed.shape[1]

    def wide(rows):
        return jnp.concatenate([scale[rows, :]] * (lanes // height), axis=1)

    for j in range(FACES):
        rows = slice(j * height, (j + 1) * height)
        rest = loads[rows, :].astype(F32) - placed[rows, :]
        base[rows, :] = solution[rows, :].astype(F32) + wide(rows) * rest
    for (dim, odd), halo in zip(swaps, halos):
        face = swap_face(dim, odd)
        rows = rows_of(face, height)

        @pl.when(has_neighbour(dim, face, sizes))
        def _():
            base[rows, :] -= wide(rows) * halo[:height, :]


def links_kernel(swaps, sizes, modes, root_map, loads, matrix_f, modes_a, *more):
    halos, (tail, ahead_loads, ahead) = more[: len(swaps)], more[len(swaps) :]
    count, height = root_map.shape[0], loads.shape[0] // FACES
    lanes = loads.shape[1]
    ahead[...] = jnp.zeros_like(ahead)
    own = dot3(root_map[...], modes[...])
    ahead[count : 2 * count, :] = own
    for (dim, odd), halo in zip(swaps, halos):
        face = swap_face(dim, odd)
        known = has_neighbour(dim, face, sizes)
        extra = halo.shape[0] - height
        pieces = [halo[height:, k * height : (k + 1) * height] for k in range(lanes // height)]
        link = jnp.where(known, jnp.concatenate(pieces, axis=0), 0.0)
        if dim == 0:
            ahead[rows_of(2 * face, count), rows_of(face, height)] = link
        else:
            ahead[count : 2 * count, rows_of(face, height)] += link
    dot = functools.partial(jnp.dot, preferred_element_type=F32)
    high, low = split(ahead[...])
    both = dot(jnp.concatenate([high, low], axis=0), matrix_f[...])
    done = modes_a.shape[0]
    tail[:done, :] = modes_a[...]
    high, low = split(both[: 3 * count, :] + both[3 * count :, :])
    tail[done : done + 3 * count, :] = high
    tail[done + 3 * count :, :] = low
    high, low = split(own)
    ahead_loads[...] = jnp.zeros_like(ahead_loads)
    ahead_loads[count : 2 * count, :] = dot(high, loads[...]) + dot(low, loads[...])


def merged_kernel(swaps, sizes, ride, ready, modes_f, root_inverse, ahead, *more):
    halos, more = more[: len(swaps)], more[len(swaps) :]
    received, (message, faces, stack) = more[:-3], more[-3:]
    modes, height = ready.shape[0], faces.shape[0] // len(swaps)
    count = message.shape[0] - modes
    high, low = stack_halos(swaps, sizes, halos, faces)
    both = jnp.dot(modes_f[: 2 * modes, :], high, preferred_element_type=F32)
    fine = jnp.dot(modes_f[:modes, :], low, preferred_element_type=F32)
    message[:modes, :] = ready[...] - (both[:modes, :] + (both[modes:, :] + fine))
    me = lax.axis_index("gx")
    stack[...] = jnp.zeros_like(stack)
    pieces = [(me, ahead)]
    for (dim, odd), halo in zip(swaps, halos):
        if ride and (dim, odd) == (0, 0):
            pieces.append((me ^ 1, halo.at[height:, :]))
    for offset, piece in zip(range(1 + ride, sizes[0]), received):
        pieces.append((source(me, offset, sizes[0]), piece))
    for index, piece in pieces:
        rows = pl.ds(pl.multiple_of(index * count, count), 3 * count)
        stack[rows, :] += piece[...]
    message[modes:, :] = dot3(root_inverse[...], stack[count:-count, :])


def root_kernel(count, coarse, root_inverse, root, *more):
    received, (message, stack) = more[: count - 1], more[count - 1 :]
    modes, height = coarse.shape[0], root.shape[0]
    me = lax.axis_index("gx")
    stack[rows_of(me, height), :] = root[...]
    for offset, piece in enumerate(received, 1):
        stack[rows_of(source(me, offset, count), height), :] = piece[...]
    message[:modes, :] = coarse[...]
    message[modes:, :] = dot3(root_inverse[...], stack[...])


def pack_kernel(region_rows, root_map, packed):
    modes, width = region_rows.shape[0], root_map.shape[1]
    packed[...] = jnp.zeros_like(packed)
    packed[:modes, :] = region_rows[...]
    packed[modes:, :width] = root_map[...]


def parts_kernel(members, sizes, packed, sibling, factors):
    modes, order = factors.shape[0] // 4, packed.shape[1]
    count = packed.shape[0] - modes
    y, z = lax.axis_index("gy"), lax.axis_index("gz")
    half = sizes[0] // 2
    depth = len(members) * modes
    row = lax.broadcasted_iota(jnp.int32, (order, depth), 0)
    column = lax.broadcasted_iota(jnp.int32, (order, depth), 1)
    wanted = jnp.full((order, depth), -1, jnp.int32)
    for k, (dy, dz) in enumerate(members):
        at_y = 2 * source(y // 2, dy, half) + y % 2
        first = (at_y * sizes[1] + source(z, dz, sizes[1])) * modes
        inside = jnp.logical_and(column >= k * modes, column < (k + 1) * modes)
        wanted = jnp.where(inside, first + column - k * modes, wanted)
    chosen = jnp.where(row == wanted, 1.0, 0.0).astype(BF16)
    for at, whole in enumerate((packed, sibling)):
        for level, piece in enumerate(split(whole[:modes, :])):
            rows = slice((2 * level + at) * modes, (2 * level + at + 1) * modes)
            factors[rows, :depth] = jnp.dot(piece, chosen, preferred_element_type=F32).astype(BF16)
        for level, piece in enumerate(split(whole[modes:, :modes].T)):
            rows = slice((2 * level + at) * modes, (2 * level + at + 1) * modes)
            factors[rows, depth:] = piece


def pair_kernel(modes, factors, first, *more):
    received, (own, out, tall) = more[:-3], more[-3:]
    total = first[modes:, :]
    tall[:modes, :] = first[:modes, :]
    for k, piece in enumerate(received, 1):
        tall[k * modes : (k + 1) * modes, :] = piece[:modes, :]
        total = total + piece[modes:, :]
    tall[(len(received) + 1) * modes :, :] = total
    high, low = split(tall[...])
    both = jnp.dot(factors[...], high, preferred_element_type=F32)
    fine = jnp.dot(factors[: 2 * modes, :], low, preferred_element_type=F32)
    total = both[: 2 * modes, :] + (both[2 * modes :, :] + fine)
    own[...] = total[:modes, :]
    out[...] = total[modes:, :]


def correction_factor(amplitude):
    high, low = split(amplitude)
    return jnp.concatenate([high, high, low], axis=0)


def middle_kernel(
    swaps, base, modes_t, own, other, matrix_f, tail, modes_b, ahead_loads,
    next_solution, placed, ready, ahead, *messages
):
    height = placed.shape[0] // FACES
    tall = correction_factor(own[...] + other[...])
    next_solution[...] = base[...] + jnp.dot(modes_t[...], tall, preferred_element_type=F32)
    local_iter = next_solution[...].astype(BF16)
    placed[...] = jnp.dot(matrix_f[...], local_iter, preferred_element_type=F32)
    more = jnp.dot(tail[...], local_iter, preferred_element_type=F32)
    modes, count = ready.shape[0], ahead.shape[0]
    ready[...] = modes_b[...] - (more[:modes, :] + more[modes : 2 * modes, :])
    more = more[2 * modes :, :]
    ahead[...] = ahead_loads[...] - (more[:count, :] + more[count:, :])
    send_faces(swaps, placed, messages)
    for message in messages:
        if message.shape[0] > height:
            message[height:, :] = ahead[...]


def last_kernel(base, modes_t, own, other, out, result, sems):
    tall = correction_factor(own[...] + other[...])
    parts = sems.shape[0]
    part = result.shape[0] // parts
    copies = []
    for k in range(parts):
        rows = slice(k * part, (k + 1) * part)
        result[rows, :] = base[rows, :] + jnp.dot(modes_t[rows, :], tall, preferred_element_type=F32)
        copies.append(pltpu.make_async_copy(result.at[rows, :], out.at[rows, :], sems.at[k]))
        copies[-1].start()
    for copy in copies:
        copy.wait()


def per_device(
    loads,
    start,
    interface_op,
    block_order,
    interface_weights,
    coarse_modes,
    region_weights,
    region_inverse,
    root_inverse,
):
    sizes = tuple(lax.axis_size(axis) for axis in AXES)
    iface = interface_op.shape[-1]
    cases = loads.shape[-1]
    height = iface // FACES
    matrix = interface_op.reshape(iface, iface)
    order = block_order.reshape(1, FACES)
    weights = interface_weights.reshape(1, iface)
    modes = coarse_modes.reshape(coarse_modes.shape[-2], iface)
    mode_count = modes.shape[0]
    root_map = region_weights.reshape(mode_count, region_weights.shape[-1]).T
    root_modes = root_map.shape[0]
    region_rows = region_inverse.reshape(mode_count, region_inverse.shape[-1])
    target = loads.reshape(iface, cases)
    solution = start.reshape(iface, cases)

    swaps = swap_list(sizes)
    half = sizes[1] // 2
    members = list(itertools.product(range(half), range(sizes[2])))

    ride = int(sizes[0] & (sizes[0] - 1) == 0)
    full = (pltpu.VMEM, (iface, cases), F32)
    places = [pltpu.SMEM((1, FACES), jnp.int32)]
    faces = [pltpu.VMEM((len(swaps) * height, cases), F32)]

    def wide(rows, dtype=BF16):
        return (pltpu.VMEM, (rows, iface), dtype)

    def held(rows):
        return (pltpu.VMEM, (rows, cases), F32)

    def along(value, offset):
        pairs = []
        for place in itertools.product(*map(range, sizes)):
            there = (partner(place[0], offset, sizes[0]),) + place[1:]
            pairs.append((flat(sizes, place), flat(sizes, there)))
        return lax.ppermute(value, AXES, pairs)

    def exchange(messages):
        return [
            lax.ppermute(message, AXES, swap_pairs(sizes, dim, odd))
            for (dim, odd), message in zip(swaps, messages)
        ]

    def base_of(solution, placed, halos):
        return call(
            functools.partial(base_kernel, swaps, sizes),
            [full],
            [solution, target, placed, scale] + halos,
            "base",
        )[0]

    for step in range(ITERS):
        if step == 0:
            inputs = [order, solution, matrix, modes, root_map]
            matrix, modes, root_map, placed, *messages = call(
                functools.partial(first_kernel, swaps),
                [(pltpu.VMEM, item.shape, item.dtype) for item in inputs[2:]]
                + [full]
                + [held(height + root_modes * height // cases)] * len(swaps),
                inputs,
                "first_product",
                places
                + [pltpu.VMEM((iface, cases), BF16)] * 2
                + [pltpu.VMEM((root_modes, iface), F32), pltpu.SemaphoreType.DMA((5,))],
                len(inputs),
            )
            modes_t, scale, modes_f, matrix_f, modes_a, modes_b, ready = call(
                functools.partial(constants_kernel, swaps, sizes),
                [
                    (pltpu.VMEM, (iface, 3 * mode_count), BF16),
                    (pltpu.VMEM, (iface, height), F32),
                    (pltpu.VMEM, (2 * mode_count + 2 * root_modes, len(swaps) * height), BF16),
                    wide(iface),
                    wide(2 * mode_count),
                    held(mode_count),
                    held(mode_count + root_modes),
                ],
                [order, matrix, modes, root_map, weights, target, placed],
                "constants",
                [pltpu.VMEM((iface, iface), BF16)] + places + [pltpu.SemaphoreType.DMA],
                1,
            )
            halos = exchange(messages)
            coarse, root = call(
                functools.partial(coarse_kernel, swaps, sizes),
                [held(mode_count), held(root_modes)],
                [ready, modes_f] + halos,
                "coarse",
                faces,
            )
            received = [along(root, offset) for offset in range(1, sizes[0])]
            packed = call(
                pack_kernel,
                [(pltpu.VMEM, (mode_count + root_modes, region_rows.shape[1]), F32)],
                [region_rows, root_map],
                "pack",
            )[0]
            sibling = lax.ppermute(packed, AXES, swap_pairs(sizes, 1, 0))
            (factors,) = call(
                functools.partial(parts_kernel, members, sizes[1:]),
                [(pltpu.VMEM, (4 * mode_count, len(members) * mode_count + root_modes), BF16)],
                [packed, sibling],
                "parts",
            )
            base = base_of(solution, placed, halos)
            tail, ahead_loads = call(
                functools.partial(links_kernel, swaps, sizes),
                [wide(2 * mode_count + 6 * root_modes), held(3 * root_modes)],
                [modes, root_map, target, matrix_f, modes_a] + halos,
                "links",
                [pltpu.VMEM((3 * root_modes, iface), F32)],
            )
            (message,) = call(
                functools.partial(root_kernel, sizes[0]),
                [held(mode_count + root_modes)],
                [coarse, root_inverse, root] + received,
                "root_part",
                [pltpu.VMEM((root_inverse.shape[1], cases), F32)],
            )
        else:
            extra = [3 * root_modes if ride and swap == (0, 0) else 0 for swap in swaps]
            solution, placed, ready, ahead, *messages = call(
                functools.partial(middle_kernel, swaps),
                [full, full, held(mode_count), held(3 * root_modes)] + [held(height + more) for more in extra],
                [base, modes_t, own, other, matrix_f, tail, modes_b, ahead_loads],
                "update_product",
            )
            received = [along(ahead, offset) for offset in range(1 + ride, sizes[0])]
            halos = exchange(messages)
            (message,) = call(
                functools.partial(merged_kernel, swaps, sizes, ride),
                [held(mode_count + root_modes)],
                [ready, modes_f, root_inverse, ahead] + halos + received,
                "coarse_root",
                faces + [pltpu.VMEM((root_inverse.shape[1] + 2 * root_modes, cases), F32)],
            )
            base = base_of(solution, placed, halos)
        pieces = []
        for dy, dz in members[1:]:
            moves = [
                (y * sizes[2] + z, (2 * partner(y // 2, dy, half) + y % 2) * sizes[2] + partner(z, dz, sizes[2]))
                for y in range(sizes[1])
                for z in range(sizes[2])
            ]
            pieces.append(lax.ppermute(message, ("gy", "gz"), moves))
        own, given = call(
            functools.partial(pair_kernel, mode_count),
            [held(mode_count), held(mode_count)],
            [factors, message] + pieces,
            "amplitude_parts",
            [pltpu.VMEM((len(members) * mode_count + root_modes, cases), F32)],
        )
        other = lax.ppermute(given, AXES, swap_pairs(sizes, 1, 0))
    (solution,) = call(
        last_kernel,
        [(jax.ShapeDtypeStruct, (iface, cases), F32)],
        [base, modes_t, own, other],
        "update_last",
        [pltpu.VMEM((iface, cases), F32), pltpu.SemaphoreType.DMA((4,))],
    )
    return solution.reshape(1, 1, 1, iface, cases)


def solution(mesh):
    placed = (
        P("gx", "gy", "gz", None, None),
        P("gx", "gy", "gz", None, None),
        P("gx", "gy", "gz", None, None),
        P("gx", "gy", "gz", None),
        P("gx", "gy", "gz", None),
        P("gx", "gy", "gz", None, None),
        P("gx", "gy", "gz", None, None),
        P("gx", ("gy", "gz"), None),
        P("gx", None),
    )
    return jax.shard_map(
        per_device,
        mesh=mesh,
        in_specs=placed,
        out_specs=P("gx", "gy", "gz", None, None),
        check_vma=False,
    )
```

```python
import functools
import itertools

import jax
import jax.numpy as jnp
from jax import lax
from jax.experimental import pallas as pl
from jax.experimental.pallas import tpu as pltpu
from jax.sharding import PartitionSpec as P

ITERS = 2
FACES = 8
AXES = ("gx", "gy", "gz")
F32 = jnp.float32
BF16 = jnp.bfloat16
ROWS = (((1,), (0,)), ((), ()))
COLS = (((0,), (0,)), ((), ()))


def neighbour(index, count, odd):
    other = index + 1 if index % 2 == odd else index - 1
    return other if 0 <= other < count else None


def swap_list(sizes):
    swaps = [(dim, odd) for odd in (1, 0) for dim in (1, 0, 2) if sizes[dim] > 1 + odd]
    return sorted(swaps, key=lambda swap: swap == (1, 0))


def flat(sizes, place):
    return (place[0] * sizes[1] + place[1]) * sizes[2] + place[2]


def swap_pairs(sizes, dim, odd):
    pairs = []
    for place in itertools.product(*map(range, sizes)):
        there = list(place)
        other = neighbour(place[dim], sizes[dim], odd)
        if other is not None:
            there[dim] = other
        elif odd and sizes[dim] % 2 == 0:
            if dim == 1:
                there[1] = sizes[1] - 1 - place[1]
            elif sizes[1] % 2 == 0:
                there[1] = place[1] ^ 1
        if tuple(there) != place:
            pairs.append((flat(sizes, place), flat(sizes, there)))
    return pairs


def swap_face(dim, odd):
    high = (lax.axis_index(AXES[dim]) + odd + 1) % 2
    return 2 * dim + high


def has_neighbour(dim, face, sizes):
    other = lax.axis_index(AXES[dim]) + 2 * (face - 2 * dim) - 1
    return jnp.logical_and(other >= 0, other < sizes[dim])


def partner(index, offset, count):
    if count & (count - 1):
        return (index + offset) % count
    return index ^ offset


def source(index, offset, count):
    if count & (count - 1):
        return lax.rem(index + count - offset, count)
    return index ^ offset


def nearest(count):
    return int(count & (count - 1) == 0)


def far_offsets(count, near):
    offsets = list(range(near, count))
    paired = list(zip(offsets[0::2], offsets[1::2]))
    return paired, offsets[2 * len(paired) :]


def core_offset(pair):
    return jnp.where(lax.axis_index("gy") % 2 == 0, pair[0], pair[1])


def split(value):
    high = value.astype(BF16)
    return high, (value - high.astype(F32)).astype(BF16)


def dot3(left, right, dims=ROWS):
    left_high, left_low = split(left)
    right_high, right_low = split(right)
    dot = functools.partial(lax.dot_general, dimension_numbers=dims, preferred_element_type=F32)
    return dot(left_high, right_high) + (dot(left_low, right_high) + dot(left_high, right_low))


def call(body, outs, ins, name, scratch=(), fixed=0):
    spaces = [pltpu.HBM] * fixed + [pltpu.VMEM] * (len(ins) - fixed)
    return pl.pallas_call(
        body,
        out_shape=[item(shape, dtype) for item, shape, dtype in outs],
        in_specs=[pl.BlockSpec(memory_space=space) for space in spaces],
        out_specs=[
            pl.BlockSpec(memory_space=pltpu.HBM if item is jax.ShapeDtypeStruct else pltpu.VMEM)
            for item, _, _ in outs
        ],
        scratch_shapes=list(scratch),
        compiler_params=pltpu.CompilerParams(vmem_limit_bytes=8 * 1024 * 1024),
        name=name,
    )(*[pltpu.with_memory_space_constraint(item, space) for item, space in zip(ins, spaces)])


def rows_of(index, height):
    return pl.ds(pl.multiple_of(index * height, height), height)


def send_faces(swaps, placed, messages):
    height = placed.shape[0] // FACES
    for (dim, odd), message in zip(swaps, messages):
        message[:height, :] = placed[rows_of(swap_face(dim, odd), height), :]


def first_kernel(swaps, order_hbm, start_hbm, *refs):
    hbm, held, (placed, *more) = refs[:4], refs[4:8], refs[8:]
    matrix, modes, root_map, region_rows = held
    messages, (order, start, local_iter, mapped, sems) = more[: len(swaps)], more[len(swaps) :]
    pairs = [(order_hbm, order), (start_hbm, start)] + list(zip(hbm, held))
    copies = [pltpu.make_async_copy(*pair, sems.at[k]) for k, pair in enumerate(pairs)]
    for copy in copies:
        copy.start()
    height, lanes = placed.shape[0] // FACES, placed.shape[1]
    copies[0].wait()
    copies[1].wait()
    for j in range(FACES):
        local_iter[j * height : (j + 1) * height, :] = start[rows_of(order[0, j], height), :]
    copies[3].wait()
    copies[4].wait()
    mapped[...] = dot3(root_map[...], modes[...])
    for (dim, odd), message in zip(swaps, messages):
        link = mapped[:, rows_of(swap_face(dim, odd), height)]
        extra = link.shape[0] * height // lanes
        end = height + extra
        for k in range(lanes // height):
            message[height:end, k * height : (k + 1) * height] = link[k * extra : (k + 1) * extra, :]
        if (dim, odd) == (1, 0):
            copies[5].wait()
            rows = region_rows.shape[0]
            message[end:, :] = jnp.zeros_like(message[end:, :])
            message[end : end + root_map.shape[0], :rows] = root_map[...]
            end += root_map.shape[0]
            for k in range(region_rows.shape[1] // lanes):
                message[end + k * rows : end + (k + 1) * rows, :] = region_rows[:, k * lanes : (k + 1) * lanes]
    copies[2].wait()
    product = jnp.dot(matrix[...], local_iter[...], preferred_element_type=F32)
    for j in range(FACES):
        placed[rows_of(order[0, j], height), :] = product[j * height : (j + 1) * height, :]
    send_faces(swaps, placed, messages)


def constants_kernel(
    swaps, sizes, order_hbm, matrix, modes, root_map, weights, loads, placed,
    modes_t, scale, modes_f, matrix_f, modes_a, modes_b, ready, wide, order, sem
):
    copy = pltpu.make_async_copy(order_hbm, order, sem)
    copy.start()
    count, height = modes.shape[0], scale.shape[1]
    high, low = split(modes[...])
    modes_t[...] = jnp.concatenate([high.T, low.T, high.T], axis=1)
    for j in range(FACES):
        block = slice(j * height, (j + 1) * height)
        scale[block, :] = jnp.broadcast_to(weights[:, block], (height, height)).T
    for at, (dim, odd) in enumerate(swaps):
        face = swap_face(dim, odd)
        columns = modes[:, rows_of(face, height)]
        columns = jnp.where(has_neighbour(dim, face, sizes), columns, 0.0)
        block = slice(at * height, (at + 1) * height)
        modes_f[:count, block], modes_f[count : 2 * count, block] = split(columns)
        rows = root_map.shape[0]
        parts = split(dot3(root_map[...], columns))
        modes_f[2 * count : 2 * count + rows, block], modes_f[2 * count + rows :, block] = parts
    dot = functools.partial(jnp.dot, preferred_element_type=F32)
    modes_b[...] = dot(high, loads[...]) + dot(low, loads[...])
    ready[:count, :] = modes_b[...] - dot3(modes[...], placed[...])
    ready[count:, :] = dot3(root_map[...], ready[:count, :])
    copy.wait()
    for j in range(FACES):
        block = slice(j * height, (j + 1) * height)
        wide[:, rows_of(order[0, j], height)] = matrix[:, block]
    for j in range(FACES):
        block = slice(j * height, (j + 1) * height)
        matrix_f[rows_of(order[0, j], height), :] = wide[block, :]
    modes_a[:count, :], modes_a[count:, :] = split(dot(high, matrix_f[...]) + dot(low, matrix_f[...]))


def stack_halos(swaps, sizes, halos, stack):
    height = stack.shape[0] // len(swaps)
    for at, ((dim, odd), halo) in enumerate(zip(swaps, halos)):
        known = has_neighbour(dim, swap_face(dim, odd), sizes)
        stack[at * height : (at + 1) * height, :] = jnp.where(known, halo[:height, :], 0.0)
    return split(stack[...])


def coarse_kernel(swaps, sizes, ready, modes_f, *more):
    halos, (coarse, root, stack) = more[: len(swaps)], more[len(swaps) :]
    modes, count = coarse.shape[0], root.shape[0]
    high, low = stack_halos(swaps, sizes, halos, stack)
    both = jnp.dot(modes_f[...], high, preferred_element_type=F32)
    fine = jnp.dot(modes_f[: 2 * modes + count, :], low, preferred_element_type=F32)
    coarse[...] = ready[:modes, :] - (both[:modes, :] + (both[modes : 2 * modes, :] + fine[:modes, :]))
    at = 2 * modes
    root[...] = ready[modes:, :] - (both[at : at + count, :] + (both[at + count :, :] + fine[at:, :]))


def base_kernel(swaps, sizes, solution, loads, placed, scale, *more):
    halos, base = more[: len(swaps)], more[-1]
    height, lanes = scale.shape[1], placed.shape[1]

    def wide(rows):
        return jnp.concatenate([scale[rows, :]] * (lanes // height), axis=1)

    for j in range(FACES):
        rows = slice(j * height, (j + 1) * height)
        rest = loads[rows, :].astype(F32) - placed[rows, :]
        base[rows, :] = solution[rows, :].astype(F32) + wide(rows) * rest
    for (dim, odd), halo in zip(swaps, halos):
        face = swap_face(dim, odd)
        rows = rows_of(face, height)

        @pl.when(has_neighbour(dim, face, sizes))
        def _():
            base[rows, :] -= wide(rows) * halo[:height, :]


def links_kernel(swaps, sizes, modes, root_map, loads, matrix_f, modes_a, *more):
    halos, (tail, ahead_loads, ahead) = more[: len(swaps)], more[len(swaps) :]
    count, height = root_map.shape[0], loads.shape[0] // FACES
    lanes = loads.shape[1]
    ahead[...] = jnp.zeros_like(ahead)
    own = dot3(root_map[...], modes[...])
    ahead[count : 2 * count, :] = own
    for (dim, odd), halo in zip(swaps, halos):
        face = swap_face(dim, odd)
        known = has_neighbour(dim, face, sizes)
        end = height + count * height // lanes
        pieces = [halo[height:end, k * height : (k + 1) * height] for k in range(lanes // height)]
        link = jnp.where(known, jnp.concatenate(pieces, axis=0), 0.0)
        if dim == 0:
            ahead[rows_of(2 * face, count), rows_of(face, height)] = link
        else:
            ahead[count : 2 * count, rows_of(face, height)] += link
    dot = functools.partial(jnp.dot, preferred_element_type=F32)
    high, low = split(ahead[...])
    both = dot(jnp.concatenate([high, low], axis=0), matrix_f[...])
    done = modes_a.shape[0]
    tail[:done, :] = modes_a[...]
    high, low = split(both[: 3 * count, :] + both[3 * count :, :])
    tail[done : done + 3 * count, :] = high
    tail[done + 3 * count :, :] = low
    high, low = split(own)
    ahead_loads[...] = jnp.zeros_like(ahead_loads)
    ahead_loads[count : 2 * count, :] = dot(high, loads[...]) + dot(low, loads[...])


def merged_kernel(swaps, sizes, ride, ready, modes_f, root_inverse, ahead, *more):
    halos, more = more[: len(swaps)], more[len(swaps) :]
    received, (message, faces, stack) = more[:-3], more[-3:]
    modes, height = ready.shape[0], faces.shape[0] // len(swaps)
    count = message.shape[0] - modes
    high, low = stack_halos(swaps, sizes, halos, faces)
    both = jnp.dot(modes_f[: 2 * modes, :], high, preferred_element_type=F32)
    fine = jnp.dot(modes_f[:modes, :], low, preferred_element_type=F32)
    message[:modes, :] = ready[...] - (both[:modes, :] + (both[modes:, :] + fine))
    me = lax.axis_index("gx")
    stack[...] = jnp.zeros_like(stack)
    pieces = [(me, ahead)]
    for (dim, odd), halo in zip(swaps, halos):
        if ride and (dim, odd) == (0, 0):
            pieces.append((me ^ 1, halo.at[height:, :]))
    paired, single = far_offsets(sizes[0], 1 + ride)
    for offset, piece in zip([core_offset(pair) for pair in paired] + single, received):
        pieces.append((source(me, offset, sizes[0]), piece))
    for index, piece in pieces:
        rows = pl.ds(pl.multiple_of(index * count, count), 3 * count)
        stack[rows, :] += piece[...]
    message[modes:, :] = dot3(root_inverse[...], stack[count:-count, :])


def sum_kernel(own, other, total):
    total[...] = own[...] + other[other.shape[0] - own.shape[0] :, :]


def root_kernel(count, coarse, root_inverse, root, *more):
    received, (message, stack) = more[:-2], more[-2:]
    modes, height = coarse.shape[0], root.shape[0]
    me = lax.axis_index("gx")
    paired, single = far_offsets(count, 1 + nearest(count))
    offsets = [core_offset(pair) for pair in paired] + list(range(1, 1 + nearest(count))) + single
    stack[...] = jnp.zeros_like(stack)
    stack[rows_of(me, height), :] = root[...]
    for offset, piece in zip(offsets, received):
        stack[rows_of(source(me, offset, count), height), :] = piece[...]
    message[:modes, :] = coarse[...]
    message[modes:, :] = dot3(root_inverse[...], stack[...])


def parts_kernel(members, sizes, region_rows, root_map, halo, factors):
    modes, order = region_rows.shape
    count, lanes = root_map.shape[0], halo.shape[1]
    blocks = order // lanes
    at = halo.shape[0] - blocks * modes
    other_rows = jnp.concatenate([halo[at + k * modes : at + (k + 1) * modes, :] for k in range(blocks)], axis=1)
    other_map = halo[at - count : at, :modes]
    y, z = lax.axis_index("gy"), lax.axis_index("gz")
    half = sizes[0] // 2
    depth = len(members) * modes
    row = lax.broadcasted_iota(jnp.int32, (order, depth), 0)
    column = lax.broadcasted_iota(jnp.int32, (order, depth), 1)
    wanted = jnp.full((order, depth), -1, jnp.int32)
    for k, (dy, dz) in enumerate(members):
        at_y = 2 * source(y // 2, dy, half) + y % 2
        first = (at_y * sizes[1] + source(z, dz, sizes[1])) * modes
        inside = jnp.logical_and(column >= k * modes, column < (k + 1) * modes)
        wanted = jnp.where(inside, first + column - k * modes, wanted)
    chosen = jnp.where(row == wanted, 1.0, 0.0).astype(BF16)
    for at, (whole, maps) in enumerate(((region_rows[...], root_map[...]), (other_rows, other_map))):
        for level, piece in enumerate(split(whole)):
            rows = slice((2 * level + at) * modes, (2 * level + at + 1) * modes)
            factors[rows, :depth] = jnp.dot(piece, chosen, preferred_element_type=F32).astype(BF16)
        for level, piece in enumerate(split(maps.T)):
            rows = slice((2 * level + at) * modes, (2 * level + at + 1) * modes)
            factors[rows, depth:] = piece


def pair_kernel(modes, factors, first, *more):
    received, (own, out, tall) = more[:-3], more[-3:]
    total = first[modes:, :]
    tall[:modes, :] = first[:modes, :]
    for k, piece in enumerate(received, 1):
        tall[k * modes : (k + 1) * modes, :] = piece[:modes, :]
        total = total + piece[modes:, :]
    tall[(len(received) + 1) * modes :, :] = total
    high, low = split(tall[...])
    both = jnp.dot(factors[...], high, preferred_element_type=F32)
    fine = jnp.dot(factors[: 2 * modes, :], low, preferred_element_type=F32)
    total = both[: 2 * modes, :] + (both[2 * modes :, :] + fine)
    own[...] = total[:modes, :]
    out[...] = total[modes:, :]


def correction_factor(amplitude):
    high, low = split(amplitude)
    return jnp.concatenate([high, high, low], axis=0)


def middle_kernel(
    swaps, base, modes_t, own, other, matrix_f, tail, modes_b, ahead_loads,
    next_solution, placed, ready, ahead, *messages
):
    height = placed.shape[0] // FACES
    tall = correction_factor(own[...] + other[...])
    next_solution[...] = base[...] + jnp.dot(modes_t[...], tall, preferred_element_type=F32)
    local_iter = next_solution[...].astype(BF16)
    placed[...] = jnp.dot(matrix_f[...], local_iter, preferred_element_type=F32)
    more = jnp.dot(tail[...], local_iter, preferred_element_type=F32)
    modes, count = ready.shape[0], ahead.shape[0]
    ready[...] = modes_b[...] - (more[:modes, :] + more[modes : 2 * modes, :])
    more = more[2 * modes :, :]
    ahead[...] = ahead_loads[...] - (more[:count, :] + more[count:, :])
    send_faces(swaps, placed, messages)
    for message in messages:
        if message.shape[0] > height:
            message[height:, :] = ahead[...]


def last_kernel(base, modes_t, own, other, out, result, sems):
    tall = correction_factor(own[...] + other[...])
    parts = sems.shape[0]
    part = result.shape[0] // parts
    copies = []
    for k in range(parts):
        rows = slice(k * part, (k + 1) * part)
        result[rows, :] = base[rows, :] + jnp.dot(modes_t[rows, :], tall, preferred_element_type=F32)
        copies.append(pltpu.make_async_copy(result.at[rows, :], out.at[rows, :], sems.at[k]))
        copies[-1].start()
    for copy in copies:
        copy.wait()


def per_device(
    loads,
    start,
    interface_op,
    block_order,
    interface_weights,
    coarse_modes,
    region_weights,
    region_inverse,
    root_inverse,
):
    sizes = tuple(lax.axis_size(axis) for axis in AXES)
    iface = interface_op.shape[-1]
    cases = loads.shape[-1]
    height = iface // FACES
    matrix = interface_op.reshape(iface, iface)
    order = block_order.reshape(1, FACES)
    weights = interface_weights.reshape(1, iface)
    modes = coarse_modes.reshape(coarse_modes.shape[-2], iface)
    mode_count = modes.shape[0]
    root_map = region_weights.reshape(mode_count, region_weights.shape[-1]).T
    root_modes = root_map.shape[0]
    region_rows = region_inverse.reshape(mode_count, region_inverse.shape[-1])
    target = loads.reshape(iface, cases)
    solution = start.reshape(iface, cases)

    swaps = swap_list(sizes)
    half = sizes[1] // 2
    members = list(itertools.product(range(half), range(sizes[2])))

    ride = nearest(sizes[0])
    paired, single = far_offsets(sizes[0], 1 + ride)
    core = swaps.index((1, 0))
    full = (pltpu.VMEM, (iface, cases), F32)
    places = [pltpu.SMEM((1, FACES), jnp.int32)]
    faces = [pltpu.VMEM((len(swaps) * height, cases), F32)]

    def wide(rows, dtype=BF16):
        return (pltpu.VMEM, (rows, iface), dtype)

    def held(rows):
        return (pltpu.VMEM, (rows, cases), F32)

    def along(value, offset):
        pairs = []
        for place in itertools.product(*map(range, sizes)):
            step = offset if isinstance(offset, int) else offset[place[1] % 2]
            there = (partner(place[0], step, sizes[0]),) + place[1:]
            pairs.append((flat(sizes, place), flat(sizes, there)))
        return lax.ppermute(value, AXES, pairs)

    def exchange(messages, order):
        moved = {}
        for dim, odd in order:
            message = messages[swaps.index((dim, odd))]
            moved[dim, odd] = lax.ppermute(message, AXES, swap_pairs(sizes, dim, odd))
        return [moved[swap] for swap in swaps]

    def core_sum(own, other):
        return call(sum_kernel, [held(own.shape[0])], [own, other], "core_sum")[0]

    def base_of(solution, placed, halos):
        return call(
            functools.partial(base_kernel, swaps, sizes),
            [full],
            [solution, target, placed, scale] + halos,
            "base",
        )[0]

    for step in range(ITERS):
        if step == 0:
            inputs = [order, solution, matrix, modes, root_map, region_rows]
            rows = [height + root_modes * height // cases] * len(swaps)
            rows[core] += root_modes + mode_count * (region_rows.shape[1] // cases)
            matrix, modes, root_map, region_rows, placed, *messages = call(
                functools.partial(first_kernel, swaps),
                [(pltpu.VMEM, item.shape, item.dtype) for item in inputs[2:]]
                + [full]
                + [held(count) for count in rows],
                inputs,
                "first_product",
                places
                + [pltpu.VMEM((iface, cases), BF16)] * 2
                + [pltpu.VMEM((root_modes, iface), F32), pltpu.SemaphoreType.DMA((6,))],
                len(inputs),
            )
            modes_t, scale, modes_f, matrix_f, modes_a, modes_b, ready = call(
                functools.partial(constants_kernel, swaps, sizes),
                [
                    (pltpu.VMEM, (iface, 3 * mode_count), BF16),
                    (pltpu.VMEM, (iface, height), F32),
                    (pltpu.VMEM, (2 * mode_count + 2 * root_modes, len(swaps) * height), BF16),
                    wide(iface),
                    wide(2 * mode_count),
                    held(mode_count),
                    held(mode_count + root_modes),
                ],
                [order, matrix, modes, root_map, weights, target, placed],
                "constants",
                [pltpu.VMEM((iface, iface), BF16)] + places + [pltpu.SemaphoreType.DMA],
                1,
            )
            halos = exchange(messages, swaps)
            coarse, root = call(
                functools.partial(coarse_kernel, swaps, sizes),
                [held(mode_count), held(root_modes)],
                [ready, modes_f] + halos,
                "coarse",
                faces,
            )
            both = core_sum(root, lax.ppermute(root, AXES, swap_pairs(sizes, 1, 0)))
            received = [along(root, offset) for offset in list(range(1, 1 + ride)) + single]
            received = [along(both, pair) for pair in paired] + received
            (factors,) = call(
                functools.partial(parts_kernel, members, sizes[1:]),
                [(pltpu.VMEM, (4 * mode_count, len(members) * mode_count + root_modes), BF16)],
                [region_rows, root_map, halos[core]],
                "parts",
            )
            base = base_of(solution, placed, halos)
            tail, ahead_loads = call(
                functools.partial(links_kernel, swaps, sizes),
                [wide(2 * mode_count + 6 * root_modes), held(3 * root_modes)],
                [modes, root_map, target, matrix_f, modes_a] + halos,
                "links",
                [pltpu.VMEM((3 * root_modes, iface), F32)],
            )
            (message,) = call(
                functools.partial(root_kernel, sizes[0]),
                [held(mode_count + root_modes)],
                [coarse, root_inverse, root] + received,
                "root_part",
                [pltpu.VMEM((root_inverse.shape[1], cases), F32)],
            )
        else:
            extra = [3 * root_modes * int(swap == (1, 0) or (ride and swap == (0, 0))) for swap in swaps]
            solution, placed, ready, ahead, *messages = call(
                functools.partial(middle_kernel, swaps),
                [full, full, held(mode_count), held(3 * root_modes)] + [held(height + more) for more in extra],
                [base, modes_t, own, other, matrix_f, tail, modes_b, ahead_loads],
                "update_product",
            )
            halos = exchange(messages, sorted(swaps, key=lambda swap: (swap != (1, 0), swap[0] == 1, swap)))
            both = core_sum(ahead, halos[core])
            received = [along(both, pair) for pair in paired] + [along(ahead, offset) for offset in single]
            (message,) = call(
                functools.partial(merged_kernel, swaps, sizes, ride),
                [held(mode_count + root_modes)],
                [ready, modes_f, root_inverse, ahead] + halos + received,
                "coarse_root",
                faces + [pltpu.VMEM((root_inverse.shape[1] + 2 * root_modes, cases), F32)],
            )
            base = base_of(solution, placed, halos)
        pieces = []
        for dy, dz in members[1:]:
            moves = [
                (y * sizes[2] + z, (2 * partner(y // 2, dy, half) + y % 2) * sizes[2] + partner(z, dz, sizes[2]))
                for y in range(sizes[1])
                for z in range(sizes[2])
            ]
            pieces.append(lax.ppermute(message, ("gy", "gz"), moves))
        own, given = call(
            functools.partial(pair_kernel, mode_count),
            [held(mode_count), held(mode_count)],
            [factors, message] + pieces,
            "amplitude_parts",
            [pltpu.VMEM((len(members) * mode_count + root_modes, cases), F32)],
        )
        other = lax.ppermute(given, AXES, swap_pairs(sizes, 1, 0))
    (solution,) = call(
        last_kernel,
        [(jax.ShapeDtypeStruct, (iface, cases), F32)],
        [base, modes_t, own, other],
        "update_last",
        [pltpu.VMEM((iface, cases), F32), pltpu.SemaphoreType.DMA((4,))],
    )
    return solution.reshape(1, 1, 1, iface, cases)


def solution(mesh):
    placed = (
        P("gx", "gy", "gz", None, None),
        P("gx", "gy", "gz", None, None),
        P("gx", "gy", "gz", None, None),
        P("gx", "gy", "gz", None),
        P("gx", "gy", "gz", None),
        P("gx", "gy", "gz", None, None),
        P("gx", "gy", "gz", None, None),
        P("gx", ("gy", "gz"), None),
        P("gx", None),
    )
    return jax.shard_map(
        per_device,
        mesh=mesh,
        in_specs=placed,
        out_specs=P("gx", "gy", "gz", None, None),
        check_vma=False,
    )
```

```python
import functools
import itertools

import jax
import jax.numpy as jnp
from jax import lax
from jax.experimental import pallas as pl
from jax.experimental.pallas import tpu as pltpu
from jax.sharding import PartitionSpec as P

ITERS = 2
FACES = 8
AXES = ("gx", "gy", "gz")
FIRST_ORDER = ((1, 1), (2, 1), (2, 0), (0, 0), (0, 1), (1, 0))
LATER_ORDER = ((1, 0), (0, 0), (0, 1), (2, 1), (2, 0), (1, 1))
F32 = jnp.float32
BF16 = jnp.bfloat16
ROWS = (((1,), (0,)), ((), ()))
COLS = (((0,), (0,)), ((), ()))


def neighbour(index, count, odd):
    other = index + 1 if index % 2 == odd else index - 1
    return other if 0 <= other < count else None


def swap_list(sizes, wanted):
    return [swap for swap in wanted if sizes[swap[0]] > 1 + swap[1]]


def flat(sizes, place):
    return (place[0] * sizes[1] + place[1]) * sizes[2] + place[2]


def swap_pairs(sizes, dim, odd):
    pairs = []
    for place in itertools.product(*map(range, sizes)):
        there = list(place)
        other = neighbour(place[dim], sizes[dim], odd)
        if other is not None:
            there[dim] = other
        elif odd and sizes[dim] % 2 == 0:
            if dim == 1:
                there[1] = sizes[1] - 1 - place[1]
            elif sizes[1] % 2 == 0:
                there[1] = place[1] ^ 1
        if tuple(there) != place:
            pairs.append((flat(sizes, place), flat(sizes, there)))
    return pairs


def swap_face(dim, odd):
    high = (lax.axis_index(AXES[dim]) + odd + 1) % 2
    return 2 * dim + high


def has_neighbour(dim, face, sizes):
    other = lax.axis_index(AXES[dim]) + 2 * (face - 2 * dim) - 1
    return jnp.logical_and(other >= 0, other < sizes[dim])


def partner(index, offset, count):
    if count & (count - 1):
        return (index + offset) % count
    return index ^ offset


def source(index, offset, count):
    if count & (count - 1):
        return lax.rem(index + count - offset, count)
    return index ^ offset


def nearest(count):
    return int(count & (count - 1) == 0)


def far_offsets(count, near):
    offsets = list(range(near, count))
    paired = list(zip(offsets[0::2], offsets[1::2]))
    return paired, offsets[2 * len(paired) :]


def core_offset(pair):
    return jnp.where(lax.axis_index("gy") % 2 == 0, pair[0], pair[1])


def split(value):
    high = value.astype(BF16)
    return high, (value - high.astype(F32)).astype(BF16)


def dot3(left, right, dims=ROWS):
    left_high, left_low = split(left)
    right_high, right_low = split(right)
    dot = functools.partial(lax.dot_general, dimension_numbers=dims, preferred_element_type=F32)
    return dot(left_high, right_high) + (dot(left_low, right_high) + dot(left_high, right_low))


def call(body, outs, ins, name, scratch=(), fixed=0):
    spaces = [pltpu.HBM] * fixed + [pltpu.VMEM] * (len(ins) - fixed)
    return pl.pallas_call(
        body,
        out_shape=[item(shape, dtype) for item, shape, dtype in outs],
        in_specs=[pl.BlockSpec(memory_space=space) for space in spaces],
        out_specs=[
            pl.BlockSpec(memory_space=pltpu.HBM if item is jax.ShapeDtypeStruct else pltpu.VMEM)
            for item, _, _ in outs
        ],
        scratch_shapes=list(scratch),
        compiler_params=pltpu.CompilerParams(vmem_limit_bytes=8 * 1024 * 1024),
        name=name,
    )(*[pltpu.with_memory_space_constraint(item, space) for item, space in zip(ins, spaces)])


def rows_of(index, height):
    return pl.ds(pl.multiple_of(index * height, height), height)


def send_faces(swaps, placed, messages):
    height = placed.shape[0] // FACES
    for (dim, odd), message in zip(swaps, messages):
        message[:height, :] = placed[rows_of(swap_face(dim, odd), height), :]


def first_kernel(swaps, order_hbm, start_hbm, *refs):
    hbm, held, (placed, *more) = refs[:3], refs[3:6], refs[6:]
    matrix, modes, root_map = held
    messages, (order, start, local_iter, mapped, sems) = more[: len(swaps)], more[len(swaps) :]
    pairs = [(order_hbm, order), (start_hbm, start)] + list(zip(hbm, held))
    copies = [pltpu.make_async_copy(*pair, sems.at[k]) for k, pair in enumerate(pairs)]
    for copy in copies:
        copy.start()
    height, lanes = placed.shape[0] // FACES, placed.shape[1]
    copies[0].wait()
    copies[1].wait()
    for j in range(FACES):
        local_iter[j * height : (j + 1) * height, :] = start[rows_of(order[0, j], height), :]
    copies[3].wait()
    copies[4].wait()
    mapped[...] = dot3(root_map[...], modes[...])
    for (dim, odd), message in zip(swaps, messages):
        link = mapped[:, rows_of(swap_face(dim, odd), height)]
        extra = link.shape[0] * height // lanes
        end = height + extra
        for k in range(lanes // height):
            message[height:end, k * height : (k + 1) * height] = link[k * extra : (k + 1) * extra, :]
    copies[2].wait()
    product = jnp.dot(matrix[...], local_iter[...], preferred_element_type=F32)
    for j in range(FACES):
        placed[rows_of(order[0, j], height), :] = product[j * height : (j + 1) * height, :]
    send_faces(swaps, placed, messages)


def constants_kernel(
    swaps, sizes, order_hbm, matrix, modes, root_map, weights, loads, placed,
    modes_t, scale, modes_f, matrix_f, modes_a, modes_b, ready, wide, order, sem
):
    copy = pltpu.make_async_copy(order_hbm, order, sem)
    copy.start()
    count, height = modes.shape[0], scale.shape[1]
    high, low = split(modes[...])
    modes_t[...] = jnp.concatenate([high.T, low.T, high.T], axis=1)
    for j in range(FACES):
        block = slice(j * height, (j + 1) * height)
        scale[block, :] = jnp.broadcast_to(weights[:, block], (height, height)).T
    for at, (dim, odd) in enumerate(swaps):
        face = swap_face(dim, odd)
        columns = modes[:, rows_of(face, height)]
        columns = jnp.where(has_neighbour(dim, face, sizes), columns, 0.0)
        block = slice(at * height, (at + 1) * height)
        modes_f[:count, block], modes_f[count : 2 * count, block] = split(columns)
        rows = root_map.shape[0]
        parts = split(dot3(root_map[...], columns))
        modes_f[2 * count : 2 * count + rows, block], modes_f[2 * count + rows :, block] = parts
    dot = functools.partial(jnp.dot, preferred_element_type=F32)
    modes_b[...] = dot(high, loads[...]) + dot(low, loads[...])
    ready[:count, :] = modes_b[...] - dot3(modes[...], placed[...])
    ready[count:, :] = dot3(root_map[...], ready[:count, :])
    copy.wait()
    for j in range(FACES):
        block = slice(j * height, (j + 1) * height)
        wide[:, rows_of(order[0, j], height)] = matrix[:, block]
    for j in range(FACES):
        block = slice(j * height, (j + 1) * height)
        matrix_f[rows_of(order[0, j], height), :] = wide[block, :]
    modes_a[:count, :], modes_a[count:, :] = split(dot(high, matrix_f[...]) + dot(low, matrix_f[...]))


def stack_halos(layout, swaps, sizes, halos, stack):
    height = stack.shape[0] // len(swaps)
    for (dim, odd), halo in zip(swaps, halos):
        at = layout.index((dim, odd))
        known = has_neighbour(dim, swap_face(dim, odd), sizes)
        stack[at * height : (at + 1) * height, :] = jnp.where(known, halo[:height, :], 0.0)
    return split(stack[...])


def coarse_kernel(swaps, sizes, ready, modes_f, region_rows, root_map, *more):
    halos, (coarse, root, note, stack) = more[: len(swaps)], more[len(swaps) :]
    modes, count = coarse.shape[0], root.shape[0]
    high, low = stack_halos(swaps, swaps, sizes, halos, stack)
    both = jnp.dot(modes_f[...], high, preferred_element_type=F32)
    fine = jnp.dot(modes_f[: 2 * modes + count, :], low, preferred_element_type=F32)
    coarse[...] = ready[:modes, :] - (both[:modes, :] + (both[modes : 2 * modes, :] + fine[:modes, :]))
    at = 2 * modes
    root[...] = ready[modes:, :] - (both[at : at + count, :] + (both[at + count :, :] + fine[at:, :]))
    lanes = root.shape[1]
    note[:count, :] = jnp.zeros_like(root)
    note[:count, :modes] = root_map[...]
    for k in range(region_rows.shape[1] // lanes):
        rows = slice(count + k * modes, count + (k + 1) * modes)
        note[rows, :] = region_rows[:, k * lanes : (k + 1) * lanes]
    note[-count:, :] = root[...]


def base_kernel(swaps, sizes, solution, loads, placed, scale, *more):
    halos, base = more[: len(swaps)], more[-1]
    height, lanes = scale.shape[1], placed.shape[1]

    def wide(rows):
        return jnp.concatenate([scale[rows, :]] * (lanes // height), axis=1)

    for j in range(FACES):
        rows = slice(j * height, (j + 1) * height)
        rest = loads[rows, :].astype(F32) - placed[rows, :]
        base[rows, :] = solution[rows, :].astype(F32) + wide(rows) * rest
    for (dim, odd), halo in zip(swaps, halos):
        face = swap_face(dim, odd)
        rows = rows_of(face, height)

        @pl.when(has_neighbour(dim, face, sizes))
        def _():
            base[rows, :] -= wide(rows) * halo[:height, :]


def links_kernel(swaps, sizes, modes, root_map, loads, matrix_f, modes_a, *more):
    halos, (tail, ahead_loads, ahead) = more[: len(swaps)], more[len(swaps) :]
    count, height = root_map.shape[0], loads.shape[0] // FACES
    lanes = loads.shape[1]
    ahead[...] = jnp.zeros_like(ahead)
    own = dot3(root_map[...], modes[...])
    ahead[count : 2 * count, :] = own
    for (dim, odd), halo in zip(swaps, halos):
        face = swap_face(dim, odd)
        known = has_neighbour(dim, face, sizes)
        end = height + count * height // lanes
        pieces = [halo[height:end, k * height : (k + 1) * height] for k in range(lanes // height)]
        link = jnp.where(known, jnp.concatenate(pieces, axis=0), 0.0)
        if dim == 0:
            ahead[rows_of(2 * face, count), rows_of(face, height)] = link
        else:
            ahead[count : 2 * count, rows_of(face, height)] += link
    dot = functools.partial(jnp.dot, preferred_element_type=F32)
    high, low = split(ahead[...])
    both = dot(jnp.concatenate([high, low], axis=0), matrix_f[...])
    done = modes_a.shape[0]
    tail[:done, :] = modes_a[...]
    high, low = split(both[: 3 * count, :] + both[3 * count :, :])
    tail[done : done + 3 * count, :] = high
    tail[done + 3 * count :, :] = low
    high, low = split(own)
    ahead_loads[...] = jnp.zeros_like(ahead_loads)
    ahead_loads[count : 2 * count, :] = dot(high, loads[...]) + dot(low, loads[...])


def merged_kernel(layout, swaps, sizes, ride, ready, modes_f, root_inverse, ahead, *more):
    halos, more = more[: len(swaps)], more[len(swaps) :]
    received, (message, faces, stack) = more[:-3], more[-3:]
    modes, height = ready.shape[0], faces.shape[0] // len(swaps)
    count = message.shape[0] - modes
    high, low = stack_halos(layout, swaps, sizes, halos, faces)
    both = jnp.dot(modes_f[: 2 * modes, :], high, preferred_element_type=F32)
    fine = jnp.dot(modes_f[:modes, :], low, preferred_element_type=F32)
    message[:modes, :] = ready[...] - (both[:modes, :] + (both[modes:, :] + fine))
    me = lax.axis_index("gx")
    stack[...] = jnp.zeros_like(stack)
    pieces = [(me, ahead)]
    for (dim, odd), halo in zip(swaps, halos):
        if ride and (dim, odd) == (0, 0):
            pieces.append((me ^ 1, halo.at[height:, :]))
    paired, single = far_offsets(sizes[0], 1 + ride)
    for offset, piece in zip([core_offset(pair) for pair in paired] + single, received):
        pieces.append((source(me, offset, sizes[0]), piece))
    for index, piece in pieces:
        rows = pl.ds(pl.multiple_of(index * count, count), 3 * count)
        stack[rows, :] += piece[...]
    message[modes:, :] = dot3(root_inverse[...], stack[count:-count, :])


def sum_kernel(own, other, total):
    total[...] = own[...] + other[other.shape[0] - own.shape[0] :, :]


def root_kernel(count, coarse, root_inverse, root, *more):
    received, (message, stack) = more[:-2], more[-2:]
    modes, height = coarse.shape[0], root.shape[0]
    me = lax.axis_index("gx")
    paired, single = far_offsets(count, 1 + nearest(count))
    offsets = [core_offset(pair) for pair in paired] + list(range(1, 1 + nearest(count))) + single
    stack[...] = jnp.zeros_like(stack)
    stack[rows_of(me, height), :] = root[...]
    for offset, piece in zip(offsets, received):
        stack[rows_of(source(me, offset, count), height), :] = piece[...]
    message[:modes, :] = coarse[...]
    message[modes:, :] = dot3(root_inverse[...], stack[...])


def parts_kernel(members, sizes, region_rows, root_map, note, factors):
    modes, order = region_rows.shape
    count, lanes = root_map.shape[0], note.shape[1]
    other_map = note[:count, :modes]
    blocks = [slice(count + k * modes, count + (k + 1) * modes) for k in range(order // lanes)]
    other_rows = jnp.concatenate([note[rows, :] for rows in blocks], axis=1)
    y, z = lax.axis_index("gy"), lax.axis_index("gz")
    half = sizes[0] // 2
    depth = len(members) * modes
    row = lax.broadcasted_iota(jnp.int32, (order, depth), 0)
    column = lax.broadcasted_iota(jnp.int32, (order, depth), 1)
    wanted = jnp.full((order, depth), -1, jnp.int32)
    for k, (dy, dz) in enumerate(members):
        at_y = 2 * source(y // 2, dy, half) + y % 2
        first = (at_y * sizes[1] + source(z, dz, sizes[1])) * modes
        inside = jnp.logical_and(column >= k * modes, column < (k + 1) * modes)
        wanted = jnp.where(inside, first + column - k * modes, wanted)
    chosen = jnp.where(row == wanted, 1.0, 0.0).astype(BF16)
    for at, (whole, maps) in enumerate(((region_rows[...], root_map[...]), (other_rows, other_map))):
        for level, piece in enumerate(split(whole)):
            rows = slice((2 * level + at) * modes, (2 * level + at + 1) * modes)
            factors[rows, :depth] = jnp.dot(piece, chosen, preferred_element_type=F32).astype(BF16)
        for level, piece in enumerate(split(maps.T)):
            rows = slice((2 * level + at) * modes, (2 * level + at + 1) * modes)
            factors[rows, depth:] = piece


def pair_kernel(modes, factors, first, *more):
    received, (own, out, tall) = more[:-3], more[-3:]
    total = first[modes:, :]
    tall[:modes, :] = first[:modes, :]
    for k, piece in enumerate(received, 1):
        tall[k * modes : (k + 1) * modes, :] = piece[:modes, :]
        total = total + piece[modes:, :]
    tall[(len(received) + 1) * modes :, :] = total
    high, low = split(tall[...])
    both = jnp.dot(factors[...], high, preferred_element_type=F32)
    fine = jnp.dot(factors[: 2 * modes, :], low, preferred_element_type=F32)
    total = both[: 2 * modes, :] + (both[2 * modes :, :] + fine)
    own[...] = total[:modes, :]
    out[...] = total[modes:, :]


def correction_factor(amplitude):
    high, low = split(amplitude)
    return jnp.concatenate([high, high, low], axis=0)


def middle_kernel(
    swaps, base, modes_t, own, other, matrix_f, tail, modes_b, ahead_loads,
    next_solution, placed, ready, ahead, *messages
):
    height = placed.shape[0] // FACES
    tall = correction_factor(own[...] + other[...])
    next_solution[...] = base[...] + jnp.dot(modes_t[...], tall, preferred_element_type=F32)
    local_iter = next_solution[...].astype(BF16)
    placed[...] = jnp.dot(matrix_f[...], local_iter, preferred_element_type=F32)
    more = jnp.dot(tail[...], local_iter, preferred_element_type=F32)
    modes, count = ready.shape[0], ahead.shape[0]
    ready[...] = modes_b[...] - (more[:modes, :] + more[modes : 2 * modes, :])
    more = more[2 * modes :, :]
    ahead[...] = ahead_loads[...] - (more[:count, :] + more[count:, :])
    send_faces(swaps, placed, messages)
    for message in messages:
        if message.shape[0] > height:
            message[height:, :] = ahead[...]


def last_kernel(base, modes_t, own, other, out, result, sems):
    tall = correction_factor(own[...] + other[...])
    parts = sems.shape[0]
    part = result.shape[0] // parts
    copies = []
    for k in range(parts):
        rows = slice(k * part, (k + 1) * part)
        result[rows, :] = base[rows, :] + jnp.dot(modes_t[rows, :], tall, preferred_element_type=F32)
        copies.append(pltpu.make_async_copy(result.at[rows, :], out.at[rows, :], sems.at[k]))
        copies[-1].start()
    for copy in copies:
        copy.wait()


def per_device(
    loads,
    start,
    interface_op,
    block_order,
    interface_weights,
    coarse_modes,
    region_weights,
    region_inverse,
    root_inverse,
):
    sizes = tuple(lax.axis_size(axis) for axis in AXES)
    iface = interface_op.shape[-1]
    cases = loads.shape[-1]
    height = iface // FACES
    matrix = interface_op.reshape(iface, iface)
    order = block_order.reshape(1, FACES)
    weights = interface_weights.reshape(1, iface)
    modes = coarse_modes.reshape(coarse_modes.shape[-2], iface)
    mode_count = modes.shape[0]
    root_map = region_weights.reshape(mode_count, region_weights.shape[-1]).T
    root_modes = root_map.shape[0]
    region_rows = region_inverse.reshape(mode_count, region_inverse.shape[-1])
    target = loads.reshape(iface, cases)
    solution = start.reshape(iface, cases)

    swaps = swap_list(sizes, FIRST_ORDER)
    later = swap_list(sizes, LATER_ORDER)
    half = sizes[1] // 2
    members = list(itertools.product(range(half), range(sizes[2])))

    ride = nearest(sizes[0])
    paired, single = far_offsets(sizes[0], 1 + ride)
    core = later.index((1, 0))
    full = (pltpu.VMEM, (iface, cases), F32)
    places = [pltpu.SMEM((1, FACES), jnp.int32)]
    faces = [pltpu.VMEM((len(swaps) * height, cases), F32)]

    def wide(rows, dtype=BF16):
        return (pltpu.VMEM, (rows, iface), dtype)

    def held(rows):
        return (pltpu.VMEM, (rows, cases), F32)

    def along(value, offset):
        pairs = []
        for place in itertools.product(*map(range, sizes)):
            step = offset if isinstance(offset, int) else offset[place[1] % 2]
            there = (partner(place[0], step, sizes[0]),) + place[1:]
            pairs.append((flat(sizes, place), flat(sizes, there)))
        return lax.ppermute(value, AXES, pairs)

    def exchange(messages, order):
        return [
            lax.ppermute(message, AXES, swap_pairs(sizes, dim, odd)) for (dim, odd), message in zip(order, messages)
        ]

    def core_sum(own, other):
        return call(sum_kernel, [held(own.shape[0])], [own, other], "core_sum")[0]

    def base_of(order, solution, placed, halos):
        return call(
            functools.partial(base_kernel, order, sizes),
            [full],
            [solution, target, placed, scale] + halos,
            "base",
        )[0]

    for step in range(ITERS):
        if step == 0:
            inputs = [order, solution, matrix, modes, root_map]
            matrix, modes, root_map, placed, *messages = call(
                functools.partial(first_kernel, swaps),
                [(pltpu.VMEM, item.shape, item.dtype) for item in inputs[2:]]
                + [full]
                + [held(height + root_modes * height // cases)] * len(swaps),
                inputs,
                "first_product",
                places
                + [pltpu.VMEM((iface, cases), BF16)] * 2
                + [pltpu.VMEM((root_modes, iface), F32), pltpu.SemaphoreType.DMA((5,))],
                len(inputs),
            )
            modes_t, scale, modes_f, matrix_f, modes_a, modes_b, ready = call(
                functools.partial(constants_kernel, swaps, sizes),
                [
                    (pltpu.VMEM, (iface, 3 * mode_count), BF16),
                    (pltpu.VMEM, (iface, height), F32),
                    (pltpu.VMEM, (2 * mode_count + 2 * root_modes, len(swaps) * height), BF16),
                    wide(iface),
                    wide(2 * mode_count),
                    held(mode_count),
                    held(mode_count + root_modes),
                ],
                [order, matrix, modes, root_map, weights, target, placed],
                "constants",
                [pltpu.VMEM((iface, iface), BF16)] + places + [pltpu.SemaphoreType.DMA],
                1,
            )
            halos = exchange(messages, swaps)
            blocks = region_rows.shape[1] // cases
            coarse, root, note = call(
                functools.partial(coarse_kernel, swaps, sizes),
                [held(mode_count), held(root_modes), held(2 * root_modes + mode_count * blocks)],
                [ready, modes_f, region_rows, root_map] + halos,
                "coarse",
                faces,
            )
            note = lax.ppermute(note, AXES, swap_pairs(sizes, 1, 0))
            both = core_sum(root, note)
            received = [along(root, offset) for offset in list(range(1, 1 + ride)) + single]
            received = [along(both, pair) for pair in paired] + received
            (factors,) = call(
                functools.partial(parts_kernel, members, sizes[1:]),
                [(pltpu.VMEM, (4 * mode_count, len(members) * mode_count + root_modes), BF16)],
                [region_rows, root_map, note],
                "parts",
            )
            base = base_of(swaps, solution, placed, halos)
            tail, ahead_loads = call(
                functools.partial(links_kernel, swaps, sizes),
                [wide(2 * mode_count + 6 * root_modes), held(3 * root_modes)],
                [modes, root_map, target, matrix_f, modes_a] + halos,
                "links",
                [pltpu.VMEM((3 * root_modes, iface), F32)],
            )
            (message,) = call(
                functools.partial(root_kernel, sizes[0]),
                [held(mode_count + root_modes)],
                [coarse, root_inverse, root] + received,
                "root_part",
                [pltpu.VMEM((root_inverse.shape[1], cases), F32)],
            )
        else:
            extra = [3 * root_modes * int(swap == (1, 0) or (ride and swap == (0, 0))) for swap in later]
            solution, placed, ready, ahead, *messages = call(
                functools.partial(middle_kernel, later),
                [full, full, held(mode_count), held(3 * root_modes)] + [held(height + more) for more in extra],
                [base, modes_t, own, other, matrix_f, tail, modes_b, ahead_loads],
                "update_product",
            )
            halos = exchange(messages, later)
            both = core_sum(ahead, halos[core])
            received = [along(both, pair) for pair in paired] + [along(ahead, offset) for offset in single]
            (message,) = call(
                functools.partial(merged_kernel, swaps, later, sizes, ride),
                [held(mode_count + root_modes)],
                [ready, modes_f, root_inverse, ahead] + halos + received,
                "coarse_root",
                faces + [pltpu.VMEM((root_inverse.shape[1] + 2 * root_modes, cases), F32)],
            )
            base = base_of(later, solution, placed, halos)
        pieces = []
        for dy, dz in members[1:]:
            moves = [
                (y * sizes[2] + z, (2 * partner(y // 2, dy, half) + y % 2) * sizes[2] + partner(z, dz, sizes[2]))
                for y in range(sizes[1])
                for z in range(sizes[2])
            ]
            pieces.append(lax.ppermute(message, ("gy", "gz"), moves))
        own, given = call(
            functools.partial(pair_kernel, mode_count),
            [held(mode_count), held(mode_count)],
            [factors, message] + pieces,
            "amplitude_parts",
            [pltpu.VMEM((len(members) * mode_count + root_modes, cases), F32)],
        )
        other = lax.ppermute(given, AXES, swap_pairs(sizes, 1, 0))
    (solution,) = call(
        last_kernel,
        [(jax.ShapeDtypeStruct, (iface, cases), F32)],
        [base, modes_t, own, other],
        "update_last",
        [pltpu.VMEM((iface, cases), F32), pltpu.SemaphoreType.DMA((4,))],
    )
    return solution.reshape(1, 1, 1, iface, cases)


def solution(mesh):
    placed = (
        P("gx", "gy", "gz", None, None),
        P("gx", "gy", "gz", None, None),
        P("gx", "gy", "gz", None, None),
        P("gx", "gy", "gz", None),
        P("gx", "gy", "gz", None),
        P("gx", "gy", "gz", None, None),
        P("gx", "gy", "gz", None, None),
        P("gx", ("gy", "gz"), None),
        P("gx", None),
    )
    return jax.shard_map(
        per_device,
        mesh=mesh,
        in_specs=placed,
        out_specs=P("gx", "gy", "gz", None, None),
        check_vma=False,
    )
```

```python
import functools
import itertools

import jax
import jax.numpy as jnp
from jax import lax
from jax.experimental import pallas as pl
from jax.experimental.pallas import tpu as pltpu
from jax.sharding import PartitionSpec as P

ITERS = 2
FACES = 8
AXES = ("gx", "gy", "gz")
FIRST_ORDER = ((1, 1), (2, 1), (2, 0), (0, 0), (0, 1), (1, 0))
LATER_ORDER = ((1, 0), (0, 0), (0, 1), (2, 1), (2, 0), (1, 1))
F32 = jnp.float32
BF16 = jnp.bfloat16
ROWS = (((1,), (0,)), ((), ()))
COLS = (((0,), (0,)), ((), ()))


def neighbour(index, count, odd):
    other = index + 1 if index % 2 == odd else index - 1
    return other if 0 <= other < count else None


def swap_list(sizes, wanted):
    return [swap for swap in wanted if sizes[swap[0]] > 1 + swap[1]]


def flat(sizes, place):
    return (place[0] * sizes[1] + place[1]) * sizes[2] + place[2]


def swap_pairs(sizes, dim, odd):
    pairs = []
    for place in itertools.product(*map(range, sizes)):
        there = list(place)
        other = neighbour(place[dim], sizes[dim], odd)
        if other is not None:
            there[dim] = other
        elif odd and sizes[dim] % 2 == 0:
            if dim == 1:
                there[1] = sizes[1] - 1 - place[1]
            elif sizes[1] % 2 == 0:
                there[1] = place[1] ^ 1
        if tuple(there) != place:
            pairs.append((flat(sizes, place), flat(sizes, there)))
    return pairs


def swap_face(dim, odd):
    high = (lax.axis_index(AXES[dim]) + odd + 1) % 2
    return 2 * dim + high


def has_neighbour(dim, face, sizes):
    other = lax.axis_index(AXES[dim]) + 2 * (face - 2 * dim) - 1
    return jnp.logical_and(other >= 0, other < sizes[dim])


def partner(index, offset, count):
    if count & (count - 1):
        return (index + offset) % count
    return index ^ offset


def source(index, offset, count):
    if count & (count - 1):
        return lax.rem(index + count - offset, count)
    return index ^ offset


def nearest(count):
    return int(count & (count - 1) == 0)


def far_offsets(count, near):
    offsets = list(range(near, count))
    paired = list(zip(offsets[0::2], offsets[1::2]))
    return paired, offsets[2 * len(paired) :]


def core_offset(pair):
    return jnp.where(lax.axis_index("gy") % 2 == 0, pair[0], pair[1])


def crossing(dy, dz):
    return int(dy != 0 or dz != 0)


def split(value):
    high = value.astype(BF16)
    return high, (value - high.astype(F32)).astype(BF16)


def dot3(left, right, dims=ROWS):
    left_high, left_low = split(left)
    right_high, right_low = split(right)
    dot = functools.partial(lax.dot_general, dimension_numbers=dims, preferred_element_type=F32)
    return dot(left_high, right_high) + (dot(left_low, right_high) + dot(left_high, right_low))


def call(body, outs, ins, name, scratch=(), fixed=0):
    spaces = [pltpu.HBM] * fixed + [pltpu.VMEM] * (len(ins) - fixed)
    return pl.pallas_call(
        body,
        out_shape=[item(shape, dtype) for item, shape, dtype in outs],
        in_specs=[pl.BlockSpec(memory_space=space) for space in spaces],
        out_specs=[
            pl.BlockSpec(memory_space=pltpu.HBM if item is jax.ShapeDtypeStruct else pltpu.VMEM)
            for item, _, _ in outs
        ],
        scratch_shapes=list(scratch),
        compiler_params=pltpu.CompilerParams(vmem_limit_bytes=8 * 1024 * 1024),
        name=name,
    )(*[pltpu.with_memory_space_constraint(item, space) for item, space in zip(ins, spaces)])


def rows_of(index, height):
    return pl.ds(pl.multiple_of(index * height, height), height)


def send_faces(swaps, placed, messages):
    height = placed.shape[0] // FACES
    for (dim, odd), message in zip(swaps, messages):
        message[:height, :] = placed[rows_of(swap_face(dim, odd), height), :]


def first_kernel(swaps, order_hbm, start_hbm, *refs):
    hbm, held, (placed, *more) = refs[:3], refs[3:6], refs[6:]
    matrix, modes, root_map = held
    messages, (order, start, local_iter, mapped, sems) = more[: len(swaps)], more[len(swaps) :]
    pairs = [(order_hbm, order), (start_hbm, start)] + list(zip(hbm, held))
    copies = [pltpu.make_async_copy(*pair, sems.at[k]) for k, pair in enumerate(pairs)]
    for copy in copies:
        copy.start()
    height, lanes = placed.shape[0] // FACES, placed.shape[1]
    copies[0].wait()
    copies[1].wait()
    for j in range(FACES):
        local_iter[j * height : (j + 1) * height, :] = start[rows_of(order[0, j], height), :]
    copies[3].wait()
    copies[4].wait()
    mapped[...] = dot3(root_map[...], modes[...])
    for (dim, odd), message in zip(swaps, messages):
        link = mapped[:, rows_of(swap_face(dim, odd), height)]
        extra = link.shape[0] * height // lanes
        end = height + extra
        for k in range(lanes // height):
            message[height:end, k * height : (k + 1) * height] = link[k * extra : (k + 1) * extra, :]
    copies[2].wait()
    product = jnp.dot(matrix[...], local_iter[...], preferred_element_type=F32)
    for j in range(FACES):
        placed[rows_of(order[0, j], height), :] = product[j * height : (j + 1) * height, :]
    send_faces(swaps, placed, messages)


def constants_kernel(
    swaps, sizes, order_hbm, matrix, modes, root_map, weights, loads, placed,
    modes_t, scale, modes_f, matrix_f, modes_a, modes_b, ready, wide, order, sem
):
    copy = pltpu.make_async_copy(order_hbm, order, sem)
    copy.start()
    count, height = modes.shape[0], scale.shape[1]
    high, low = split(modes[...])
    modes_t[...] = jnp.concatenate([high.T, low.T, high.T], axis=1)
    for j in range(FACES):
        block = slice(j * height, (j + 1) * height)
        scale[block, :] = jnp.broadcast_to(weights[:, block], (height, height)).T
    for at, (dim, odd) in enumerate(swaps):
        face = swap_face(dim, odd)
        columns = modes[:, rows_of(face, height)]
        columns = jnp.where(has_neighbour(dim, face, sizes), columns, 0.0)
        block = slice(at * height, (at + 1) * height)
        modes_f[:count, block], modes_f[count : 2 * count, block] = split(columns)
        rows = root_map.shape[0]
        parts = split(dot3(root_map[...], columns))
        modes_f[2 * count : 2 * count + rows, block], modes_f[2 * count + rows :, block] = parts
    dot = functools.partial(jnp.dot, preferred_element_type=F32)
    modes_b[...] = dot(high, loads[...]) + dot(low, loads[...])
    ready[:count, :] = modes_b[...] - dot3(modes[...], placed[...])
    ready[count:, :] = dot3(root_map[...], ready[:count, :])
    copy.wait()
    for j in range(FACES):
        block = slice(j * height, (j + 1) * height)
        wide[:, rows_of(order[0, j], height)] = matrix[:, block]
    for j in range(FACES):
        block = slice(j * height, (j + 1) * height)
        matrix_f[rows_of(order[0, j], height), :] = wide[block, :]
    modes_a[:count, :], modes_a[count:, :] = split(dot(high, matrix_f[...]) + dot(low, matrix_f[...]))


def stack_halos(layout, swaps, sizes, halos, stack):
    height = stack.shape[0] // len(swaps)
    for (dim, odd), halo in zip(swaps, halos):
        at = layout.index((dim, odd))
        known = has_neighbour(dim, swap_face(dim, odd), sizes)
        stack[at * height : (at + 1) * height, :] = jnp.where(known, halo[:height, :], 0.0)
    return split(stack[...])


def coarse_kernel(swaps, sizes, ready, modes_f, region_rows, root_map, *more):
    halos, (coarse, root, note, stack) = more[: len(swaps)], more[len(swaps) :]
    modes, count = coarse.shape[0], root.shape[0]
    high, low = stack_halos(swaps, swaps, sizes, halos, stack)
    both = jnp.dot(modes_f[...], high, preferred_element_type=F32)
    fine = jnp.dot(modes_f[: 2 * modes + count, :], low, preferred_element_type=F32)
    coarse[...] = ready[:modes, :] - (both[:modes, :] + (both[modes : 2 * modes, :] + fine[:modes, :]))
    at = 2 * modes
    root[...] = ready[modes:, :] - (both[at : at + count, :] + (both[at + count :, :] + fine[at:, :]))
    lanes = root.shape[1]
    note[:count, :] = jnp.zeros_like(root)
    note[:count, :modes] = root_map[...]
    for k in range(region_rows.shape[1] // lanes):
        rows = slice(count + k * modes, count + (k + 1) * modes)
        note[rows, :] = region_rows[:, k * lanes : (k + 1) * lanes]
    note[-count:, :] = root[...]


def base_kernel(swaps, sizes, solution, loads, placed, scale, *more):
    halos, base = more[: len(swaps)], more[-1]
    height, lanes = scale.shape[1], placed.shape[1]

    def wide(rows):
        return jnp.concatenate([scale[rows, :]] * (lanes // height), axis=1)

    for j in range(FACES):
        rows = slice(j * height, (j + 1) * height)
        rest = loads[rows, :].astype(F32) - placed[rows, :]
        base[rows, :] = solution[rows, :].astype(F32) + wide(rows) * rest
    for (dim, odd), halo in zip(swaps, halos):
        face = swap_face(dim, odd)
        rows = rows_of(face, height)

        @pl.when(has_neighbour(dim, face, sizes))
        def _():
            base[rows, :] -= wide(rows) * halo[:height, :]


def links_kernel(swaps, sizes, modes, root_map, loads, matrix_f, modes_a, *more):
    halos, (tail, ahead_loads, ahead) = more[: len(swaps)], more[len(swaps) :]
    count, height = root_map.shape[0], loads.shape[0] // FACES
    lanes = loads.shape[1]
    ahead[...] = jnp.zeros_like(ahead)
    own = dot3(root_map[...], modes[...])
    ahead[count : 2 * count, :] = own
    for (dim, odd), halo in zip(swaps, halos):
        face = swap_face(dim, odd)
        known = has_neighbour(dim, face, sizes)
        end = height + count * height // lanes
        pieces = [halo[height:end, k * height : (k + 1) * height] for k in range(lanes // height)]
        link = jnp.where(known, jnp.concatenate(pieces, axis=0), 0.0)
        if dim == 0:
            ahead[rows_of(2 * face, count), rows_of(face, height)] = link
        else:
            ahead[count : 2 * count, rows_of(face, height)] += link
    dot = functools.partial(jnp.dot, preferred_element_type=F32)
    high, low = split(ahead[...])
    both = dot(jnp.concatenate([high, low], axis=0), matrix_f[...])
    done = modes_a.shape[0]
    tail[:done, :] = modes_a[...]
    high, low = split(both[: 3 * count, :] + both[3 * count :, :])
    tail[done : done + 3 * count, :] = high
    tail[done + 3 * count :, :] = low
    high, low = split(own)
    ahead_loads[...] = jnp.zeros_like(ahead_loads)
    ahead_loads[count : 2 * count, :] = dot(high, loads[...]) + dot(low, loads[...])


def merged_kernel(layout, swaps, sizes, ride, ready, modes_f, root_inverse, ahead, *more):
    halos, more = more[: len(swaps)], more[len(swaps) :]
    received, (message, faces, stack) = more[:-3], more[-3:]
    modes, height = ready.shape[0], faces.shape[0] // len(swaps)
    count = message.shape[0] - modes
    high, low = stack_halos(layout, swaps, sizes, halos, faces)
    both = jnp.dot(modes_f[: 2 * modes, :], high, preferred_element_type=F32)
    fine = jnp.dot(modes_f[:modes, :], low, preferred_element_type=F32)
    message[:modes, :] = ready[...] - (both[:modes, :] + (both[modes:, :] + fine))
    me = lax.axis_index("gx")
    stack[...] = jnp.zeros_like(stack)
    pieces = [(me, ahead)]
    for (dim, odd), halo in zip(swaps, halos):
        if ride and (dim, odd) == (0, 0):
            pieces.append((me ^ 1, halo.at[height:, :]))
    paired, single = far_offsets(sizes[0], 1 + ride)
    for offset, piece in zip([core_offset(pair) for pair in paired] + single, received):
        pieces.append((source(me, offset, sizes[0]), piece))
    for index, piece in pieces:
        rows = pl.ds(pl.multiple_of(index * count, count), 3 * count)
        stack[rows, :] += piece[...]
    message[modes:, :] = dot3(root_inverse[...], stack[count:-count, :])


def sum_kernel(own, other, total):
    total[...] = own[...] + other[other.shape[0] - own.shape[0] :, :]


def root_kernel(count, coarse, root_inverse, root, *more):
    received, (message, stack) = more[:-2], more[-2:]
    modes, height = coarse.shape[0], root.shape[0]
    me = lax.axis_index("gx")
    paired, single = far_offsets(count, 1 + nearest(count))
    offsets = [core_offset(pair) for pair in paired] + list(range(1, 1 + nearest(count))) + single
    stack[...] = jnp.zeros_like(stack)
    stack[rows_of(me, height), :] = root[...]
    for offset, piece in zip(offsets, received):
        stack[rows_of(source(me, offset, count), height), :] = piece[...]
    message[:modes, :] = coarse[...]
    message[modes:, :] = dot3(root_inverse[...], stack[...])


def parts_kernel(members, sizes, region_rows, root_map, note, factors):
    modes, order = region_rows.shape
    count, lanes = root_map.shape[0], note.shape[1]
    other_map = note[:count, :modes]
    blocks = [slice(count + k * modes, count + (k + 1) * modes) for k in range(order // lanes)]
    other_rows = jnp.concatenate([note[rows, :] for rows in blocks], axis=1)
    y, z = lax.axis_index("gy"), lax.axis_index("gz")
    half = sizes[0] // 2
    depth = len(members) * modes
    row = lax.broadcasted_iota(jnp.int32, (order, depth), 0)
    column = lax.broadcasted_iota(jnp.int32, (order, depth), 1)
    wanted = jnp.full((order, depth), -1, jnp.int32)
    for k, (dy, dz) in enumerate(members):
        at_y = 2 * source(y // 2, dy, half) + (y + crossing(dy, dz)) % 2
        first = (at_y * sizes[1] + source(z, dz, sizes[1])) * modes
        inside = jnp.logical_and(column >= k * modes, column < (k + 1) * modes)
        wanted = jnp.where(inside, first + column - k * modes, wanted)
    chosen = jnp.where(row == wanted, 1.0, 0.0).astype(BF16)
    for at, (whole, maps) in enumerate(((region_rows[...], root_map[...]), (other_rows, other_map))):
        for level, piece in enumerate(split(whole)):
            rows = slice((2 * level + at) * modes, (2 * level + at + 1) * modes)
            factors[rows, :depth] = jnp.dot(piece, chosen, preferred_element_type=F32).astype(BF16)
        for level, piece in enumerate(split(maps.T)):
            rows = slice((2 * level + at) * modes, (2 * level + at + 1) * modes)
            factors[rows, depth:] = piece


def pair_kernel(modes, factors, first, *more):
    received, (own, out, tall) = more[:-3], more[-3:]
    total = first[modes:, :]
    tall[:modes, :] = first[:modes, :]
    for k, piece in enumerate(received, 1):
        tall[k * modes : (k + 1) * modes, :] = piece[:modes, :]
        total = total + piece[modes:, :]
    tall[(len(received) + 1) * modes :, :] = total
    high, low = split(tall[...])
    both = jnp.dot(factors[...], high, preferred_element_type=F32)
    fine = jnp.dot(factors[: 2 * modes, :], low, preferred_element_type=F32)
    total = both[: 2 * modes, :] + (both[2 * modes :, :] + fine)
    own[...] = total[:modes, :]
    out[...] = total[modes:, :]


def correction_factor(amplitude):
    high, low = split(amplitude)
    return jnp.concatenate([high, high, low], axis=0)


def middle_kernel(
    swaps, base, modes_t, own, other, matrix_f, tail, modes_b, ahead_loads,
    next_solution, placed, ready, ahead, *messages
):
    height = placed.shape[0] // FACES
    tall = correction_factor(own[...] + other[...])
    next_solution[...] = base[...] + jnp.dot(modes_t[...], tall, preferred_element_type=F32)
    local_iter = next_solution[...].astype(BF16)
    placed[...] = jnp.dot(matrix_f[...], local_iter, preferred_element_type=F32)
    more = jnp.dot(tail[...], local_iter, preferred_element_type=F32)
    modes, count = ready.shape[0], ahead.shape[0]
    ready[...] = modes_b[...] - (more[:modes, :] + more[modes : 2 * modes, :])
    more = more[2 * modes :, :]
    ahead[...] = ahead_loads[...] - (more[:count, :] + more[count:, :])
    send_faces(swaps, placed, messages)
    for message in messages:
        if message.shape[0] > height:
            message[height:, :] = ahead[...]


def last_kernel(base, modes_t, own, other, out, result, sems):
    tall = correction_factor(own[...] + other[...])
    parts = sems.shape[0]
    part = result.shape[0] // parts
    copies = []
    for k in range(parts):
        rows = slice(k * part, (k + 1) * part)
        result[rows, :] = base[rows, :] + jnp.dot(modes_t[rows, :], tall, preferred_element_type=F32)
        copies.append(pltpu.make_async_copy(result.at[rows, :], out.at[rows, :], sems.at[k]))
        copies[-1].start()
    for copy in copies:
        copy.wait()


def per_device(
    loads,
    start,
    interface_op,
    block_order,
    interface_weights,
    coarse_modes,
    region_weights,
    region_inverse,
    root_inverse,
):
    sizes = tuple(lax.axis_size(axis) for axis in AXES)
    iface = interface_op.shape[-1]
    cases = loads.shape[-1]
    height = iface // FACES
    matrix = interface_op.reshape(iface, iface)
    order = block_order.reshape(1, FACES)
    weights = interface_weights.reshape(1, iface)
    modes = coarse_modes.reshape(coarse_modes.shape[-2], iface)
    mode_count = modes.shape[0]
    root_map = region_weights.reshape(mode_count, region_weights.shape[-1]).T
    root_modes = root_map.shape[0]
    region_rows = region_inverse.reshape(mode_count, region_inverse.shape[-1])
    target = loads.reshape(iface, cases)
    solution = start.reshape(iface, cases)

    swaps = swap_list(sizes, FIRST_ORDER)
    later = swap_list(sizes, LATER_ORDER)
    half = sizes[1] // 2
    members = list(itertools.product(range(half), range(sizes[2])))

    ride = nearest(sizes[0])
    paired, single = far_offsets(sizes[0], 1 + ride)
    core = later.index((1, 0))
    full = (pltpu.VMEM, (iface, cases), F32)
    places = [pltpu.SMEM((1, FACES), jnp.int32)]
    faces = [pltpu.VMEM((len(swaps) * height, cases), F32)]

    def wide(rows, dtype=BF16):
        return (pltpu.VMEM, (rows, iface), dtype)

    def held(rows):
        return (pltpu.VMEM, (rows, cases), F32)

    def along(value, offset):
        pairs = []
        for place in itertools.product(*map(range, sizes)):
            step = offset if isinstance(offset, int) else offset[place[1] % 2]
            there = (partner(place[0], step, sizes[0]), place[1], place[2])
            pairs.append((flat(sizes, place), flat(sizes, there)))
        return lax.ppermute(value, AXES, pairs)

    def exchange(messages, order):
        return [
            lax.ppermute(message, AXES, swap_pairs(sizes, dim, odd)) for (dim, odd), message in zip(order, messages)
        ]

    def core_sum(own, other):
        return call(sum_kernel, [held(own.shape[0])], [own, other], "core_sum")[0]

    def base_of(order, solution, placed, halos):
        return call(
            functools.partial(base_kernel, order, sizes),
            [full],
            [solution, target, placed, scale] + halos,
            "base",
        )[0]

    for step in range(ITERS):
        if step == 0:
            inputs = [order, solution, matrix, modes, root_map]
            matrix, modes, root_map, placed, *messages = call(
                functools.partial(first_kernel, swaps),
                [(pltpu.VMEM, item.shape, item.dtype) for item in inputs[2:]]
                + [full]
                + [held(height + root_modes * height // cases)] * len(swaps),
                inputs,
                "first_product",
                places
                + [pltpu.VMEM((iface, cases), BF16)] * 2
                + [pltpu.VMEM((root_modes, iface), F32), pltpu.SemaphoreType.DMA((5,))],
                len(inputs),
            )
            modes_t, scale, modes_f, matrix_f, modes_a, modes_b, ready = call(
                functools.partial(constants_kernel, swaps, sizes),
                [
                    (pltpu.VMEM, (iface, 3 * mode_count), BF16),
                    (pltpu.VMEM, (iface, height), F32),
                    (pltpu.VMEM, (2 * mode_count + 2 * root_modes, len(swaps) * height), BF16),
                    wide(iface),
                    wide(2 * mode_count),
                    held(mode_count),
                    held(mode_count + root_modes),
                ],
                [order, matrix, modes, root_map, weights, target, placed],
                "constants",
                [pltpu.VMEM((iface, iface), BF16)] + places + [pltpu.SemaphoreType.DMA],
                1,
            )
            halos = exchange(messages, swaps)
            blocks = region_rows.shape[1] // cases
            coarse, root, note = call(
                functools.partial(coarse_kernel, swaps, sizes),
                [held(mode_count), held(root_modes), held(2 * root_modes + mode_count * blocks)],
                [ready, modes_f, region_rows, root_map] + halos,
                "coarse",
                faces,
            )
            note = lax.ppermute(note, AXES, swap_pairs(sizes, 1, 0))
            both = core_sum(root, note)
            received = [along(root, offset) for offset in list(range(1, 1 + ride)) + single]
            received = [along(both, pair) for pair in paired] + received
            (factors,) = call(
                functools.partial(parts_kernel, members, sizes[1:]),
                [(pltpu.VMEM, (4 * mode_count, len(members) * mode_count + root_modes), BF16)],
                [region_rows, root_map, note],
                "parts",
            )
            base = base_of(swaps, solution, placed, halos)
            tail, ahead_loads = call(
                functools.partial(links_kernel, swaps, sizes),
                [wide(2 * mode_count + 6 * root_modes), held(3 * root_modes)],
                [modes, root_map, target, matrix_f, modes_a] + halos,
                "links",
                [pltpu.VMEM((3 * root_modes, iface), F32)],
            )
            (message,) = call(
                functools.partial(root_kernel, sizes[0]),
                [held(mode_count + root_modes)],
                [coarse, root_inverse, root] + received,
                "root_part",
                [pltpu.VMEM((root_inverse.shape[1], cases), F32)],
            )
        else:
            extra = [3 * root_modes * int(swap == (1, 0) or (ride and swap == (0, 0))) for swap in later]
            solution, placed, ready, ahead, *messages = call(
                functools.partial(middle_kernel, later),
                [full, full, held(mode_count), held(3 * root_modes)] + [held(height + more) for more in extra],
                [base, modes_t, own, other, matrix_f, tail, modes_b, ahead_loads],
                "update_product",
            )
            halos = exchange(messages, later)
            both = core_sum(ahead, halos[core])
            received = [along(both, pair) for pair in paired] + [along(ahead, offset) for offset in single]
            (message,) = call(
                functools.partial(merged_kernel, swaps, later, sizes, ride),
                [held(mode_count + root_modes)],
                [ready, modes_f, root_inverse, ahead] + halos + received,
                "coarse_root",
                faces + [pltpu.VMEM((root_inverse.shape[1] + 2 * root_modes, cases), F32)],
            )
            base = base_of(later, solution, placed, halos)
        pieces = []
        for dy, dz in members[1:]:
            moves = []
            for place in itertools.product(*map(range, sizes)):
                x, y, z = place
                at_y = 2 * partner(y // 2, dy, half) + (y + crossing(dy, dz)) % 2
                moves.append((flat(sizes, place), flat(sizes, (x, at_y, partner(z, dz, sizes[2])))))
            pieces.append(lax.ppermute(message, AXES, moves))
        own, given = call(
            functools.partial(pair_kernel, mode_count),
            [held(mode_count), held(mode_count)],
            [factors, message] + pieces,
            "amplitude_parts",
            [pltpu.VMEM((len(members) * mode_count + root_modes, cases), F32)],
        )
        other = lax.ppermute(given, AXES, swap_pairs(sizes, 1, 0))
    (solution,) = call(
        last_kernel,
        [(jax.ShapeDtypeStruct, (iface, cases), F32)],
        [base, modes_t, own, other],
        "update_last",
        [pltpu.VMEM((iface, cases), F32), pltpu.SemaphoreType.DMA((4,))],
    )
    return solution.reshape(1, 1, 1, iface, cases)


def solution(mesh):
    placed = (
        P("gx", "gy", "gz", None, None),
        P("gx", "gy", "gz", None, None),
        P("gx", "gy", "gz", None, None),
        P("gx", "gy", "gz", None),
        P("gx", "gy", "gz", None),
        P("gx", "gy", "gz", None, None),
        P("gx", "gy", "gz", None, None),
        P("gx", ("gy", "gz"), None),
        P("gx", None),
    )
    return jax.shard_map(
        per_device,
        mesh=mesh,
        in_specs=placed,
        out_specs=P("gx", "gy", "gz", None, None),
        check_vma=False,
    )
```

```python
import functools
import itertools

import jax
import jax.numpy as jnp
from jax import lax
from jax.experimental import pallas as pl
from jax.experimental.pallas import tpu as pltpu
from jax.sharding import PartitionSpec as P

ITERS = 2
FACES = 8
AXES = ("gx", "gy", "gz")
FIRST_ORDER = ((0, 0), (2, 1), (2, 0), (1, 1), (0, 1), (1, 0))
LATER_ORDER = ((1, 0), (0, 0), (0, 1), (2, 1), (2, 0), (1, 1))
F32 = jnp.float32
BF16 = jnp.bfloat16
ROWS = (((1,), (0,)), ((), ()))
COLS = (((0,), (0,)), ((), ()))


def neighbour(index, count, odd):
    other = index + 1 if index % 2 == odd else index - 1
    return other if 0 <= other < count else None


def swap_list(sizes, wanted):
    return [swap for swap in wanted if sizes[swap[0]] > 1 + swap[1]]


def flat(sizes, place):
    return (place[0] * sizes[1] + place[1]) * sizes[2] + place[2]


def swap_pairs(sizes, dim, odd):
    pairs = []
    for place in itertools.product(*map(range, sizes)):
        there = list(place)
        other = neighbour(place[dim], sizes[dim], odd)
        if other is not None:
            there[dim] = other
        elif odd and sizes[dim] % 2 == 0:
            if dim == 1:
                there[1] = sizes[1] - 1 - place[1]
            elif sizes[1] % 2 == 0:
                there[1] = place[1] ^ 1
        if tuple(there) != place:
            pairs.append((flat(sizes, place), flat(sizes, there)))
    return pairs


def swap_face(dim, odd):
    high = (lax.axis_index(AXES[dim]) + odd + 1) % 2
    return 2 * dim + high


def has_neighbour(dim, face, sizes):
    other = lax.axis_index(AXES[dim]) + 2 * (face - 2 * dim) - 1
    return jnp.logical_and(other >= 0, other < sizes[dim])


def partner(index, offset, count):
    if count & (count - 1):
        return (index + offset) % count
    return index ^ offset


def source(index, offset, count):
    if count & (count - 1):
        return lax.rem(index + count - offset, count)
    return index ^ offset


def nearest(count):
    return int(count & (count - 1) == 0)


def far_offsets(count, near):
    offsets = list(range(near, count))
    paired = list(zip(offsets[0::2], offsets[1::2]))
    return paired, offsets[2 * len(paired) :]


def core_offset(pair):
    return jnp.where(lax.axis_index("gy") % 2 == 0, pair[0], pair[1])


def crossing(dy, dz):
    return int(dy != 0 or dz != 0)


def split(value):
    high = value.astype(BF16)
    return high, (value - high.astype(F32)).astype(BF16)


def dot3(left, right, dims=ROWS):
    left_high, left_low = split(left)
    right_high, right_low = split(right)
    dot = functools.partial(lax.dot_general, dimension_numbers=dims, preferred_element_type=F32)
    return dot(left_high, right_high) + (dot(left_low, right_high) + dot(left_high, right_low))


def call(body, outs, ins, name, scratch=(), fixed=0):
    spaces = [pltpu.HBM] * fixed + [pltpu.VMEM] * (len(ins) - fixed)
    return pl.pallas_call(
        body,
        out_shape=[item(shape, dtype) for item, shape, dtype in outs],
        in_specs=[pl.BlockSpec(memory_space=space) for space in spaces],
        out_specs=[
            pl.BlockSpec(memory_space=pltpu.HBM if item is jax.ShapeDtypeStruct else pltpu.VMEM)
            for item, _, _ in outs
        ],
        scratch_shapes=list(scratch),
        compiler_params=pltpu.CompilerParams(vmem_limit_bytes=8 * 1024 * 1024),
        name=name,
    )(*[pltpu.with_memory_space_constraint(item, space) for item, space in zip(ins, spaces)])


def rows_of(index, height):
    return pl.ds(pl.multiple_of(index * height, height), height)


def send_faces(swaps, placed, messages):
    height = placed.shape[0] // FACES
    for (dim, odd), message in zip(swaps, messages):
        message[:height, :] = placed[rows_of(swap_face(dim, odd), height), :]


def first_kernel(swaps, order_hbm, start_hbm, *refs):
    hbm, held, (placed, *more) = refs[:3], refs[3:6], refs[6:]
    matrix, modes, root_map = held
    messages, (order, start, local_iter, mapped, sems) = more[: len(swaps)], more[len(swaps) :]
    pairs = [(order_hbm, order), (start_hbm, start)] + list(zip(hbm, held))
    copies = [pltpu.make_async_copy(*pair, sems.at[k]) for k, pair in enumerate(pairs)]
    for copy in copies:
        copy.start()
    height, lanes = placed.shape[0] // FACES, placed.shape[1]
    copies[0].wait()
    copies[1].wait()
    for j in range(FACES):
        local_iter[j * height : (j + 1) * height, :] = start[rows_of(order[0, j], height), :]
    copies[3].wait()
    copies[4].wait()
    mapped[...] = dot3(root_map[...], modes[...])
    for (dim, odd), message in zip(swaps, messages):
        link = mapped[:, rows_of(swap_face(dim, odd), height)]
        extra = link.shape[0] * height // lanes
        end = height + extra
        for k in range(lanes // height):
            message[height:end, k * height : (k + 1) * height] = link[k * extra : (k + 1) * extra, :]
    copies[2].wait()
    product = jnp.dot(matrix[...], local_iter[...], preferred_element_type=F32)
    for j in range(FACES):
        placed[rows_of(order[0, j], height), :] = product[j * height : (j + 1) * height, :]
    send_faces(swaps, placed, messages)


def constants_kernel(
    swaps, sizes, order_hbm, matrix, modes, root_map, weights, loads, placed,
    modes_t, scale, modes_f, matrix_f, modes_a, modes_b, ready, wide, order, sem
):
    copy = pltpu.make_async_copy(order_hbm, order, sem)
    copy.start()
    count, height = modes.shape[0], scale.shape[1]
    high, low = split(modes[...])
    modes_t[...] = jnp.concatenate([high.T, low.T, high.T], axis=1)
    for j in range(FACES):
        block = slice(j * height, (j + 1) * height)
        scale[block, :] = jnp.broadcast_to(weights[:, block], (height, height)).T
    for at, (dim, odd) in enumerate(swaps):
        face = swap_face(dim, odd)
        columns = modes[:, rows_of(face, height)]
        columns = jnp.where(has_neighbour(dim, face, sizes), columns, 0.0)
        block = slice(at * height, (at + 1) * height)
        modes_f[:count, block], modes_f[count : 2 * count, block] = split(columns)
        rows = root_map.shape[0]
        parts = split(dot3(root_map[...], columns))
        modes_f[2 * count : 2 * count + rows, block], modes_f[2 * count + rows :, block] = parts
    dot = functools.partial(jnp.dot, preferred_element_type=F32)
    modes_b[...] = dot(high, loads[...]) + dot(low, loads[...])
    ready[:count, :] = modes_b[...] - dot3(modes[...], placed[...])
    ready[count:, :] = dot3(root_map[...], ready[:count, :])
    copy.wait()
    for j in range(FACES):
        block = slice(j * height, (j + 1) * height)
        wide[:, rows_of(order[0, j], height)] = matrix[:, block]
    for j in range(FACES):
        block = slice(j * height, (j + 1) * height)
        matrix_f[rows_of(order[0, j], height), :] = wide[block, :]
    modes_a[:count, :], modes_a[count:, :] = split(dot(high, matrix_f[...]) + dot(low, matrix_f[...]))


def stack_halos(layout, swaps, sizes, halos, stack):
    height = stack.shape[0] // len(swaps)
    for (dim, odd), halo in zip(swaps, halos):
        at = layout.index((dim, odd))
        known = has_neighbour(dim, swap_face(dim, odd), sizes)
        stack[at * height : (at + 1) * height, :] = jnp.where(known, halo[:height, :], 0.0)
    return split(stack[...])


def coarse_kernel(swaps, sizes, ready, modes_f, region_rows, root_map, *more):
    halos, (coarse, root, note, stack) = more[: len(swaps)], more[len(swaps) :]
    modes, count = coarse.shape[0], root.shape[0]
    high, low = stack_halos(swaps, swaps, sizes, halos, stack)
    both = jnp.dot(modes_f[...], high, preferred_element_type=F32)
    fine = jnp.dot(modes_f[: 2 * modes + count, :], low, preferred_element_type=F32)
    coarse[...] = ready[:modes, :] - (both[:modes, :] + (both[modes : 2 * modes, :] + fine[:modes, :]))
    at = 2 * modes
    root[...] = ready[modes:, :] - (both[at : at + count, :] + (both[at + count :, :] + fine[at:, :]))
    lanes = root.shape[1]
    note[:count, :] = jnp.zeros_like(root)
    note[:count, :modes] = root_map[...]
    for k in range(region_rows.shape[1] // lanes):
        rows = slice(count + k * modes, count + (k + 1) * modes)
        note[rows, :] = region_rows[:, k * lanes : (k + 1) * lanes]
    note[-count:, :] = root[...]


def base_kernel(swaps, sizes, solution, loads, placed, scale, *more):
    halos, base = more[: len(swaps)], more[-1]
    height, lanes = scale.shape[1], placed.shape[1]

    def wide(rows):
        return jnp.concatenate([scale[rows, :]] * (lanes // height), axis=1)

    for j in range(FACES):
        rows = slice(j * height, (j + 1) * height)
        rest = loads[rows, :].astype(F32) - placed[rows, :]
        base[rows, :] = solution[rows, :].astype(F32) + wide(rows) * rest
    for (dim, odd), halo in zip(swaps, halos):
        face = swap_face(dim, odd)
        rows = rows_of(face, height)

        @pl.when(has_neighbour(dim, face, sizes))
        def _():
            base[rows, :] -= wide(rows) * halo[:height, :]


def links_kernel(swaps, sizes, modes, root_map, loads, matrix_f, modes_a, *more):
    halos, (tail, ahead_loads, ahead) = more[: len(swaps)], more[len(swaps) :]
    count, height = root_map.shape[0], loads.shape[0] // FACES
    lanes = loads.shape[1]
    ahead[...] = jnp.zeros_like(ahead)
    own = dot3(root_map[...], modes[...])
    ahead[count : 2 * count, :] = own
    for (dim, odd), halo in zip(swaps, halos):
        face = swap_face(dim, odd)
        known = has_neighbour(dim, face, sizes)
        end = height + count * height // lanes
        pieces = [halo[height:end, k * height : (k + 1) * height] for k in range(lanes // height)]
        link = jnp.where(known, jnp.concatenate(pieces, axis=0), 0.0)
        if dim == 0:
            ahead[rows_of(2 * face, count), rows_of(face, height)] = link
        else:
            ahead[count : 2 * count, rows_of(face, height)] += link
    dot = functools.partial(jnp.dot, preferred_element_type=F32)
    high, low = split(ahead[...])
    both = dot(jnp.concatenate([high, low], axis=0), matrix_f[...])
    done = modes_a.shape[0]
    tail[:done, :] = modes_a[...]
    high, low = split(both[: 3 * count, :] + both[3 * count :, :])
    tail[done : done + 3 * count, :] = high
    tail[done + 3 * count :, :] = low
    high, low = split(own)
    ahead_loads[...] = jnp.zeros_like(ahead_loads)
    ahead_loads[count : 2 * count, :] = dot(high, loads[...]) + dot(low, loads[...])


def merged_kernel(layout, swaps, sizes, ride, ready, modes_f, root_inverse, ahead, *more):
    halos, more = more[: len(swaps)], more[len(swaps) :]
    received, (message, faces, stack) = more[:-3], more[-3:]
    modes, height = ready.shape[0], faces.shape[0] // len(swaps)
    count = message.shape[0] - modes
    high, low = stack_halos(layout, swaps, sizes, halos, faces)
    both = jnp.dot(modes_f[: 2 * modes, :], high, preferred_element_type=F32)
    fine = jnp.dot(modes_f[:modes, :], low, preferred_element_type=F32)
    message[:modes, :] = ready[...] - (both[:modes, :] + (both[modes:, :] + fine))
    me = lax.axis_index("gx")
    stack[...] = jnp.zeros_like(stack)
    pieces = [(me, ahead)]
    for (dim, odd), halo in zip(swaps, halos):
        if ride and (dim, odd) == (0, 0):
            pieces.append((me ^ 1, halo.at[height:, :]))
    paired, single = far_offsets(sizes[0], 1 + ride)
    for offset, piece in zip([core_offset(pair) for pair in paired] + single, received):
        pieces.append((source(me, offset, sizes[0]), piece))
    for index, piece in pieces:
        rows = pl.ds(pl.multiple_of(index * count, count), 3 * count)
        stack[rows, :] += piece[...]
    message[modes:, :] = dot3(root_inverse[...], stack[count:-count, :])


def sum_kernel(own, other, total):
    total[...] = own[...] + other[other.shape[0] - own.shape[0] :, :]


def root_kernel(count, coarse, root_inverse, root, *more):
    received, (message, stack) = more[:-2], more[-2:]
    modes, height = coarse.shape[0], root.shape[0]
    me = lax.axis_index("gx")
    paired, single = far_offsets(count, 1 + nearest(count))
    offsets = [core_offset(pair) for pair in paired] + list(range(1, 1 + nearest(count))) + single
    stack[...] = jnp.zeros_like(stack)
    stack[rows_of(me, height), :] = root[...]
    for offset, piece in zip(offsets, received):
        stack[rows_of(source(me, offset, count), height), :] = piece[...]
    message[:modes, :] = coarse[...]
    message[modes:, :] = dot3(root_inverse[...], stack[...])


def parts_kernel(members, sizes, region_rows, root_map, note, factors):
    modes, order = region_rows.shape
    count, lanes = root_map.shape[0], note.shape[1]
    other_map = note[:count, :modes]
    blocks = [slice(count + k * modes, count + (k + 1) * modes) for k in range(order // lanes)]
    other_rows = jnp.concatenate([note[rows, :] for rows in blocks], axis=1)
    y, z = lax.axis_index("gy"), lax.axis_index("gz")
    half = sizes[0] // 2
    depth = len(members) * modes
    row = lax.broadcasted_iota(jnp.int32, (order, depth), 0)
    column = lax.broadcasted_iota(jnp.int32, (order, depth), 1)
    wanted = jnp.full((order, depth), -1, jnp.int32)
    for k, (dy, dz) in enumerate(members):
        at_y = 2 * source(y // 2, dy, half) + (y + crossing(dy, dz)) % 2
        first = (at_y * sizes[1] + source(z, dz, sizes[1])) * modes
        inside = jnp.logical_and(column >= k * modes, column < (k + 1) * modes)
        wanted = jnp.where(inside, first + column - k * modes, wanted)
    chosen = jnp.where(row == wanted, 1.0, 0.0).astype(BF16)
    for at, (whole, maps) in enumerate(((region_rows[...], root_map[...]), (other_rows, other_map))):
        for level, piece in enumerate(split(whole)):
            rows = slice((2 * level + at) * modes, (2 * level + at + 1) * modes)
            factors[rows, :depth] = jnp.dot(piece, chosen, preferred_element_type=F32).astype(BF16)
        for level, piece in enumerate(split(maps.T)):
            rows = slice((2 * level + at) * modes, (2 * level + at + 1) * modes)
            factors[rows, depth:] = piece


def pair_kernel(modes, factors, first, *more):
    received, (own, out, tall) = more[:-3], more[-3:]
    total = first[modes:, :]
    tall[:modes, :] = first[:modes, :]
    for k, piece in enumerate(received, 1):
        tall[k * modes : (k + 1) * modes, :] = piece[:modes, :]
        total = total + piece[modes:, :]
    tall[(len(received) + 1) * modes :, :] = total
    high, low = split(tall[...])
    both = jnp.dot(factors[...], high, preferred_element_type=F32)
    fine = jnp.dot(factors[: 2 * modes, :], low, preferred_element_type=F32)
    total = both[: 2 * modes, :] + (both[2 * modes :, :] + fine)
    own[...] = total[:modes, :]
    out[...] = total[modes:, :]


def correction_factor(amplitude):
    high, low = split(amplitude)
    return jnp.concatenate([high, high, low], axis=0)


def middle_kernel(
    swaps, base, modes_t, own, other, matrix_f, tail, modes_b, ahead_loads,
    next_solution, placed, ready, ahead, *messages
):
    height = placed.shape[0] // FACES
    tall = correction_factor(own[...] + other[...])
    next_solution[...] = base[...] + jnp.dot(modes_t[...], tall, preferred_element_type=F32)
    local_iter = next_solution[...].astype(BF16)
    placed[...] = jnp.dot(matrix_f[...], local_iter, preferred_element_type=F32)
    more = jnp.dot(tail[...], local_iter, preferred_element_type=F32)
    modes, count = ready.shape[0], ahead.shape[0]
    ready[...] = modes_b[...] - (more[:modes, :] + more[modes : 2 * modes, :])
    more = more[2 * modes :, :]
    ahead[...] = ahead_loads[...] - (more[:count, :] + more[count:, :])
    send_faces(swaps, placed, messages)
    for message in messages:
        if message.shape[0] > height:
            message[height:, :] = ahead[...]


def last_kernel(base, modes_t, own, other, out, result, sems):
    tall = correction_factor(own[...] + other[...])
    parts = sems.shape[0]
    part = result.shape[0] // parts
    copies = []
    for k in range(parts):
        rows = slice(k * part, (k + 1) * part)
        result[rows, :] = base[rows, :] + jnp.dot(modes_t[rows, :], tall, preferred_element_type=F32)
        copies.append(pltpu.make_async_copy(result.at[rows, :], out.at[rows, :], sems.at[k]))
        copies[-1].start()
    for copy in copies:
        copy.wait()


def per_device(
    loads,
    start,
    interface_op,
    block_order,
    interface_weights,
    coarse_modes,
    region_weights,
    region_inverse,
    root_inverse,
):
    sizes = tuple(lax.axis_size(axis) for axis in AXES)
    iface = interface_op.shape[-1]
    cases = loads.shape[-1]
    height = iface // FACES
    matrix = interface_op.reshape(iface, iface)
    order = block_order.reshape(1, FACES)
    weights = interface_weights.reshape(1, iface)
    modes = coarse_modes.reshape(coarse_modes.shape[-2], iface)
    mode_count = modes.shape[0]
    root_map = region_weights.reshape(mode_count, region_weights.shape[-1]).T
    root_modes = root_map.shape[0]
    region_rows = region_inverse.reshape(mode_count, region_inverse.shape[-1])
    target = loads.reshape(iface, cases)
    solution = start.reshape(iface, cases)

    swaps = swap_list(sizes, FIRST_ORDER)
    later = swap_list(sizes, LATER_ORDER)
    half = sizes[1] // 2
    members = list(itertools.product(range(half), range(sizes[2])))

    ride = nearest(sizes[0])
    paired, single = far_offsets(sizes[0], 1 + ride)
    core = later.index((1, 0))
    full = (pltpu.VMEM, (iface, cases), F32)
    places = [pltpu.SMEM((1, FACES), jnp.int32)]
    faces = [pltpu.VMEM((len(swaps) * height, cases), F32)]

    def wide(rows, dtype=BF16):
        return (pltpu.VMEM, (rows, iface), dtype)

    def held(rows):
        return (pltpu.VMEM, (rows, cases), F32)

    def along(value, offset):
        pairs = []
        for place in itertools.product(*map(range, sizes)):
            step = offset if isinstance(offset, int) else offset[place[1] % 2]
            there = (partner(place[0], step, sizes[0]), place[1], place[2])
            pairs.append((flat(sizes, place), flat(sizes, there)))
        return lax.ppermute(value, AXES, pairs)

    def exchange(messages, order):
        return [
            lax.ppermute(message, AXES, swap_pairs(sizes, dim, odd)) for (dim, odd), message in zip(order, messages)
        ]

    def core_sum(own, other):
        return call(sum_kernel, [held(own.shape[0])], [own, other], "core_sum")[0]

    def base_of(order, solution, placed, halos):
        return call(
            functools.partial(base_kernel, order, sizes),
            [full],
            [solution, target, placed, scale] + halos,
            "base",
        )[0]

    for step in range(ITERS):
        if step == 0:
            inputs = [order, solution, matrix, modes, root_map]
            matrix, modes, root_map, placed, *messages = call(
                functools.partial(first_kernel, swaps),
                [(pltpu.VMEM, item.shape, item.dtype) for item in inputs[2:]]
                + [full]
                + [held(height + root_modes * height // cases)] * len(swaps),
                inputs,
                "first_product",
                places
                + [pltpu.VMEM((iface, cases), BF16)] * 2
                + [pltpu.VMEM((root_modes, iface), F32), pltpu.SemaphoreType.DMA((5,))],
                len(inputs),
            )
            modes_t, scale, modes_f, matrix_f, modes_a, modes_b, ready = call(
                functools.partial(constants_kernel, swaps, sizes),
                [
                    (pltpu.VMEM, (iface, 3 * mode_count), BF16),
                    (pltpu.VMEM, (iface, height), F32),
                    (pltpu.VMEM, (2 * mode_count + 2 * root_modes, len(swaps) * height), BF16),
                    wide(iface),
                    wide(2 * mode_count),
                    held(mode_count),
                    held(mode_count + root_modes),
                ],
                [order, matrix, modes, root_map, weights, target, placed],
                "constants",
                [pltpu.VMEM((iface, iface), BF16)] + places + [pltpu.SemaphoreType.DMA],
                1,
            )
            halos = exchange(messages, swaps)
            blocks = region_rows.shape[1] // cases
            coarse, root, note = call(
                functools.partial(coarse_kernel, swaps, sizes),
                [held(mode_count), held(root_modes), held(2 * root_modes + mode_count * blocks)],
                [ready, modes_f, region_rows, root_map] + halos,
                "coarse",
                faces,
            )
            note = lax.ppermute(note, AXES, swap_pairs(sizes, 1, 0))
            both = core_sum(root, note)
            received = [along(root, offset) for offset in list(range(1, 1 + ride)) + single]
            received = [along(both, pair) for pair in paired] + received
            (factors,) = call(
                functools.partial(parts_kernel, members, sizes[1:]),
                [(pltpu.VMEM, (4 * mode_count, len(members) * mode_count + root_modes), BF16)],
                [region_rows, root_map, note],
                "parts",
            )
            base = base_of(swaps, solution, placed, halos)
            tail, ahead_loads = call(
                functools.partial(links_kernel, swaps, sizes),
                [wide(2 * mode_count + 6 * root_modes), held(3 * root_modes)],
                [modes, root_map, target, matrix_f, modes_a] + halos,
                "links",
                [pltpu.VMEM((3 * root_modes, iface), F32)],
            )
            (message,) = call(
                functools.partial(root_kernel, sizes[0]),
                [held(mode_count + root_modes)],
                [coarse, root_inverse, root] + received,
                "root_part",
                [pltpu.VMEM((root_inverse.shape[1], cases), F32)],
            )
        else:
            extra = [3 * root_modes * int(swap == (1, 0) or (ride and swap == (0, 0))) for swap in later]
            solution, placed, ready, ahead, *messages = call(
                functools.partial(middle_kernel, later),
                [full, full, held(mode_count), held(3 * root_modes)] + [held(height + more) for more in extra],
                [base, modes_t, own, other, matrix_f, tail, modes_b, ahead_loads],
                "update_product",
            )
            halos = exchange(messages, later)
            both = core_sum(ahead, halos[core])
            received = [along(both, pair) for pair in paired] + [along(ahead, offset) for offset in single]
            (message,) = call(
                functools.partial(merged_kernel, swaps, later, sizes, ride),
                [held(mode_count + root_modes)],
                [ready, modes_f, root_inverse, ahead] + halos + received,
                "coarse_root",
                faces + [pltpu.VMEM((root_inverse.shape[1] + 2 * root_modes, cases), F32)],
            )
            base = base_of(later, solution, placed, halos)
        pieces = []
        for dy, dz in members[1:]:
            moves = []
            for place in itertools.product(*map(range, sizes)):
                x, y, z = place
                at_y = 2 * partner(y // 2, dy, half) + (y + crossing(dy, dz)) % 2
                moves.append((flat(sizes, place), flat(sizes, (x, at_y, partner(z, dz, sizes[2])))))
            pieces.append(lax.ppermute(message, AXES, moves))
        own, given = call(
            functools.partial(pair_kernel, mode_count),
            [held(mode_count), held(mode_count)],
            [factors, message] + pieces,
            "amplitude_parts",
            [pltpu.VMEM((len(members) * mode_count + root_modes, cases), F32)],
        )
        other = lax.ppermute(given, AXES, swap_pairs(sizes, 1, 0))
    (solution,) = call(
        last_kernel,
        [(jax.ShapeDtypeStruct, (iface, cases), F32)],
        [base, modes_t, own, other],
        "update_last",
        [pltpu.VMEM((iface, cases), F32), pltpu.SemaphoreType.DMA((4,))],
    )
    return solution.reshape(1, 1, 1, iface, cases)


def solution(mesh):
    placed = (
        P("gx", "gy", "gz", None, None),
        P("gx", "gy", "gz", None, None),
        P("gx", "gy", "gz", None, None),
        P("gx", "gy", "gz", None),
        P("gx", "gy", "gz", None),
        P("gx", "gy", "gz", None, None),
        P("gx", "gy", "gz", None, None),
        P("gx", ("gy", "gz"), None),
        P("gx", None),
    )
    return jax.shard_map(
        per_device,
        mesh=mesh,
        in_specs=placed,
        out_specs=P("gx", "gy", "gz", None, None),
        check_vma=False,
    )
```

```python
import functools
import itertools

import jax
import jax.numpy as jnp
from jax import lax
from jax.experimental import pallas as pl
from jax.experimental.pallas import tpu as pltpu
from jax.sharding import PartitionSpec as P

ITERS = 2
FACES = 8
AXES = ("gx", "gy", "gz")
FIRST_ORDER = ((0, 0), (2, 1), (2, 0), (1, 1), (0, 1), (1, 0))
LATER_ORDER = ((1, 0), (0, 0), (0, 1), (2, 1), (2, 0), (1, 1))
F32 = jnp.float32
BF16 = jnp.bfloat16
ROWS = (((1,), (0,)), ((), ()))
COLS = (((0,), (0,)), ((), ()))


def neighbour(index, count, odd):
    other = index + 1 if index % 2 == odd else index - 1
    return other if 0 <= other < count else None


def swap_list(sizes, wanted):
    return [swap for swap in wanted if sizes[swap[0]] > 1 + swap[1]]


def flat(sizes, place):
    return (place[0] * sizes[1] + place[1]) * sizes[2] + place[2]


def swap_pairs(sizes, dim, odd):
    pairs = []
    for place in itertools.product(*map(range, sizes)):
        there = list(place)
        other = neighbour(place[dim], sizes[dim], odd)
        if other is not None:
            there[dim] = other
        elif odd and sizes[dim] % 2 == 0:
            if dim == 1:
                there[1] = sizes[1] - 1 - place[1]
            elif sizes[1] % 2 == 0:
                there[1] = place[1] ^ 1
        if tuple(there) != place:
            pairs.append((flat(sizes, place), flat(sizes, there)))
    return pairs


def swap_face(dim, odd):
    high = (lax.axis_index(AXES[dim]) + odd + 1) % 2
    return 2 * dim + high


def has_neighbour(dim, face, sizes):
    other = lax.axis_index(AXES[dim]) + 2 * (face - 2 * dim) - 1
    return jnp.logical_and(other >= 0, other < sizes[dim])


def partner(index, offset, count):
    if count & (count - 1):
        return (index + offset) % count
    return index ^ offset


def source(index, offset, count):
    if count & (count - 1):
        return lax.rem(index + count - offset, count)
    return index ^ offset


def nearest(count):
    return int(count & (count - 1) == 0)


def far_offsets(count, near):
    offsets = list(range(near, count))
    paired = list(zip(offsets[0::2], offsets[1::2]))
    return paired, offsets[2 * len(paired) :]


def core_offset(pair):
    return jnp.where(lax.axis_index("gy") % 2 == 0, pair[0], pair[1])


def crossing(dy, dz):
    return int(dy != 0 or dz != 0)


def split(value):
    high = value.astype(BF16)
    return high, (value - high.astype(F32)).astype(BF16)


def dot3(left, right, dims=ROWS):
    left_high, left_low = split(left)
    right_high, right_low = split(right)
    dot = functools.partial(lax.dot_general, dimension_numbers=dims, preferred_element_type=F32)
    return dot(left_high, right_high) + (dot(left_low, right_high) + dot(left_high, right_low))


def call(body, outs, ins, name, scratch=(), fixed=0):
    spaces = [pltpu.HBM] * fixed + [pltpu.VMEM] * (len(ins) - fixed)
    return pl.pallas_call(
        body,
        out_shape=[item(shape, dtype) for item, shape, dtype in outs],
        in_specs=[pl.BlockSpec(memory_space=space) for space in spaces],
        out_specs=[
            pl.BlockSpec(memory_space=pltpu.HBM if item is jax.ShapeDtypeStruct else pltpu.VMEM)
            for item, _, _ in outs
        ],
        scratch_shapes=list(scratch),
        compiler_params=pltpu.CompilerParams(vmem_limit_bytes=8 * 1024 * 1024),
        name=name,
    )(*[pltpu.with_memory_space_constraint(item, space) for item, space in zip(ins, spaces)])


def rows_of(index, height):
    return pl.ds(pl.multiple_of(index * height, height), height)


def send_faces(swaps, placed, messages):
    height = placed.shape[0] // FACES
    for (dim, odd), message in zip(swaps, messages):
        message[:height, :] = placed[rows_of(swap_face(dim, odd), height), :]


def first_kernel(swaps, order_hbm, start_hbm, *refs):
    hbm, held, (placed, *more) = refs[:3], refs[3:6], refs[6:]
    matrix, modes, root_map = held
    messages, (order, start, local_iter, mapped, sems) = more[: len(swaps)], more[len(swaps) :]
    pairs = [(order_hbm, order), (start_hbm, start)] + list(zip(hbm, held))
    copies = [pltpu.make_async_copy(*pair, sems.at[k]) for k, pair in enumerate(pairs)]
    for copy in copies:
        copy.start()
    height, lanes = placed.shape[0] // FACES, placed.shape[1]
    copies[0].wait()
    copies[1].wait()
    for j in range(FACES):
        local_iter[j * height : (j + 1) * height, :] = start[rows_of(order[0, j], height), :]
    copies[3].wait()
    copies[4].wait()
    mapped[...] = dot3(root_map[...], modes[...])
    for (dim, odd), message in zip(swaps, messages):
        link = mapped[:, rows_of(swap_face(dim, odd), height)]
        extra = link.shape[0] * height // lanes
        end = height + extra
        for k in range(lanes // height):
            message[height:end, k * height : (k + 1) * height] = link[k * extra : (k + 1) * extra, :]
    copies[2].wait()
    product = jnp.dot(matrix[...], local_iter[...], preferred_element_type=F32)
    for j in range(FACES):
        placed[rows_of(order[0, j], height), :] = product[j * height : (j + 1) * height, :]
    send_faces(swaps, placed, messages)


def constants_kernel(
    swaps, sizes, order_hbm, matrix, modes, root_map, weights, loads, placed,
    modes_t, scale, modes_f, matrix_f, modes_a, modes_b, ready, wide, order, sem
):
    copy = pltpu.make_async_copy(order_hbm, order, sem)
    copy.start()
    count, height = modes.shape[0], scale.shape[1]
    high, low = split(modes[...])
    modes_t[...] = jnp.concatenate([high.T, low.T, high.T], axis=1)
    for j in range(FACES):
        block = slice(j * height, (j + 1) * height)
        scale[block, :] = jnp.broadcast_to(weights[:, block], (height, height)).T
    for at, (dim, odd) in enumerate(swaps):
        face = swap_face(dim, odd)
        columns = modes[:, rows_of(face, height)]
        columns = jnp.where(has_neighbour(dim, face, sizes), columns, 0.0)
        block = slice(at * height, (at + 1) * height)
        modes_f[:count, block], modes_f[count : 2 * count, block] = split(columns)
        rows = root_map.shape[0]
        parts = split(dot3(root_map[...], columns))
        modes_f[2 * count : 2 * count + rows, block], modes_f[2 * count + rows :, block] = parts
    dot = functools.partial(jnp.dot, preferred_element_type=F32)
    modes_b[...] = dot(high, loads[...]) + dot(low, loads[...])
    ready[:count, :] = modes_b[...] - dot3(modes[...], placed[...])
    ready[count:, :] = dot3(root_map[...], ready[:count, :])
    copy.wait()
    for j in range(FACES):
        block = slice(j * height, (j + 1) * height)
        wide[:, rows_of(order[0, j], height)] = matrix[:, block]
    for j in range(FACES):
        block = slice(j * height, (j + 1) * height)
        matrix_f[rows_of(order[0, j], height), :] = wide[block, :]
    modes_a[:count, :], modes_a[count:, :] = split(dot(high, matrix_f[...]) + dot(low, matrix_f[...]))


def stack_halos(layout, swaps, sizes, halos, stack):
    height = stack.shape[0] // len(swaps)
    for (dim, odd), halo in zip(swaps, halos):
        at = layout.index((dim, odd))
        known = has_neighbour(dim, swap_face(dim, odd), sizes)
        stack[at * height : (at + 1) * height, :] = jnp.where(known, halo[:height, :], 0.0)
    return split(stack[...])


def coarse_kernel(swaps, sizes, ready, modes_f, region_rows, root_map, *more):
    halos, (coarse, root, note, stack) = more[: len(swaps)], more[len(swaps) :]
    modes, count = coarse.shape[0], root.shape[0]
    high, low = stack_halos(swaps, swaps, sizes, halos, stack)
    both = jnp.dot(modes_f[...], high, preferred_element_type=F32)
    fine = jnp.dot(modes_f[: 2 * modes + count, :], low, preferred_element_type=F32)
    coarse[...] = ready[:modes, :] - (both[:modes, :] + (both[modes : 2 * modes, :] + fine[:modes, :]))
    at = 2 * modes
    root[...] = ready[modes:, :] - (both[at : at + count, :] + (both[at + count :, :] + fine[at:, :]))
    lanes = root.shape[1]
    note[:count, :] = jnp.zeros_like(root)
    note[:count, :modes] = root_map[...]
    for k in range(region_rows.shape[1] // lanes):
        rows = slice(count + k * modes, count + (k + 1) * modes)
        note[rows, :] = region_rows[:, k * lanes : (k + 1) * lanes]
    note[-count:, :] = root[...]


def base_kernel(swaps, sizes, solution, loads, placed, scale, *more):
    halos, base = more[: len(swaps)], more[-1]
    height, lanes = scale.shape[1], placed.shape[1]

    def wide(rows):
        return jnp.concatenate([scale[rows, :]] * (lanes // height), axis=1)

    for j in range(FACES):
        rows = slice(j * height, (j + 1) * height)
        rest = loads[rows, :].astype(F32) - placed[rows, :]
        base[rows, :] = solution[rows, :].astype(F32) + wide(rows) * rest
    for (dim, odd), halo in zip(swaps, halos):
        face = swap_face(dim, odd)
        rows = rows_of(face, height)

        @pl.when(has_neighbour(dim, face, sizes))
        def _():
            base[rows, :] -= wide(rows) * halo[:height, :]


def links_kernel(swaps, sizes, modes, root_map, loads, matrix_f, modes_a, *more):
    halos, (tail, ahead_loads, ahead) = more[: len(swaps)], more[len(swaps) :]
    count, height = root_map.shape[0], loads.shape[0] // FACES
    lanes = loads.shape[1]
    ahead[...] = jnp.zeros_like(ahead)
    own = dot3(root_map[...], modes[...])
    ahead[count : 2 * count, :] = own
    for (dim, odd), halo in zip(swaps, halos):
        face = swap_face(dim, odd)
        known = has_neighbour(dim, face, sizes)
        end = height + count * height // lanes
        pieces = [halo[height:end, k * height : (k + 1) * height] for k in range(lanes // height)]
        link = jnp.where(known, jnp.concatenate(pieces, axis=0), 0.0)
        if dim == 0:
            ahead[rows_of(2 * face, count), rows_of(face, height)] = link
        else:
            ahead[count : 2 * count, rows_of(face, height)] += link
    dot = functools.partial(jnp.dot, preferred_element_type=F32)
    high, low = split(ahead[...])
    both = dot(jnp.concatenate([high, low], axis=0), matrix_f[...])
    done = modes_a.shape[0]
    tail[:done, :] = modes_a[...]
    high, low = split(both[: 3 * count, :] + both[3 * count :, :])
    tail[done : done + 3 * count, :] = high
    tail[done + 3 * count :, :] = low
    high, low = split(own)
    ahead_loads[...] = jnp.zeros_like(ahead_loads)
    ahead_loads[count : 2 * count, :] = dot(high, loads[...]) + dot(low, loads[...])


def merged_kernel(layout, swaps, sizes, ride, ready, modes_f, root_inverse, ahead, *more):
    halos, more = more[: len(swaps)], more[len(swaps) :]
    received, (message, faces, stack) = more[:-3], more[-3:]
    modes, height = ready.shape[0], faces.shape[0] // len(swaps)
    count = message.shape[0] - modes
    high, low = stack_halos(layout, swaps, sizes, halos, faces)
    both = jnp.dot(modes_f[: 2 * modes, :], high, preferred_element_type=F32)
    fine = jnp.dot(modes_f[:modes, :], low, preferred_element_type=F32)
    message[:modes, :] = ready[...] - (both[:modes, :] + (both[modes:, :] + fine))
    me = lax.axis_index("gx")
    stack[...] = jnp.zeros_like(stack)
    pieces = [(me, ahead)]
    for (dim, odd), halo in zip(swaps, halos):
        if ride and (dim, odd) == (0, 0):
            pieces.append((me ^ 1, halo.at[height:, :]))
    paired, single = far_offsets(sizes[0], 1 + ride)
    for offset, piece in zip([core_offset(pair) for pair in paired] + single, received):
        pieces.append((source(me, offset, sizes[0]), piece))
    for index, piece in pieces:
        rows = pl.ds(pl.multiple_of(index * count, count), 3 * count)
        stack[rows, :] += piece[...]
    message[modes:, :] = dot3(root_inverse[...], stack[count:-count, :])


def sum_kernel(own, other, total):
    total[...] = own[...] + other[other.shape[0] - own.shape[0] :, :]


def root_kernel(count, pieces, coarse, root_inverse, root, *more):
    received, (message, stack) = more[:pieces], more[-2:]
    modes, height = coarse.shape[0], root.shape[0]
    me = lax.axis_index("gx")
    paired, single = far_offsets(count, 1 + nearest(count))
    offsets = [core_offset(pair) for pair in paired] + list(range(1, 1 + nearest(count))) + single
    stack[...] = jnp.zeros_like(stack)
    stack[rows_of(me, height), :] = root[...]
    for offset, piece in zip(offsets, received):
        stack[rows_of(source(me, offset, count), height), :] = piece[...]
    message[:modes, :] = coarse[...]
    message[modes:, :] = dot3(root_inverse[...], stack[...])


def parts_kernel(members, sizes, region_rows, root_map, note, factors):
    modes, order = region_rows.shape
    count, lanes = root_map.shape[0], note.shape[1]
    other_map = note[:count, :modes]
    blocks = [slice(count + k * modes, count + (k + 1) * modes) for k in range(order // lanes)]
    other_rows = jnp.concatenate([note[rows, :] for rows in blocks], axis=1)
    y, z = lax.axis_index("gy"), lax.axis_index("gz")
    half = sizes[0] // 2
    depth = len(members) * modes
    row = lax.broadcasted_iota(jnp.int32, (order, depth), 0)
    column = lax.broadcasted_iota(jnp.int32, (order, depth), 1)
    wanted = jnp.full((order, depth), -1, jnp.int32)
    for k, (dy, dz) in enumerate(members):
        at_y = 2 * source(y // 2, dy, half) + (y + crossing(dy, dz)) % 2
        first = (at_y * sizes[1] + source(z, dz, sizes[1])) * modes
        inside = jnp.logical_and(column >= k * modes, column < (k + 1) * modes)
        wanted = jnp.where(inside, first + column - k * modes, wanted)
    chosen = jnp.where(row == wanted, 1.0, 0.0).astype(BF16)
    for at, (whole, maps) in enumerate(((region_rows[...], root_map[...]), (other_rows, other_map))):
        for level, piece in enumerate(split(whole)):
            rows = slice((2 * level + at) * modes, (2 * level + at + 1) * modes)
            factors[rows, :depth] = jnp.dot(piece, chosen, preferred_element_type=F32).astype(BF16)
        for level, piece in enumerate(split(maps.T)):
            rows = slice((2 * level + at) * modes, (2 * level + at + 1) * modes)
            factors[rows, depth:] = piece


def pair_kernel(modes, factors, first, *more):
    received, (own, out, tall) = more[:-3], more[-3:]
    total = first[modes:, :]
    tall[:modes, :] = first[:modes, :]
    for k, piece in enumerate(received, 1):
        tall[k * modes : (k + 1) * modes, :] = piece[:modes, :]
        total = total + piece[modes:, :]
    tall[(len(received) + 1) * modes :, :] = total
    high, low = split(tall[...])
    both = jnp.dot(factors[...], high, preferred_element_type=F32)
    fine = jnp.dot(factors[: 2 * modes, :], low, preferred_element_type=F32)
    total = both[: 2 * modes, :] + (both[2 * modes :, :] + fine)
    own[...] = total[:modes, :]
    out[...] = total[modes:, :]


def correction_factor(amplitude):
    high, low = split(amplitude)
    return jnp.concatenate([high, high, low], axis=0)


def middle_kernel(
    swaps, base, modes_t, own, other, matrix_f, tail, modes_b, ahead_loads,
    next_solution, placed, ready, ahead, *messages
):
    height = placed.shape[0] // FACES
    tall = correction_factor(own[...] + other[...])
    next_solution[...] = base[...] + jnp.dot(modes_t[...], tall, preferred_element_type=F32)
    local_iter = next_solution[...].astype(BF16)
    placed[...] = jnp.dot(matrix_f[...], local_iter, preferred_element_type=F32)
    more = jnp.dot(tail[...], local_iter, preferred_element_type=F32)
    modes, count = ready.shape[0], ahead.shape[0]
    ready[...] = modes_b[...] - (more[:modes, :] + more[modes : 2 * modes, :])
    more = more[2 * modes :, :]
    ahead[...] = ahead_loads[...] - (more[:count, :] + more[count:, :])
    send_faces(swaps, placed, messages)
    for message in messages:
        if message.shape[0] > height:
            message[height:, :] = ahead[...]


def last_kernel(base, modes_t, own, other, out, result, sems):
    tall = correction_factor(own[...] + other[...])
    parts = sems.shape[0]
    part = result.shape[0] // parts
    copies = []
    for k in range(parts):
        rows = slice(k * part, (k + 1) * part)
        result[rows, :] = base[rows, :] + jnp.dot(modes_t[rows, :], tall, preferred_element_type=F32)
        copies.append(pltpu.make_async_copy(result.at[rows, :], out.at[rows, :], sems.at[k]))
        copies[-1].start()
    for copy in copies:
        copy.wait()


def per_device(
    loads,
    start,
    interface_op,
    block_order,
    interface_weights,
    coarse_modes,
    region_weights,
    region_inverse,
    root_inverse,
):
    sizes = tuple(lax.axis_size(axis) for axis in AXES)
    iface = interface_op.shape[-1]
    cases = loads.shape[-1]
    height = iface // FACES
    matrix = interface_op.reshape(iface, iface)
    order = block_order.reshape(1, FACES)
    weights = interface_weights.reshape(1, iface)
    modes = coarse_modes.reshape(coarse_modes.shape[-2], iface)
    mode_count = modes.shape[0]
    root_map = region_weights.reshape(mode_count, region_weights.shape[-1]).T
    root_modes = root_map.shape[0]
    region_rows = region_inverse.reshape(mode_count, region_inverse.shape[-1])
    target = loads.reshape(iface, cases)
    solution = start.reshape(iface, cases)

    swaps = swap_list(sizes, FIRST_ORDER)
    later = swap_list(sizes, LATER_ORDER)
    half = sizes[1] // 2
    members = list(itertools.product(range(half), range(sizes[2])))

    ride = nearest(sizes[0])
    paired, single = far_offsets(sizes[0], 1 + ride)
    core = later.index((1, 0))
    full = (pltpu.VMEM, (iface, cases), F32)
    places = [pltpu.SMEM((1, FACES), jnp.int32)]
    faces = [pltpu.VMEM((len(swaps) * height, cases), F32)]

    def wide(rows, dtype=BF16):
        return (pltpu.VMEM, (rows, iface), dtype)

    def held(rows):
        return (pltpu.VMEM, (rows, cases), F32)

    def along(value, offset):
        pairs = []
        for place in itertools.product(*map(range, sizes)):
            step = offset if isinstance(offset, int) else offset[place[1] % 2]
            there = (partner(place[0], step, sizes[0]), place[1], place[2])
            pairs.append((flat(sizes, place), flat(sizes, there)))
        return lax.ppermute(value, AXES, pairs)

    def exchange(messages, order):
        return [
            lax.ppermute(message, AXES, swap_pairs(sizes, dim, odd)) for (dim, odd), message in zip(order, messages)
        ]

    def core_sum(own, other):
        return call(sum_kernel, [held(own.shape[0])], [own, other], "core_sum")[0]

    def base_of(order, solution, placed, halos):
        return call(
            functools.partial(base_kernel, order, sizes),
            [full],
            [solution, target, placed, scale] + halos,
            "base",
        )[0]

    for step in range(ITERS):
        if step == 0:
            inputs = [order, solution, matrix, modes, root_map]
            matrix, modes, root_map, placed, *messages = call(
                functools.partial(first_kernel, swaps),
                [(pltpu.VMEM, item.shape, item.dtype) for item in inputs[2:]]
                + [full]
                + [held(height + root_modes * height // cases)] * len(swaps),
                inputs,
                "first_product",
                places
                + [pltpu.VMEM((iface, cases), BF16)] * 2
                + [pltpu.VMEM((root_modes, iface), F32), pltpu.SemaphoreType.DMA((5,))],
                len(inputs),
            )
            modes_t, scale, modes_f, matrix_f, modes_a, modes_b, ready = call(
                functools.partial(constants_kernel, swaps, sizes),
                [
                    (pltpu.VMEM, (iface, 3 * mode_count), BF16),
                    (pltpu.VMEM, (iface, height), F32),
                    (pltpu.VMEM, (2 * mode_count + 2 * root_modes, len(swaps) * height), BF16),
                    wide(iface),
                    wide(2 * mode_count),
                    held(mode_count),
                    held(mode_count + root_modes),
                ],
                [order, matrix, modes, root_map, weights, target, placed],
                "constants",
                [pltpu.VMEM((iface, iface), BF16)] + places + [pltpu.SemaphoreType.DMA],
                1,
            )
            halos = exchange(messages, swaps)
            blocks = region_rows.shape[1] // cases
            coarse, root, note = call(
                functools.partial(coarse_kernel, swaps, sizes),
                [held(mode_count), held(root_modes), held(2 * root_modes + mode_count * blocks)],
                [ready, modes_f, region_rows, root_map] + halos,
                "coarse",
                faces,
            )
            note = lax.ppermute(note, AXES, swap_pairs(sizes, 1, 0))
            both = core_sum(root, note)
            received = [along(root, offset) for offset in list(range(1, 1 + ride)) + single]
            received = [along(both, pair) for pair in paired] + received
            (factors,) = call(
                functools.partial(parts_kernel, members, sizes[1:]),
                [(pltpu.VMEM, (4 * mode_count, len(members) * mode_count + root_modes), BF16)],
                [region_rows, root_map, note],
                "parts",
            )
            base = base_of(swaps, solution, placed, halos)
            tail, ahead_loads = call(
                functools.partial(links_kernel, swaps, sizes),
                [wide(2 * mode_count + 6 * root_modes), held(3 * root_modes)],
                [modes, root_map, target, matrix_f, modes_a] + halos,
                "links",
                [pltpu.VMEM((3 * root_modes, iface), F32)],
            )
            (message,) = call(
                functools.partial(root_kernel, sizes[0], len(received)),
                [held(mode_count + root_modes)],
                [coarse, root_inverse, root] + received + [ahead_loads],
                "root_part",
                [pltpu.VMEM((root_inverse.shape[1], cases), F32)],
            )
        else:
            extra = [3 * root_modes * int(swap == (1, 0) or (ride and swap == (0, 0))) for swap in later]
            solution, placed, ready, ahead, *messages = call(
                functools.partial(middle_kernel, later),
                [full, full, held(mode_count), held(3 * root_modes)] + [held(height + more) for more in extra],
                [base, modes_t, own, other, matrix_f, tail, modes_b, ahead_loads],
                "update_product",
            )
            halos = exchange(messages, later)
            both = core_sum(ahead, halos[core])
            received = [along(both, pair) for pair in paired] + [along(ahead, offset) for offset in single]
            (message,) = call(
                functools.partial(merged_kernel, swaps, later, sizes, ride),
                [held(mode_count + root_modes)],
                [ready, modes_f, root_inverse, ahead] + halos + received,
                "coarse_root",
                faces + [pltpu.VMEM((root_inverse.shape[1] + 2 * root_modes, cases), F32)],
            )
            base = base_of(later, solution, placed, halos)
        pieces = []
        for dy, dz in members[1:]:
            moves = []
            for place in itertools.product(*map(range, sizes)):
                x, y, z = place
                at_y = 2 * partner(y // 2, dy, half) + (y + crossing(dy, dz)) % 2
                moves.append((flat(sizes, place), flat(sizes, (x, at_y, partner(z, dz, sizes[2])))))
            pieces.append(lax.ppermute(message, AXES, moves))
        own, given = call(
            functools.partial(pair_kernel, mode_count),
            [held(mode_count), held(mode_count)],
            [factors, message] + pieces,
            "amplitude_parts",
            [pltpu.VMEM((len(members) * mode_count + root_modes, cases), F32)],
        )
        other = lax.ppermute(given, AXES, swap_pairs(sizes, 1, 0))
    (solution,) = call(
        last_kernel,
        [(jax.ShapeDtypeStruct, (iface, cases), F32)],
        [base, modes_t, own, other],
        "update_last",
        [pltpu.VMEM((iface, cases), F32), pltpu.SemaphoreType.DMA((4,))],
    )
    return solution.reshape(1, 1, 1, iface, cases)


def solution(mesh):
    placed = (
        P("gx", "gy", "gz", None, None),
        P("gx", "gy", "gz", None, None),
        P("gx", "gy", "gz", None, None),
        P("gx", "gy", "gz", None),
        P("gx", "gy", "gz", None),
        P("gx", "gy", "gz", None, None),
        P("gx", "gy", "gz", None, None),
        P("gx", ("gy", "gz"), None),
        P("gx", None),
    )
    return jax.shard_map(
        per_device,
        mesh=mesh,
        in_specs=placed,
        out_specs=P("gx", "gy", "gz", None, None),
        check_vma=False,
    )
```

```python
import functools
import itertools

import jax
import jax.numpy as jnp
from jax import lax
from jax.experimental import pallas as pl
from jax.experimental.pallas import tpu as pltpu
from jax.sharding import PartitionSpec as P

ITERS = 2
FACES = 8
AXES = ("gx", "gy", "gz")
FIRST_ORDER = ((0, 0), (2, 1), (2, 0), (1, 1), (0, 1), (1, 0))
LATER_ORDER = ((1, 0), (0, 0), (0, 1), (2, 1), (2, 0), (1, 1))
F32 = jnp.float32
BF16 = jnp.bfloat16
ROWS = (((1,), (0,)), ((), ()))
COLS = (((0,), (0,)), ((), ()))


def neighbour(index, count, odd):
    other = index + 1 if index % 2 == odd else index - 1
    return other if 0 <= other < count else None


def swap_list(sizes, wanted):
    return [swap for swap in wanted if sizes[swap[0]] > 1 + swap[1]]


def flat(sizes, place):
    return (place[0] * sizes[1] + place[1]) * sizes[2] + place[2]


def swap_pairs(sizes, dim, odd):
    pairs = []
    for place in itertools.product(*map(range, sizes)):
        there = list(place)
        other = neighbour(place[dim], sizes[dim], odd)
        if other is not None:
            there[dim] = other
        elif odd and sizes[dim] % 2 == 0:
            if dim == 1:
                there[1] = sizes[1] - 1 - place[1]
            elif sizes[1] % 2 == 0:
                there[1] = place[1] ^ 1
        if tuple(there) != place:
            pairs.append((flat(sizes, place), flat(sizes, there)))
    return pairs


def swap_face(dim, odd):
    high = (lax.axis_index(AXES[dim]) + odd + 1) % 2
    return 2 * dim + high


def has_neighbour(dim, face, sizes):
    other = lax.axis_index(AXES[dim]) + 2 * (face - 2 * dim) - 1
    return jnp.logical_and(other >= 0, other < sizes[dim])


def partner(index, offset, count):
    if count & (count - 1):
        return (index + offset) % count
    return index ^ offset


def source(index, offset, count):
    if count & (count - 1):
        return lax.rem(index + count - offset, count)
    return index ^ offset


def nearest(count):
    return int(count & (count - 1) == 0)


def far_offsets(count, near):
    offsets = list(range(near, count))
    paired = list(zip(offsets[0::2], offsets[1::2]))
    return paired, offsets[2 * len(paired) :]


def core_offset(pair):
    return jnp.where(lax.axis_index("gy") % 2 == 0, pair[0], pair[1])


def crossing(dy, dz):
    return int(dy != 0 or dz != 0)


def split(value):
    high = value.astype(BF16)
    return high, (value - high.astype(F32)).astype(BF16)


def dot3(left, right, dims=ROWS):
    left_high, left_low = split(left)
    right_high, right_low = split(right)
    dot = functools.partial(lax.dot_general, dimension_numbers=dims, preferred_element_type=F32)
    return dot(left_high, right_high) + (dot(left_low, right_high) + dot(left_high, right_low))


def call(body, outs, ins, name, scratch=(), fixed=0):
    spaces = [pltpu.HBM] * fixed + [pltpu.VMEM] * (len(ins) - fixed)
    return pl.pallas_call(
        body,
        out_shape=[item(shape, dtype) for item, shape, dtype in outs],
        in_specs=[pl.BlockSpec(memory_space=space) for space in spaces],
        out_specs=[
            pl.BlockSpec(memory_space=pltpu.HBM if item is jax.ShapeDtypeStruct else pltpu.VMEM)
            for item, _, _ in outs
        ],
        scratch_shapes=list(scratch),
        compiler_params=pltpu.CompilerParams(vmem_limit_bytes=8 * 1024 * 1024),
        name=name,
    )(*[pltpu.with_memory_space_constraint(item, space) for item, space in zip(ins, spaces)])


def rows_of(index, height):
    return pl.ds(pl.multiple_of(index * height, height), height)


def send_faces(swaps, placed, messages):
    height = placed.shape[0] // FACES
    for (dim, odd), message in zip(swaps, messages):
        message[:height, :] = placed[rows_of(swap_face(dim, odd), height), :]


def first_kernel(swaps, order_hbm, start_hbm, *refs):
    hbm, held, (placed, *more) = refs[:3], refs[3:6], refs[6:]
    matrix, modes, root_map = held
    messages, (order, start, local_iter, mapped, sems) = more[: len(swaps)], more[len(swaps) :]
    pairs = [(order_hbm, order), (start_hbm, start)] + list(zip(hbm, held))
    copies = [pltpu.make_async_copy(*pair, sems.at[k]) for k, pair in enumerate(pairs)]
    for k, copy in enumerate(copies):
        copy.start(priority=int(k == 2))
    height, lanes = placed.shape[0] // FACES, placed.shape[1]
    copies[0].wait()
    copies[1].wait()
    for j in range(FACES):
        local_iter[j * height : (j + 1) * height, :] = start[rows_of(order[0, j], height), :]
    copies[3].wait()
    copies[4].wait()
    mapped[...] = dot3(root_map[...], modes[...])
    for (dim, odd), message in zip(swaps, messages):
        link = mapped[:, rows_of(swap_face(dim, odd), height)]
        extra = link.shape[0] * height // lanes
        end = height + extra
        for k in range(lanes // height):
            message[height:end, k * height : (k + 1) * height] = link[k * extra : (k + 1) * extra, :]
    copies[2].wait()
    product = jnp.dot(matrix[...], local_iter[...], preferred_element_type=F32)
    for j in range(FACES):
        placed[rows_of(order[0, j], height), :] = product[j * height : (j + 1) * height, :]
    send_faces(swaps, placed, messages)


def constants_kernel(
    swaps, sizes, order_hbm, matrix, modes, root_map, weights, loads, placed,
    modes_t, scale, modes_f, matrix_f, modes_a, modes_b, ready, wide, order, sem
):
    copy = pltpu.make_async_copy(order_hbm, order, sem)
    copy.start()
    count, height = modes.shape[0], scale.shape[1]
    high, low = split(modes[...])
    modes_t[...] = jnp.concatenate([high.T, low.T, high.T], axis=1)
    for j in range(FACES):
        block = slice(j * height, (j + 1) * height)
        scale[block, :] = jnp.broadcast_to(weights[:, block], (height, height)).T
    for at, (dim, odd) in enumerate(swaps):
        face = swap_face(dim, odd)
        columns = modes[:, rows_of(face, height)]
        columns = jnp.where(has_neighbour(dim, face, sizes), columns, 0.0)
        block = slice(at * height, (at + 1) * height)
        modes_f[:count, block], modes_f[count : 2 * count, block] = split(columns)
        rows = root_map.shape[0]
        parts = split(dot3(root_map[...], columns))
        modes_f[2 * count : 2 * count + rows, block], modes_f[2 * count + rows :, block] = parts
    dot = functools.partial(jnp.dot, preferred_element_type=F32)
    modes_b[...] = dot(high, loads[...]) + dot(low, loads[...])
    ready[:count, :] = modes_b[...] - dot3(modes[...], placed[...])
    ready[count:, :] = dot3(root_map[...], ready[:count, :])
    copy.wait()
    for j in range(FACES):
        block = slice(j * height, (j + 1) * height)
        wide[:, rows_of(order[0, j], height)] = matrix[:, block]
    for j in range(FACES):
        block = slice(j * height, (j + 1) * height)
        matrix_f[rows_of(order[0, j], height), :] = wide[block, :]
    modes_a[:count, :], modes_a[count:, :] = split(dot(high, matrix_f[...]) + dot(low, matrix_f[...]))


def stack_halos(layout, swaps, sizes, halos, stack):
    height = stack.shape[0] // len(swaps)
    for (dim, odd), halo in zip(swaps, halos):
        at = layout.index((dim, odd))
        known = has_neighbour(dim, swap_face(dim, odd), sizes)
        stack[at * height : (at + 1) * height, :] = jnp.where(known, halo[:height, :], 0.0)
    return split(stack[...])


def coarse_kernel(swaps, sizes, ready, modes_f, region_rows, root_map, *more):
    halos, (coarse, root, note, stack) = more[: len(swaps)], more[len(swaps) :]
    modes, count = coarse.shape[0], root.shape[0]
    high, low = stack_halos(swaps, swaps, sizes, halos, stack)
    both = jnp.dot(modes_f[...], high, preferred_element_type=F32)
    fine = jnp.dot(modes_f[: 2 * modes + count, :], low, preferred_element_type=F32)
    coarse[...] = ready[:modes, :] - (both[:modes, :] + (both[modes : 2 * modes, :] + fine[:modes, :]))
    at = 2 * modes
    root[...] = ready[modes:, :] - (both[at : at + count, :] + (both[at + count :, :] + fine[at:, :]))
    lanes = root.shape[1]
    note[:count, :] = jnp.zeros_like(root)
    note[:count, :modes] = root_map[...]
    for k in range(region_rows.shape[1] // lanes):
        rows = slice(count + k * modes, count + (k + 1) * modes)
        note[rows, :] = region_rows[:, k * lanes : (k + 1) * lanes]
    note[-count:, :] = root[...]


def base_kernel(swaps, sizes, solution, loads, placed, scale, *more):
    halos, base = more[: len(swaps)], more[-1]
    height, lanes = scale.shape[1], placed.shape[1]

    def wide(rows):
        return jnp.concatenate([scale[rows, :]] * (lanes // height), axis=1)

    for j in range(FACES):
        rows = slice(j * height, (j + 1) * height)
        rest = loads[rows, :].astype(F32) - placed[rows, :]
        base[rows, :] = solution[rows, :].astype(F32) + wide(rows) * rest
    for (dim, odd), halo in zip(swaps, halos):
        face = swap_face(dim, odd)
        rows = rows_of(face, height)

        @pl.when(has_neighbour(dim, face, sizes))
        def _():
            base[rows, :] -= wide(rows) * halo[:height, :]


def links_kernel(swaps, sizes, modes, root_map, loads, matrix_f, modes_a, *more):
    halos, (tail, ahead_loads, ahead) = more[: len(swaps)], more[len(swaps) :]
    count, height = root_map.shape[0], loads.shape[0] // FACES
    lanes = loads.shape[1]
    ahead[...] = jnp.zeros_like(ahead)
    own = dot3(root_map[...], modes[...])
    ahead[count : 2 * count, :] = own
    for (dim, odd), halo in zip(swaps, halos):
        face = swap_face(dim, odd)
        known = has_neighbour(dim, face, sizes)
        end = height + count * height // lanes
        pieces = [halo[height:end, k * height : (k + 1) * height] for k in range(lanes // height)]
        link = jnp.where(known, jnp.concatenate(pieces, axis=0), 0.0)
        if dim == 0:
            ahead[rows_of(2 * face, count), rows_of(face, height)] = link
        else:
            ahead[count : 2 * count, rows_of(face, height)] += link
    dot = functools.partial(jnp.dot, preferred_element_type=F32)
    high, low = split(ahead[...])
    both = dot(jnp.concatenate([high, low], axis=0), matrix_f[...])
    done = modes_a.shape[0]
    tail[:done, :] = modes_a[...]
    high, low = split(both[: 3 * count, :] + both[3 * count :, :])
    tail[done : done + 3 * count, :] = high
    tail[done + 3 * count :, :] = low
    high, low = split(own)
    ahead_loads[...] = jnp.zeros_like(ahead_loads)
    ahead_loads[count : 2 * count, :] = dot(high, loads[...]) + dot(low, loads[...])


def merged_kernel(layout, swaps, sizes, ride, ready, modes_f, root_inverse, ahead, *more):
    halos, more = more[: len(swaps)], more[len(swaps) :]
    received, (message, faces, stack) = more[:-3], more[-3:]
    modes, height = ready.shape[0], faces.shape[0] // len(swaps)
    count = message.shape[0] - modes
    high, low = stack_halos(layout, swaps, sizes, halos, faces)
    both = jnp.dot(modes_f[: 2 * modes, :], high, preferred_element_type=F32)
    fine = jnp.dot(modes_f[:modes, :], low, preferred_element_type=F32)
    message[:modes, :] = ready[...] - (both[:modes, :] + (both[modes:, :] + fine))
    me = lax.axis_index("gx")
    stack[...] = jnp.zeros_like(stack)
    pieces = [(me, ahead)]
    for (dim, odd), halo in zip(swaps, halos):
        if ride and (dim, odd) == (0, 0):
            pieces.append((me ^ 1, halo.at[height:, :]))
    paired, single = far_offsets(sizes[0], 1 + ride)
    for offset, piece in zip([core_offset(pair) for pair in paired] + single, received):
        pieces.append((source(me, offset, sizes[0]), piece))
    for index, piece in pieces:
        rows = pl.ds(pl.multiple_of(index * count, count), 3 * count)
        stack[rows, :] += piece[...]
    message[modes:, :] = dot3(root_inverse[...], stack[count:-count, :])


def sum_kernel(own, other, total):
    total[...] = own[...] + other[other.shape[0] - own.shape[0] :, :]


def root_kernel(count, coarse, root_inverse, root, *more):
    received, (message, stack) = more[:-2], more[-2:]
    modes, height = coarse.shape[0], root.shape[0]
    me = lax.axis_index("gx")
    paired, single = far_offsets(count, 1 + nearest(count))
    offsets = [core_offset(pair) for pair in paired] + list(range(1, 1 + nearest(count))) + single
    stack[...] = jnp.zeros_like(stack)
    stack[rows_of(me, height), :] = root[...]
    for offset, piece in zip(offsets, received):
        stack[rows_of(source(me, offset, count), height), :] = piece[...]
    message[:modes, :] = coarse[...]
    message[modes:, :] = dot3(root_inverse[...], stack[...])


def parts_kernel(members, sizes, region_rows, root_map, note, factors):
    modes, order = region_rows.shape
    count, lanes = root_map.shape[0], note.shape[1]
    other_map = note[:count, :modes]
    blocks = [slice(count + k * modes, count + (k + 1) * modes) for k in range(order // lanes)]
    other_rows = jnp.concatenate([note[rows, :] for rows in blocks], axis=1)
    y, z = lax.axis_index("gy"), lax.axis_index("gz")
    half = sizes[0] // 2
    depth = len(members) * modes
    row = lax.broadcasted_iota(jnp.int32, (order, depth), 0)
    column = lax.broadcasted_iota(jnp.int32, (order, depth), 1)
    wanted = jnp.full((order, depth), -1, jnp.int32)
    for k, (dy, dz) in enumerate(members):
        at_y = 2 * source(y // 2, dy, half) + (y + crossing(dy, dz)) % 2
        first = (at_y * sizes[1] + source(z, dz, sizes[1])) * modes
        inside = jnp.logical_and(column >= k * modes, column < (k + 1) * modes)
        wanted = jnp.where(inside, first + column - k * modes, wanted)
    chosen = jnp.where(row == wanted, 1.0, 0.0).astype(BF16)
    for at, (whole, maps) in enumerate(((region_rows[...], root_map[...]), (other_rows, other_map))):
        for level, piece in enumerate(split(whole)):
            rows = slice((2 * level + at) * modes, (2 * level + at + 1) * modes)
            factors[rows, :depth] = jnp.dot(piece, chosen, preferred_element_type=F32).astype(BF16)
        for level, piece in enumerate(split(maps.T)):
            rows = slice((2 * level + at) * modes, (2 * level + at + 1) * modes)
            factors[rows, depth:] = piece


def pair_kernel(modes, factors, first, *more):
    received, (own, out, tall) = more[:-3], more[-3:]
    total = first[modes:, :]
    tall[:modes, :] = first[:modes, :]
    for k, piece in enumerate(received, 1):
        tall[k * modes : (k + 1) * modes, :] = piece[:modes, :]
        total = total + piece[modes:, :]
    tall[(len(received) + 1) * modes :, :] = total
    high, low = split(tall[...])
    both = jnp.dot(factors[...], high, preferred_element_type=F32)
    fine = jnp.dot(factors[: 2 * modes, :], low, preferred_element_type=F32)
    total = both[: 2 * modes, :] + (both[2 * modes :, :] + fine)
    own[...] = total[:modes, :]
    out[...] = total[modes:, :]


def correction_factor(amplitude):
    high, low = split(amplitude)
    return jnp.concatenate([high, high, low], axis=0)


def middle_kernel(
    swaps, base, modes_t, own, other, matrix_f, tail, modes_b, ahead_loads,
    next_solution, placed, ready, ahead, *messages
):
    height = placed.shape[0] // FACES
    tall = correction_factor(own[...] + other[...])
    next_solution[...] = base[...] + jnp.dot(modes_t[...], tall, preferred_element_type=F32)
    local_iter = next_solution[...].astype(BF16)
    placed[...] = jnp.dot(matrix_f[...], local_iter, preferred_element_type=F32)
    more = jnp.dot(tail[...], local_iter, preferred_element_type=F32)
    modes, count = ready.shape[0], ahead.shape[0]
    ready[...] = modes_b[...] - (more[:modes, :] + more[modes : 2 * modes, :])
    more = more[2 * modes :, :]
    ahead[...] = ahead_loads[...] - (more[:count, :] + more[count:, :])
    send_faces(swaps, placed, messages)
    for message in messages:
        if message.shape[0] > height:
            message[height:, :] = ahead[...]


def last_kernel(base, modes_t, own, other, out, result, sems):
    tall = correction_factor(own[...] + other[...])
    parts = sems.shape[0]
    part = result.shape[0] // parts
    copies = []
    for k in range(parts):
        rows = slice(k * part, (k + 1) * part)
        result[rows, :] = base[rows, :] + jnp.dot(modes_t[rows, :], tall, preferred_element_type=F32)
        copies.append(pltpu.make_async_copy(result.at[rows, :], out.at[rows, :], sems.at[k]))
        copies[-1].start()
    for copy in copies:
        copy.wait()


def per_device(
    loads,
    start,
    interface_op,
    block_order,
    interface_weights,
    coarse_modes,
    region_weights,
    region_inverse,
    root_inverse,
):
    sizes = tuple(lax.axis_size(axis) for axis in AXES)
    iface = interface_op.shape[-1]
    cases = loads.shape[-1]
    height = iface // FACES
    matrix = interface_op.reshape(iface, iface)
    order = block_order.reshape(1, FACES)
    weights = interface_weights.reshape(1, iface)
    modes = coarse_modes.reshape(coarse_modes.shape[-2], iface)
    mode_count = modes.shape[0]
    root_map = region_weights.reshape(mode_count, region_weights.shape[-1]).T
    root_modes = root_map.shape[0]
    region_rows = region_inverse.reshape(mode_count, region_inverse.shape[-1])
    target = loads.reshape(iface, cases)
    solution = start.reshape(iface, cases)

    swaps = swap_list(sizes, FIRST_ORDER)
    later = swap_list(sizes, LATER_ORDER)
    half = sizes[1] // 2
    members = list(itertools.product(range(half), range(sizes[2])))

    ride = nearest(sizes[0])
    paired, single = far_offsets(sizes[0], 1 + ride)
    core = later.index((1, 0))
    full = (pltpu.VMEM, (iface, cases), F32)
    places = [pltpu.SMEM((1, FACES), jnp.int32)]
    faces = [pltpu.VMEM((len(swaps) * height, cases), F32)]

    def wide(rows, dtype=BF16):
        return (pltpu.VMEM, (rows, iface), dtype)

    def held(rows):
        return (pltpu.VMEM, (rows, cases), F32)

    def along(value, offset):
        pairs = []
        for place in itertools.product(*map(range, sizes)):
            step = offset if isinstance(offset, int) else offset[place[1] % 2]
            there = (partner(place[0], step, sizes[0]), place[1], place[2])
            pairs.append((flat(sizes, place), flat(sizes, there)))
        return lax.ppermute(value, AXES, pairs)

    def exchange(messages, order):
        return [
            lax.ppermute(message, AXES, swap_pairs(sizes, dim, odd)) for (dim, odd), message in zip(order, messages)
        ]

    def core_sum(own, other):
        return call(sum_kernel, [held(own.shape[0])], [own, other], "core_sum")[0]

    def base_of(order, solution, placed, halos):
        return call(
            functools.partial(base_kernel, order, sizes),
            [full],
            [solution, target, placed, scale] + halos,
            "base",
        )[0]

    for step in range(ITERS):
        if step == 0:
            inputs = [order, solution, matrix, modes, root_map]
            matrix, modes, root_map, placed, *messages = call(
                functools.partial(first_kernel, swaps),
                [(pltpu.VMEM, item.shape, item.dtype) for item in inputs[2:]]
                + [full]
                + [held(height + root_modes * height // cases)] * len(swaps),
                inputs,
                "first_product",
                places
                + [pltpu.VMEM((iface, cases), BF16)] * 2
                + [pltpu.VMEM((root_modes, iface), F32), pltpu.SemaphoreType.DMA((5,))],
                len(inputs),
            )
            modes_t, scale, modes_f, matrix_f, modes_a, modes_b, ready = call(
                functools.partial(constants_kernel, swaps, sizes),
                [
                    (pltpu.VMEM, (iface, 3 * mode_count), BF16),
                    (pltpu.VMEM, (iface, height), F32),
                    (pltpu.VMEM, (2 * mode_count + 2 * root_modes, len(swaps) * height), BF16),
                    wide(iface),
                    wide(2 * mode_count),
                    held(mode_count),
                    held(mode_count + root_modes),
                ],
                [order, matrix, modes, root_map, weights, target, placed],
                "constants",
                [pltpu.VMEM((iface, iface), BF16)] + places + [pltpu.SemaphoreType.DMA],
                1,
            )
            halos = exchange(messages, swaps)
            blocks = region_rows.shape[1] // cases
            coarse, root, note = call(
                functools.partial(coarse_kernel, swaps, sizes),
                [held(mode_count), held(root_modes), held(2 * root_modes + mode_count * blocks)],
                [ready, modes_f, region_rows, root_map] + halos,
                "coarse",
                faces,
            )
            note = lax.ppermute(note, AXES, swap_pairs(sizes, 1, 0))
            both = core_sum(root, note)
            received = [along(root, offset) for offset in list(range(1, 1 + ride)) + single]
            received = [along(both, pair) for pair in paired] + received
            (factors,) = call(
                functools.partial(parts_kernel, members, sizes[1:]),
                [(pltpu.VMEM, (4 * mode_count, len(members) * mode_count + root_modes), BF16)],
                [region_rows, root_map, note],
                "parts",
            )
            base = base_of(swaps, solution, placed, halos)
            tail, ahead_loads = call(
                functools.partial(links_kernel, swaps, sizes),
                [wide(2 * mode_count + 6 * root_modes), held(3 * root_modes)],
                [modes, root_map, target, matrix_f, modes_a] + halos,
                "links",
                [pltpu.VMEM((3 * root_modes, iface), F32)],
            )
            (message,) = call(
                functools.partial(root_kernel, sizes[0]),
                [held(mode_count + root_modes)],
                [coarse, root_inverse, root] + received,
                "root_part",
                [pltpu.VMEM((root_inverse.shape[1], cases), F32)],
            )
        else:
            extra = [3 * root_modes * int(swap == (1, 0) or (ride and swap == (0, 0))) for swap in later]
            solution, placed, ready, ahead, *messages = call(
                functools.partial(middle_kernel, later),
                [full, full, held(mode_count), held(3 * root_modes)] + [held(height + more) for more in extra],
                [base, modes_t, own, other, matrix_f, tail, modes_b, ahead_loads],
                "update_product",
            )
            halos = exchange(messages, later)
            both = core_sum(ahead, halos[core])
            received = [along(both, pair) for pair in paired] + [along(ahead, offset) for offset in single]
            (message,) = call(
                functools.partial(merged_kernel, swaps, later, sizes, ride),
                [held(mode_count + root_modes)],
                [ready, modes_f, root_inverse, ahead] + halos + received,
                "coarse_root",
                faces + [pltpu.VMEM((root_inverse.shape[1] + 2 * root_modes, cases), F32)],
            )
            base = base_of(later, solution, placed, halos)
        pieces = []
        for dy, dz in members[1:]:
            moves = []
            for place in itertools.product(*map(range, sizes)):
                x, y, z = place
                at_y = 2 * partner(y // 2, dy, half) + (y + crossing(dy, dz)) % 2
                moves.append((flat(sizes, place), flat(sizes, (x, at_y, partner(z, dz, sizes[2])))))
            pieces.append(lax.ppermute(message, AXES, moves))
        own, given = call(
            functools.partial(pair_kernel, mode_count),
            [held(mode_count), held(mode_count)],
            [factors, message] + pieces,
            "amplitude_parts",
            [pltpu.VMEM((len(members) * mode_count + root_modes, cases), F32)],
        )
        other = lax.ppermute(given, AXES, swap_pairs(sizes, 1, 0))
    (solution,) = call(
        last_kernel,
        [(jax.ShapeDtypeStruct, (iface, cases), F32)],
        [base, modes_t, own, other],
        "update_last",
        [pltpu.VMEM((iface, cases), F32), pltpu.SemaphoreType.DMA((4,))],
    )
    return solution.reshape(1, 1, 1, iface, cases)


def solution(mesh):
    placed = (
        P("gx", "gy", "gz", None, None),
        P("gx", "gy", "gz", None, None),
        P("gx", "gy", "gz", None, None),
        P("gx", "gy", "gz", None),
        P("gx", "gy", "gz", None),
        P("gx", "gy", "gz", None, None),
        P("gx", "gy", "gz", None, None),
        P("gx", ("gy", "gz"), None),
        P("gx", None),
    )
    return jax.shard_map(
        per_device,
        mesh=mesh,
        in_specs=placed,
        out_specs=P("gx", "gy", "gz", None, None),
        check_vma=False,
    )
```
